128 devices in a mesh: dp: 16 (over z, y), row: 2 (over x_lo), col: 4 (over x_hi, core).
Axes of the slice: x: 4 (x_hi: 2, x_lo: 2; x = x_hi * 2 + x_lo), y: 4, z: 4, core: 2. Of those that a mesh axis runs over, the one named last changes fastest.
Arguments:
- hidden_in: bfloat16 [8192, 1024], P(('dp', 'row'), 'col'), may hold values from -6 to 6
- seg_ids: int32 [8192], P(('dp', 'row')), may hold values from 0 to 7, as said below
- key_mask: int32 [8192], P(('dp', 'row')), may hold values 0 or 1
- w_qkv: bfloat16 [2, 1024, 3, 1024], P(None, 'row', None, 'col'), may hold values from -0.1875 to 0.1875
- qv_bias: float32 [2, 2, 1024], P(None, None, 'col'), may hold values from -4 to 4
- w_out: bfloat16 [2, 1024, 1024], P(None, 'col', 'row'), may hold values from -2 to 2
- out_bias: float32 [2, 1024], P(None, 'col'), may hold values from -4 to 4
- ln_gain: float32 [2, 2, 1024], P(None, None, 'col'), may hold values from 0.5 to 1.5
- ln_shift: float32 [2, 2, 1024], P(None, None, 'col'), may hold values from -4 to 4
- w_up: bfloat16 [2, 1024, 4096], P(None, 'row', 'col'), may hold values from -0.1875 to 0.1875
- up_bias: float32 [2, 4096], P(None, 'col'), may hold values from -6 to 6
- w_down: bfloat16 [2, 4096, 1024], P(None, 'col', 'row'), may hold values from -0.09375 to 0.09375
- down_bias: float32 [2, 1024], P(None, 'col'), may hold values from -4 to 4
- grad_out: bfloat16 [8192, 1024], P(('dp', 'row'), 'col'), may hold values from -6 to 6
Outputs:
- hidden_out: bfloat16 [8192, 1024], P(('dp', 'row'), 'col')
- grad_in: bfloat16 [8192, 1024], P(('dp', 'row'), 'col')
- grad_w_qkv: float32 [2, 1024, 3, 1024], P(None, 'row', None, 'col')
- grad_qv_bias: float32 [2, 2, 1024], P(None, None, 'col')
- grad_w_out: float32 [2, 1024, 1024], P(None, 'col', 'row')
- grad_out_bias: float32 [2, 1024], P(None, 'col')
- grad_ln_gain: float32 [2, 2, 1024], P(None, None, 'col')
- grad_ln_shift: float32 [2, 2, 1024], P(None, None, 'col')
- grad_w_up: float32 [2, 1024, 4096], P(None, 'row', 'col')
- grad_up_bias: float32 [2, 4096], P(None, 'col')
- grad_w_down: float32 [2, 4096, 1024], P(None, 'col', 'row')
- grad_down_bias: float32 [2, 1024], P(None, 'col')
The draws below stay inside these ranges and needn't reach their ends.
Inputs may be any that keep to these rules, and one draw needn't show every extreme that they name: `seg_ids`: within each aligned block of 256 tokens the ids start at 0 and never fall; a change of id starts a new sequence. In every draw one block holds a single sequence of 256 tokens, and some block reaches the largest id.
All inputs are finite; a program needn't handle non-finite values. No bound on the sum of `key_mask` on one device may be relied on, other than what follows from the above.
Results may differ from the reference program's by a relative error of at most 0.035.
Values may be sent and summed in bfloat16 or wider, within the bound.
A program may use at most 128 MiB of HBM per device.

```python
import jax
import jax.numpy as jnp
from jax import lax

D = 1024
HD = 64
HEADS = 16
FF = 4096
LAYERS = 2
TOK_DR = 256
TOKENS = 8192


def draw_seg_ids(key, part):
    key = jax.random.fold_in(key, 11)
    groups = TOKENS // TOK_DR
    first_key, second_key = jax.random.split(key)
    breaks = jax.random.randint(first_key, (groups, TOK_DR), 0, max(TOK_DR // 4, 2)) == 0
    places = jnp.arange(TOK_DR, dtype=jnp.int32)
    group_index = jnp.arange(groups, dtype=jnp.int32)
    single = jax.random.randint(second_key, (), 0, groups)
    forced_group = (single + 1) % groups
    forced = (group_index[:, None] == forced_group) & (places[None, :] % max(TOK_DR // 8, 1) == 0)
    breaks = (breaks | forced) & (places[None, :] > 0)
    breaks = breaks & (group_index[:, None] != single)
    counted = jnp.cumsum(breaks.astype(jnp.int32), axis=1)
    return jnp.minimum(counted, 7).reshape(TOKENS).astype(jnp.int32)


def with_ends(values, key, low, top_value):
    dims = values.shape
    index_at = [jax.random.randint(jax.random.fold_in(key, axis), (), 0, dims[axis]) for axis in range(len(dims))]
    values = values.at[tuple(index_at)].set(low)
    longest = dims.index(max(dims))
    index_at[longest] = (index_at[longest] + 1) % dims[longest]
    return values.at[tuple(index_at)].set(top_value)


def levels(own_key, dims, cuts, low, high):
    def one(dim, parts):
        heights = jax.random.uniform(jax.random.fold_in(jax.random.fold_in(own_key, 6), dim), (parts,), jnp.float32, low / len(cuts), high / len(cuts))
        return jnp.repeat(jnp.exp(heights), dims[dim] // parts).reshape((-1,) + (1,) * (len(dims) - dim - 1))

    factor_of = one(*cuts[0])
    for cut in cuts[1:]:
        factor_of = factor_of * one(*cut)
    return factor_of


def gaussian(rng, dims, scale, bound, cuts=(), held_as=jnp.bfloat16):
    values = scale * jax.random.normal(rng, dims, jnp.float32)
    if cuts:
        values = values * levels(rng, dims, cuts, -0.22, 0.18)
    return jnp.clip(values, -bound, bound).astype(held_as)


def setup_inputs(seed: int = 0) -> dict:
    key_list = jax.random.split(jax.random.key(seed), 15)
    return {
        "hidden_in": gaussian(key_list[0], (TOKENS, D), 1.0, 6.0, ((0, 32), (1, 4))),
        "seg_ids": draw_seg_ids(jax.random.fold_in(key_list[14], 71), 0),
        "key_mask": with_ends((jax.random.randint(key_list[2], (TOKENS,), 0, 8) < 7).astype(jnp.int32), jax.random.fold_in(key_list[2], 1), 0, 1),
        "w_qkv": gaussian(key_list[3], (LAYERS, D, 3, D), D ** -0.5, 0.1875, ((1, 2), (3, 4))),
        "qv_bias": gaussian(key_list[4], (LAYERS, 2, D), 0.3, 4.0, ((2, 4),), jnp.float32),
        "w_out": gaussian(key_list[5], (LAYERS, D, D), (max(D // 128, 1)) ** -0.5, 2.0, ((1, 4), (2, 2))),
        "out_bias": gaussian(key_list[6], (LAYERS, D), 0.3, 4.0, ((1, 4),), jnp.float32),
        "ln_gain": jnp.clip(1.0 + 0.1 * jax.random.normal(key_list[7], (LAYERS, 2, D), jnp.float32), 0.5, 1.5),
        "ln_shift": gaussian(key_list[8], (LAYERS, 2, D), 0.3, 4.0, ((2, 4),), jnp.float32),
        "w_up": gaussian(key_list[9], (LAYERS, D, FF), D ** -0.5, 0.1875, ((1, 2), (2, 4))),
        "up_bias": gaussian(key_list[10], (LAYERS, FF), 0.5, 6.0, ((1, 4),), jnp.float32),
        "w_down": gaussian(key_list[11], (LAYERS, FF, D), FF ** -0.5, 0.09375, ((1, 4), (2, 2))),
        "down_bias": gaussian(key_list[12], (LAYERS, D), 0.3, 4.0, ((1, 4),), jnp.float32),
        "grad_out": gaussian(key_list[13], (TOKENS, D), 1.0, 6.0, ((0, 32), (1, 4))),
    }


EPSILON = 1e-05
MASKED = -1e+30
HIGHEST = lax.Precision.HIGHEST

@jax.custom_vjp
def low(v):
    return lax.optimization_barrier(v.astype(jnp.bfloat16)).astype(jnp.float32)

@jax.custom_vjp
def low_back(v):
    return v

def low_keep(v):
    return (low(v), None)

def low_pass(kept, grad):
    return (grad,)

def back_keep(v):
    return (v, None)

def back_low(kept, grad):
    return (low(grad),)
low.defvjp(low_keep, low_pass)
low_back.defvjp(back_keep, back_low)

def layer_norm(values_in, gain_vec, shift_vec):
    mean_row = lax.optimization_barrier(jnp.mean(values_in, axis=-1, keepdims=True))
    spread = lax.optimization_barrier(jnp.mean(values_in * values_in, axis=-1, keepdims=True)) - mean_row * mean_row
    return (values_in - mean_row) * lax.rsqrt(spread + EPSILON) * gain_vec + shift_vec

def attend(query_rows, key_rows, value_rows, segments, keep_keys):
    tok_rows = query_rows.shape[0]
    query_heads = query_rows.reshape(tok_rows, HEADS, HD)
    key_heads = key_rows.reshape(tok_rows, HEADS, HD)
    value_heads = value_rows.reshape(tok_rows, HEADS, HD)
    scores = low_back(jnp.einsum('qhd,khd->hqk', query_heads, key_heads, precision=HIGHEST))
    places = jnp.arange(tok_rows, dtype=jnp.int32)
    allowed = (segments[:, None] == segments[None, :]) & ((keep_keys[None, :] == 1) | (places[:, None] == places[None, :]))
    scaled = jnp.where(allowed[None], scores * HD ** (-0.5), MASKED)
    highest = lax.optimization_barrier(jnp.max(scaled, axis=2, keepdims=True))
    raised = jnp.exp(scaled - highest)
    probs_low = low(raised / lax.optimization_barrier(jnp.sum(raised, axis=2, keepdims=True)))
    context = jnp.einsum('hqk,khd->qhd', probs_low, value_heads, precision=HIGHEST)
    return context.reshape(tok_rows, HEADS * HD)

def attention(queries, keyset, valueset, seg_ids, key_mask):
    groups = queries.shape[0] // TOK_DR
    members = (queries.reshape(groups, TOK_DR, D), keyset.reshape(groups, TOK_DR, D), valueset.reshape(groups, TOK_DR, D), seg_ids.reshape(groups, TOK_DR), key_mask.reshape(groups, TOK_DR))
    saved_attend = jax.checkpoint(attend)

    def one_group(group_members):
        return saved_attend(group_members[0], group_members[1], group_members[2], group_members[3], group_members[4])
    return lax.map(one_group, members).reshape(groups * TOK_DR, D)

def layer_forward(hidden, weights, layer_index, seg_ids, key_mask):
    w_qkv, qv_bias, w_out, out_bias, ln_gain, ln_shift, w_up, up_bias, w_down, down_bias = weights
    lowered = low(hidden)
    mixed = low_back(jnp.einsum('td,dje->tje', lowered, w_qkv[layer_index], precision=HIGHEST))
    queries = low(mixed[:, 0] + qv_bias[layer_index, 0])
    keyset = low(mixed[:, 1])
    valueset = low(mixed[:, 2] + qv_bias[layer_index, 1])
    context = low(low_back(attention(queries, keyset, valueset, seg_ids, key_mask)))
    attended = low_back(jnp.dot(context, w_out[layer_index], precision=HIGHEST)) + out_bias[layer_index]
    middle = layer_norm(hidden + attended, ln_gain[layer_index, 0], ln_shift[layer_index, 0])
    lifted = low_back(jnp.dot(low(middle), w_up[layer_index], precision=HIGHEST)) + up_bias[layer_index]
    activated = low(jax.nn.gelu(lifted, approximate=False))
    dropped = low_back(jnp.dot(activated, w_down[layer_index], precision=HIGHEST)) + down_bias[layer_index]
    return layer_norm(middle + dropped, ln_gain[layer_index, 1], ln_shift[layer_index, 1])

def reference(hidden_in, seg_ids, key_mask, w_qkv, qv_bias, w_out, out_bias, ln_gain, ln_shift, w_up, up_bias, w_down, down_bias, grad_out):
    floats = (w_qkv.astype(jnp.float32), qv_bias.astype(jnp.float32), w_out.astype(jnp.float32), out_bias.astype(jnp.float32), ln_gain.astype(jnp.float32), ln_shift.astype(jnp.float32), w_up.astype(jnp.float32), up_bias.astype(jnp.float32), w_down.astype(jnp.float32), down_bias.astype(jnp.float32))

    def forward(hidden, *weights):
        for layer_index in range(LAYERS):
            hidden = layer_forward(hidden, weights, layer_index, seg_ids, key_mask)
        return hidden
    result, pullback = jax.vjp(forward, hidden_in.astype(jnp.float32), *floats)
    gradients = pullback(grad_out.astype(jnp.float32))
    return (result.astype(jnp.bfloat16), gradients[0].astype(jnp.bfloat16), gradients[1], gradients[2], gradients[3], gradients[4], gradients[5], gradients[6], gradients[7], gradients[8], gradients[9], gradients[10])
```

```python
import functools

import jax
import jax.numpy as jnp
from jax import lax
from jax.experimental import pallas as pl
from jax.experimental.pallas import tpu as pltpu
from jax.sharding import PartitionSpec as P

D = 1024
HD = 64
LAYERS = 2
TOK = 256
OWN = 64
COLS = 256
HEADS_LOCAL = 4
SLABS = 6
EPSILON = 1e-05
MASKED = -1e30
SCALE = HD**-0.5
MESH = pl.DeviceIdType.MESH
BF = jnp.bfloat16
F32 = jnp.float32


def dot(a, b):
    return jnp.dot(a, b, preferred_element_type=F32)


def dot_nt(a, b):
    return lax.dot_general(a, b, (((1,), (1,)), ((), ())), preferred_element_type=F32)


def dot_tn(a, b):
    return lax.dot_general(a, b, (((0,), (0,)), ((), ())), preferred_element_type=F32)


def norm_back(upstream, normed, inverse, gain):
    scaled = upstream * gain
    mean_one = jnp.sum(scaled, axis=1, keepdims=True) / D
    mean_two = jnp.sum(scaled * normed, axis=1, keepdims=True) / D
    return inverse * (scaled - mean_one - normed * mean_two)


def kernel(
    hid, gout, mask, small, upb, qvb, wq, wo, wu, wd,
    hout, gin, gbig, gsmall,
    WQ, WO, WU, WD, PF, A2H, A2G, S, M, U, GS, GF, F1,
    STATE, MID, SEC, FIR, QKV, CTX, PR, DG, ACT, NRM, INV, LL, ML, GC,
    PS, XS, L1, L2, HS, HOB, GIB,
    G, R1, A1, R2, A2, R3, FB,
    SGF, SU, SQ, RC, SM, SZ, SY, SR,
    w_ssem, w_rsem, w_lsem, in_s, in_r, ag_s, ag_r, rs_s, rs_r, gr_s, gr_r, out_s, out_r, lsem, sm_s, sm_r,
):
    dp = lax.axis_index("dp")
    row = lax.axis_index("row")
    col = lax.axis_index("col")
    z, y = lax.div(dp, 4), lax.rem(dp, 4)
    xh, core = lax.div(col, 2), lax.rem(col, 2)
    col_core = xh * 2 + (1 - core)
    col_cross = (1 - xh) * 2 + core
    col_diag = (1 - xh) * 2 + (1 - core)
    core_dev = (dp, row, col_core)
    cross_dev = (dp, row, col_cross)
    row_dev = (dp, 1 - row, col)

    def col_dev(d):
        return (dp, row, lax.rem(col + d, 4))

    def axis_place(axis):
        return z if axis == 0 else y

    def axis_dev(axis, d):
        if axis == 0:
            return (lax.rem(z + d, 4) * 4 + y, row, col)
        return (z * 4 + lax.rem(y + d, 4), row, col)

    def chunk(j, rows=OWN):
        return pl.ds(pl.multiple_of(j * rows, rows), rows)

    def remote(src, dst, ssem, rsem, dev):
        return pltpu.make_async_remote_copy(
            src_ref=src, dst_ref=dst, send_sem=ssem, recv_sem=rsem, device_id=dev, device_id_type=MESH
        )

    barrier = pltpu.get_barrier_semaphore()
    for dev in [col_dev(1), col_dev(2), col_dev(3), row_dev] + [axis_dev(a, d) for a in (0, 1) for d in (1, 2, 3)]:
        pl.semaphore_signal(barrier, 1, device_id=dev, device_id_type=MESH)
    pl.semaphore_wait(barrier, 10)

    def in_copies(d):
        to = lax.rem(col + d, 4)
        dev = (dp, row, to)
        return [
            remote(hid.at[chunk(to)], A2H.at[:, chunk(col, COLS)], in_s.at[0, d - 1], in_r.at[0, d - 1], dev),
            remote(small, PF.at[:, chunk(col, COLS)], in_s.at[1, d - 1], in_r.at[1, d - 1], dev),
            remote(gout.at[chunk(to)], A2G.at[:, chunk(col, COLS)], in_s.at[2, d - 1], in_r.at[2, d - 1], dev),
        ]

    def in_arrivals(d):
        source = lax.rem(col + 4 - d, 4)
        return [
            remote(hid.at[chunk(col)], A2H.at[:, chunk(source, COLS)], in_s.at[0, d - 1], in_r.at[0, d - 1], col_dev(d)),
            remote(small, PF.at[:, chunk(source, COLS)], in_s.at[1, d - 1], in_r.at[1, d - 1], col_dev(d)),
            remote(gout.at[chunk(col)], A2G.at[:, chunk(source, COLS)], in_s.at[2, d - 1], in_r.at[2, d - 1], col_dev(d)),
        ]

    for d in (1, 2, 3):
        for c in in_copies(d):
            c.start()

    pairs = ((wq, WQ), (wo, WO), (wu, WU), (wd, WD))

    def w_local(l, n):
        return pltpu.make_async_copy(pairs[n][0].at[l], pairs[n][1].at[l, row], w_lsem.at[l, n])

    def w_remote(l, n, half):
        return remote(pairs[n][0].at[l], pairs[n][1].at[l, half], w_ssem.at[l, n], w_rsem.at[l, n], row_dev)

    for l in range(LAYERS):
        for n in range(4):
            w_remote(l, n, row).start()
            w_local(l, n).start()

    def w_wait(l, n):
        w_local(l, n).wait()
        w_remote(l, n, 1 - row).wait_recv()

    A2H[:, chunk(col, COLS)] = hid[chunk(col), :]
    A2G[:, chunk(col, COLS)] = gout[chunk(col), :]
    PF[:, chunk(col, COLS)] = small[...]
    for d in (1, 2, 3):
        for c in in_arrivals(d):
            c.wait_recv()
    S[...] = A2H[...].astype(F32)
    U[...] = A2G[...].astype(F32)

    def ag_send(k, X):
        out = []
        for p in (0, 1):
            rows = pl.ds(pl.multiple_of(col * OWN + p * 32, 32), 32)
            out.append(remote(X.at[rows], X.at[rows], ag_s.at[k, p], ag_r.at[k, p], cross_dev))
        out.append(remote(X.at[chunk(col)], X.at[chunk(col)], ag_s.at[k, 2], ag_r.at[k, 2], core_dev))
        return out

    def ag_forward(k, X, p):
        rows = pl.ds(pl.multiple_of(col_cross * OWN + p * 32, 32), 32)
        return remote(X.at[rows], X.at[rows], ag_s.at[k, 3 + p], ag_r.at[k, 3 + p], core_dev)

    def ag_start(k, X):
        for c in ag_send(k, X):
            c.start()

    def ag_finish(k, X):
        for p in (0, 1):
            rows = pl.ds(pl.multiple_of(col_cross * OWN + p * 32, 32), 32)
            remote(X.at[rows], X.at[rows], ag_s.at[k, p], ag_r.at[k, p], cross_dev).wait_recv()
            ag_forward(k, X, p).start()
        remote(X.at[chunk(col_core)], X.at[chunk(col_core)], ag_s.at[k, 2], ag_r.at[k, 2], core_dev).wait_recv()
        for p in (0, 1):
            rows = pl.ds(pl.multiple_of(col_diag * OWN + p * 32, 32), 32)
            remote(X.at[rows], X.at[rows], ag_s.at[k, 3 + p], ag_r.at[k, 3 + p], core_dev).wait_recv()

    def ag_drain(k, X):
        for c in ag_send(k, X):
            c.wait_send()
        for p in (0, 1):
            ag_forward(k, X, p).wait_send()

    def half(h):
        return pl.ds(h * 512, 512)

    def rs_first(k, par, h, t):
        to = (1 - xh) * 2 + (1 - core) if t == 0 else col_core
        return remote(
            PS.at[chunk(to), half(h)], L1.at[par, t, :, half(h)], rs_s.at[k, h * 3 + t], rs_r.at[k, h * 3 + t], core_dev
        )

    def rs_cross(k, par, h):
        return remote(XS.at[:, half(h)], L2.at[par, :, half(h)], rs_s.at[k, h * 3 + 2], rs_r.at[k, h * 3 + 2], cross_dev)

    def rs_send(k, par, h):
        for t in (0, 1):
            rs_first(k, par, h, t).start()

    def rs_mid(k, par, h):
        rs_first(k, par, h, 0).wait_recv()
        total = PS[chunk(col_cross), half(h)].astype(F32) + L1[par, 0, :, half(h)].astype(F32)
        XS[:, half(h)] = total.astype(BF)
        rs_cross(k, par, h).start()

    def rs_end(k, par, h):
        rs_first(k, par, h, 1).wait_recv()
        total = PS[chunk(col), half(h)].astype(F32) + L1[par, 1, :, half(h)].astype(F32)
        rs_cross(k, par, h).wait_recv()
        return total + L2[par, :, half(h)].astype(F32)

    def rs_drain(k, par):
        for h in (0, 1):
            for t in (0, 1):
                rs_first(k, par, h, t).wait_send()
            rs_cross(k, par, h).wait_send()

    def gr_one(l, s, d):
        axis = s % 2
        to = lax.rem(axis_place(axis) + d, 4)
        return remote(
            G.at[l, s, :, chunk(to, 128), :], R1.at[l, s, d - 1], gr_s.at[l, s, d - 1], gr_r.at[l, s, d - 1], axis_dev(axis, d)
        )

    def gr_two(l, s, d):
        axis = 1 - s % 2
        to = lax.rem(axis_place(axis) + d, 4)
        return remote(
            A1.at[l, s, :, chunk(to, 32), :], R2.at[l, s, d - 1], gr_s.at[l, s, 2 + d], gr_r.at[l, s, 2 + d], axis_dev(axis, d)
        )

    def gr_row(l, s):
        return remote(A2.at[l, s, 1 - row], R3.at[l, s], gr_s.at[l, s, 6], gr_r.at[l, s, 6], row_dev)

    def gr_four(l, s, d, place):
        axis = 1 - s % 2
        rows = FB.at[l, s, chunk(place, 32), :]
        return remote(rows, rows, gr_s.at[l, s, 6 + d], gr_r.at[l, s, 6 + d], axis_dev(axis, d))

    def gr_five(l, s, d, place):
        axis = s % 2
        return remote(
            FB.at[l, s], gbig.at[l, s, chunk(place, 128), :], gr_s.at[l, s, 9 + d], gr_r.at[l, s, 9 + d], axis_dev(axis, d)
        )

    def gr_local(l, s):
        return pltpu.make_async_copy(FB.at[l, s], gbig.at[l, s, chunk(axis_place(s % 2), 128), :], lsem.at[l, s])

    def t1(l, s):
        for d in (1, 2, 3):
            gr_one(l, s, d).start()

    def t2(l, s):
        for d in (1, 2, 3):
            gr_one(l, s, d).wait_recv()
        own = chunk(axis_place(s % 2), 128)
        for r in (0, 1):
            total = G[l, s, r, own, :].astype(F32)
            for d in (0, 1, 2):
                total = total + R1[l, s, d, r].astype(F32)
            A1[l, s, r] = total.astype(BF)
        for d in (1, 2, 3):
            gr_two(l, s, d).start()

    def t3(l, s):
        for d in (1, 2, 3):
            gr_two(l, s, d).wait_recv()
        own = chunk(axis_place(1 - s % 2), 32)
        for r in (0, 1):
            total = A1[l, s, r, own, :].astype(F32)
            for d in (0, 1, 2):
                total = total + R2[l, s, d, r].astype(F32)
            A2[l, s, r] = total.astype(BF)
        gr_row(l, s).start()

    def t4(l, s):
        gr_row(l, s).wait_recv()
        place = axis_place(1 - s % 2)
        FB[l, s, chunk(place, 32), :] = (A2[l, s, row].astype(F32) + R3[l, s].astype(F32)).astype(BF)
        for d in (1, 2, 3):
            gr_four(l, s, d, place).start()

    def t5(l, s):
        place = axis_place(1 - s % 2)
        for d in (1, 2, 3):
            gr_four(l, s, d, lax.rem(place + 4 - d, 4)).wait_recv()
        own = axis_place(s % 2)
        for d in (1, 2, 3):
            gr_five(l, s, d, own).start()
        gr_local(l, s).start()

    def t6(l, s):
        own = axis_place(s % 2)
        for d in (1, 2, 3):
            gr_five(l, s, d, lax.rem(own + 4 - d, 4)).wait_recv()
        gr_local(l, s).wait()
        place = axis_place(1 - s % 2)
        for d in (1, 2, 3):
            gr_one(l, s, d).wait_send()
            gr_two(l, s, d).wait_send()
            gr_four(l, s, d, place).wait_send()
            gr_five(l, s, d, own).wait_send()
        gr_row(l, s).wait_send()

    def both(step, l, first):
        step(l, first)
        step(l, first + 1)

    def vec(l, r):
        return PF[pl.ds(l * 8 + r, 1), :]

    def norm_into(values, l, n, gain, shift):
        mean_row = jnp.sum(values, axis=1, keepdims=True) / D
        squares = jnp.sum(values * values, axis=1, keepdims=True) / D
        inverse = lax.rsqrt(squares - mean_row * mean_row + EPSILON)
        normed = (values - mean_row) * inverse
        NRM[l, n] = normed
        INV[l, n] = jnp.broadcast_to(inverse, (OWN, 128))
        return normed * gain + shift

    def forward(l, carry):
        X = STATE.at[l]
        X[chunk(col), :] = S[...].astype(BF)
        ag_start(l * 4, X)
        w_wait(l, 0)
        ag_finish(l * 4, X)
        for j in range(3):
            lanes = pl.ds(j * COLS, COLS)
            mixed = dot(STATE[l, :, :512], WQ[l, 0, :, lanes]) + dot(STATE[l, :, 512:], WQ[l, 1, :, lanes])
            if j != 1:
                mixed = mixed + qvb[l, j // 2 : j // 2 + 1, :]
            QKV[l, j] = mixed.astype(BF)
        ag_drain(l * 4, X)
        for h in range(HEADS_LOCAL):
            lanes = slice(h * HD, (h + 1) * HD)
            scores = dot_nt(QKV[l, 0, :, lanes], QKV[l, 1, :, lanes])
            scaled = jnp.where(mask[...] > 0.5, scores * SCALE, MASKED)
            raised = jnp.exp(scaled - jnp.max(scaled, axis=1, keepdims=True))
            probs = raised / jnp.sum(raised, axis=1, keepdims=True)
            PR[l, h] = probs
            CTX[l, :, lanes] = dot(probs.astype(BF), QKV[l, 2, :, lanes]).astype(BF)
        w_wait(l, 1)
        k = l * 4
        for h in (0, 1):
            PS[:, half(h)] = dot(CTX[l], WO[l, h]).astype(BF)
            rs_send(k, 0, h)
        rs_mid(k, 0, 0)
        rs_mid(k, 0, 1)
        for h in (0, 1):
            F1[:, half(h)] = S[:, half(h)] + rs_end(k, 0, h)
        rs_drain(k, 0)
        middle = norm_into(F1[...] + vec(l, 0), l, 0, vec(l, 1), vec(l, 2))
        M[...] = middle
        X = MID.at[l]
        X[chunk(col), :] = middle.astype(BF)
        ag_start(l * 4 + 1, X)
        w_wait(l, 2)
        ag_finish(l * 4 + 1, X)

        def lift(n, c):
            lanes = chunk(n, COLS)
            lifted = dot(MID[l, :, :512], WU[l, 0, :, lanes]) + dot(MID[l, :, 512:], WU[l, 1, :, lanes])
            lifted = lifted + upb[pl.ds(l, 1), lanes]
            phi = 0.5 * (1.0 + lax.erf(lifted * (0.5**0.5)))
            density = jnp.exp(-0.5 * lifted * lifted) * 0.3989422804014327
            DG[l, :, lanes] = phi + lifted * density
            ACT[l, :, lanes] = (lifted * phi).astype(BF)
            return c

        lax.fori_loop(0, 4, lift, 0)
        ag_drain(l * 4 + 1, X)
        w_wait(l, 3)
        k = l * 4 + 1
        for h in (0, 1):
            for q in (0, 1):
                lanes = pl.ds(h * 512 + q * 256, 256)
                PS[:, lanes] = dot(ACT[l], WD[l, h, :, pl.ds(q * 256, 256)]).astype(BF)
            rs_send(k, 1, h)
        rs_mid(k, 1, 0)
        rs_mid(k, 1, 1)
        for h in (0, 1):
            F1[:, half(h)] = M[:, half(h)] + rs_end(k, 1, h)
        rs_drain(k, 1)
        S[...] = norm_into(F1[...] + vec(l, 5), l, 1, vec(l, 3), vec(l, 4))
        return carry

    lax.fori_loop(0, LAYERS, forward, 0)

    def out_copies(n, d):
        buf = (HOB, GIB)[n]
        to = lax.rem(col + d, 4)
        return remote(
            HS.at[n, :, chunk(to, COLS)], buf.at[chunk(col)], out_s.at[n, d - 1], out_r.at[n, d - 1], (dp, row, to)
        )

    def out_arrivals(n, d):
        buf = (HOB, GIB)[n]
        source = lax.rem(col + 4 - d, 4)
        return remote(
            HS.at[n, :, chunk(col, COLS)], buf.at[chunk(source)], out_s.at[n, d - 1], out_r.at[n, d - 1], col_dev(d)
        )

    HS[0] = S[...].astype(BF)
    for d in (1, 2, 3):
        out_copies(0, d).start()
    HOB[chunk(col), :] = HS[0, :, chunk(col, COLS)]

    def backward(i, carry):
        l = LAYERS - 1 - i
        prev = l + 1
        upstream = U[...]
        normed = NRM[l, 1]
        SGF[l, 3:4, :] = jnp.sum(upstream * normed, axis=0, keepdims=True)
        SGF[l, 4:5, :] = jnp.sum(upstream, axis=0, keepdims=True)
        grad_second = norm_back(upstream, normed, INV[l, 1, :, :1], vec(l, 3))
        GS[...] = grad_second
        SGF[l, 5:6, :] = jnp.sum(grad_second, axis=0, keepdims=True)
        SEC[chunk(col), :] = grad_second.astype(BF)
        k = l * 4 + 2
        ag_start(k, SEC)

        @pl.when(i > 0)
        def _():
            both(t2, prev, 2)
            both(t3, prev, 0)

        ag_finish(k, SEC)

        def pull(n, c):
            lanes = chunk(n, COLS)
            grad_act = dot_nt(SEC[:, :512], WD[l, 0, lanes, :]) + dot_nt(SEC[:, 512:], WD[l, 1, lanes, :])
            grad_lifted = grad_act * DG[l, :, lanes]
            SU[l, :, lanes] = jnp.sum(grad_lifted, axis=0, keepdims=True)
            LL[:, lanes] = grad_lifted.astype(BF)
            return c

        lax.fori_loop(0, 4, pull, 0)
        for h in (0, 1):
            for q in (0, 1):
                lanes = pl.ds(h * 512 + q * 256, 256)
                PS[:, lanes] = dot_nt(LL[...], WU[l, h, pl.ds(q * 256, 256), :]).astype(BF)
            rs_send(k, 0, h)
        rs_mid(k, 0, 0)
        rs_mid(k, 0, 1)

        def down_grad(f, c):
            total = dot_tn(ACT[l, :, chunk(f, COLS)], SEC[...]).astype(BF)
            rows = chunk(lax.rem(f, 2), COLS)
            for r in (0, 1):
                G[l, lax.div(f, 2), r, rows, :] = total[:, r * 512 : (r + 1) * 512]
            return c

        lax.fori_loop(0, 4, down_grad, 0)
        both(t1, l, 0)
        ag_drain(k, SEC)

        @pl.when(i > 0)
        def _():
            both(t2, prev, 4)
            both(t3, prev, 2)
            both(t4, prev, 0)

        for h in (0, 1):
            GS[:, half(h)] = GS[:, half(h)] + rs_end(k, 0, h)
        rs_drain(k, 0)
        grad_middle = GS[...]
        normed = NRM[l, 0]
        SGF[l, 1:2, :] = jnp.sum(grad_middle * normed, axis=0, keepdims=True)
        SGF[l, 2:3, :] = jnp.sum(grad_middle, axis=0, keepdims=True)
        grad_first = norm_back(grad_middle, normed, INV[l, 0, :, :1], vec(l, 1))
        GF[...] = grad_first
        SGF[l, 0:1, :] = jnp.sum(grad_first, axis=0, keepdims=True)
        FIR[chunk(col), :] = grad_first.astype(BF)
        k = l * 4 + 3
        ag_start(k, FIR)

        def up_grad(n, c):
            total = dot_tn(MID[l, :, chunk(n, COLS)], LL[...]).astype(BF)
            rows = chunk(lax.rem(n, 2), COLS)
            for r in (0, 1):
                G[l, 2 + r, lax.div(n, 2), rows, :] = total[:, r * 512 : (r + 1) * 512]
            return c

        lax.fori_loop(0, 4, up_grad, 0)
        both(t1, l, 2)

        @pl.when(i > 0)
        def _():
            both(t3, prev, 4)
            both(t4, prev, 2)
            both(t5, prev, 0)

        ag_finish(k, FIR)
        GC[...] = (dot_nt(FIR[:, :512], WO[l, 0]) + dot_nt(FIR[:, 512:], WO[l, 1])).astype(BF)
        for h in range(HEADS_LOCAL):
            lanes = slice(h * HD, (h + 1) * HD)
            probs = PR[l, h]
            grad_probs = dot_nt(GC[:, lanes], QKV[l, 2, :, lanes])
            centre = jnp.sum(probs * grad_probs, axis=1, keepdims=True)
            grad_scores = (probs * (grad_probs - centre) * SCALE).astype(BF)
            grad_query = dot(grad_scores, QKV[l, 1, :, lanes])
            grad_key = dot_tn(grad_scores, QKV[l, 0, :, lanes])
            grad_value = dot_tn(probs.astype(BF), GC[:, lanes])
            SQ[l, 0:1, lanes] = jnp.sum(grad_query, axis=0, keepdims=True)
            SQ[l, 1:2, lanes] = jnp.sum(grad_value, axis=0, keepdims=True)
            ML[:, h * HD : (h + 1) * HD] = grad_query.astype(BF)
            ML[:, COLS + h * HD : COLS + (h + 1) * HD] = grad_key.astype(BF)
            ML[:, 2 * COLS + h * HD : 2 * COLS + (h + 1) * HD] = grad_value.astype(BF)
        for h in (0, 1):
            for q in (0, 1):
                lanes = pl.ds(h * 512 + q * 256, 256)
                PS[:, lanes] = dot_nt(ML[...], WQ[l, h, pl.ds(q * 256, 256), :]).astype(BF)
            rs_send(k, 1, h)
        rs_mid(k, 1, 0)
        rs_mid(k, 1, 1)
        total = dot_tn(CTX[l], FIR[...]).astype(BF)
        for r in (0, 1):
            G[l, 5, r, 0:256, :] = total[:, r * 512 : (r + 1) * 512]

        def qkv_grad(r, c):
            for q in (0, 1):
                total = dot_tn(STATE[l, :, chunk(2 * r + q, COLS)], ML[...]).astype(BF)
                G[l, 4, r, q * 256 : (q + 1) * 256, :] = total[:, :512]
                G[l, 5, r, 256:512, q * 256 : (q + 1) * 256] = total[:, 512:]
            return c

        lax.fori_loop(0, 2, qkv_grad, 0)
        both(t1, l, 4)
        ag_drain(k, FIR)
        both(t2, l, 0)

        @pl.when(i > 0)
        def _():
            both(t4, prev, 4)
            both(t5, prev, 2)

        for h in (0, 1):
            U[:, half(h)] = GF[:, half(h)] + rs_end(k, 1, h)
        rs_drain(k, 1)
        return carry

    lax.fori_loop(0, LAYERS, backward, 0)

    HS[1] = U[...].astype(BF)
    for d in (1, 2, 3):
        out_copies(1, d).start()
    GIB[chunk(col), :] = HS[1, :, chunk(col, COLS)]

    def sc_copy(d):
        to = lax.rem(col + d, 4)
        return remote(SGF.at[:, :, chunk(to, COLS)], RC.at[d - 1], sm_s.at[0, d - 1], sm_r.at[0, d - 1], (dp, row, to))

    def sd_copy(axis, d, place):
        buf = (SZ, SY)[axis]
        return remote(
            buf.at[axis_place(axis)], buf.at[place], sm_s.at[1 + axis, d - 1], sm_r.at[1 + axis, d - 1], axis_dev(axis, d)
        )

    def sr_copy():
        return remote(SM, SR, sm_s.at[3, 0], sm_r.at[3, 0], row_dev)

    for d in (1, 2, 3):
        sc_copy(d).start()
    both(t2, 0, 2)
    both(t3, 0, 0)
    both(t5, 1, 4)
    for d in (1, 2, 3):
        sc_copy(d).wait_recv()
    feature = SGF[:, :, chunk(col, COLS)]
    for d in (0, 1, 2):
        feature = feature + RC[d]
    for l in range(LAYERS):
        SZ[z, 8 * l : 8 * l + 8, :] = feature[l]
        for q in range(4):
            SZ[z, 16 + 4 * l + q : 17 + 4 * l + q, :] = SU[l, :, q * COLS : (q + 1) * COLS]
        SZ[z, 24 + 2 * l : 26 + 2 * l, :] = SQ[l]
    SZ[z, 28:32, :] = jnp.zeros((4, COLS), F32)
    for d in (1, 2, 3):
        sd_copy(0, d, z).start()
    both(t2, 0, 4)
    both(t3, 0, 2)
    both(t4, 0, 0)
    for d in (1, 2, 3):
        sd_copy(0, d, lax.rem(z + 4 - d, 4)).wait_recv()
    SY[y] = SZ[0] + SZ[1] + SZ[2] + SZ[3]
    for d in (1, 2, 3):
        sd_copy(1, d, y).start()
    both(t3, 0, 4)
    both(t4, 0, 2)
    both(t5, 0, 0)
    for d in (1, 2, 3):
        sd_copy(1, d, lax.rem(y + 4 - d, 4)).wait_recv()
    SM[...] = SY[0] + SY[1] + SY[2] + SY[3]
    sr_copy().start()
    both(t4, 0, 4)
    both(t5, 0, 2)
    sr_copy().wait_recv()
    gsmall[...] = SM[...] + SR[...]
    both(t5, 0, 4)

    for n in (0, 1):
        for d in (1, 2, 3):
            out_arrivals(n, d).wait_recv()
    hout[...] = HOB[...]
    gin[...] = GIB[...]

    for d in (1, 2, 3):
        for c in in_copies(d):
            c.wait_send()
        for n in (0, 1):
            out_copies(n, d).wait_send()
        sc_copy(d).wait_send()
        sd_copy(0, d, z).wait_send()
        sd_copy(1, d, y).wait_send()
    sr_copy().wait_send()
    for l in range(LAYERS):
        for n in range(4):
            w_remote(l, n, row).wait_send()

    def finish(l, c):
        for s in range(SLABS):
            t6(l, s)
        return c

    lax.fori_loop(0, LAYERS, finish, 0)


def step_call(*args):
    vmem = pl.BlockSpec(memory_space=pltpu.VMEM)
    hbm = pl.BlockSpec(memory_space=pl.ANY)
    dma = pltpu.SemaphoreType.DMA
    V = pltpu.VMEM
    L = LAYERS
    scratch = [
        V((L, 2, 512, 768), BF), V((L, 2, 256, 512), BF), V((L, 2, 512, 1024), BF), V((L, 2, 1024, 512), BF),
        V((16, 1024), F32), V((OWN, D), BF), V((OWN, D), BF),
        V((OWN, D), F32), V((OWN, D), F32), V((OWN, D), F32), V((OWN, D), F32), V((OWN, D), F32), V((OWN, D), F32),
        V((L, TOK, D), BF), V((L, TOK, D), BF), V((TOK, D), BF), V((TOK, D), BF),
        V((L, 3, TOK, COLS), BF), V((L, TOK, COLS), BF), V((L, HEADS_LOCAL, TOK, TOK), F32),
        V((L, TOK, 1024), F32), V((L, TOK, 1024), BF), V((L, 2, OWN, D), F32), V((L, 2, OWN, 128), F32),
        V((TOK, 1024), BF), V((TOK, 768), BF), V((TOK, COLS), BF),
        V((TOK, D), BF), V((OWN, D), BF), V((2, 2, OWN, D), BF), V((2, OWN, D), BF),
        V((2, OWN, D), BF), V((TOK, COLS), BF), V((TOK, COLS), BF),
        V((L, SLABS, 2, 512, 512), BF), V((L, SLABS, 3, 2, 128, 512), BF), V((L, SLABS, 2, 128, 512), BF),
        V((L, SLABS, 3, 2, 32, 512), BF), V((L, SLABS, 2, 32, 512), BF), V((L, SLABS, 32, 512), BF),
        V((L, SLABS, 128, 512), BF),
        V((L, 8, D), F32), V((L, 1, 1024), F32), V((L, 2, COLS), F32), V((3, L, 8, COLS), F32),
        V((32, COLS), F32), V((4, 32, COLS), F32), V((4, 32, COLS), F32), V((32, COLS), F32),
        dma((L, 4)), dma((L, 4)), dma((L, 4)), dma((3, 3)), dma((3, 3)),
        dma((8, 5)), dma((8, 5)), dma((8, 6)), dma((8, 6)),
        dma((L, SLABS, 13)), dma((L, SLABS, 13)), dma((2, 3)), dma((2, 3)), dma((L, SLABS)), dma((4, 3)), dma((4, 3)),
    ]
    return pl.pallas_call(
        kernel,
        out_shape=[
            jax.ShapeDtypeStruct((TOK, COLS), BF),
            jax.ShapeDtypeStruct((TOK, COLS), BF),
            jax.ShapeDtypeStruct((L, SLABS, 512, 512), BF),
            jax.ShapeDtypeStruct((32, COLS), F32),
        ],
        in_specs=[vmem] * 6 + [hbm] * 4,
        out_specs=[vmem, vmem, hbm, vmem],
        scratch_shapes=scratch,
        compiler_params=pltpu.CompilerParams(
            collective_id=0, has_side_effects=True, vmem_limit_bytes=63 * 2**20
        ),
        name="encoder_step",
    )(*args)


def shards(
    hidden_in, seg_ids, key_mask, w_qkv, qv_bias, w_out, out_bias, ln_gain, ln_shift,
    w_up, up_bias, w_down, down_bias, grad_out,
):
    places = jnp.arange(TOK, dtype=jnp.int32)
    allowed = (seg_ids[:, None] == seg_ids[None, :]) & (
        (key_mask[None, :] == 1) | (places[:, None] == places[None, :])
    )
    zero = jnp.zeros((LAYERS, COLS), F32)
    small = jnp.stack(
        [out_bias, ln_gain[:, 0], ln_shift[:, 0], ln_gain[:, 1], ln_shift[:, 1], down_bias, zero, zero], axis=1
    ).reshape(LAYERS * 8, COLS)
    hout, gin, big, sums = step_call(
        hidden_in, grad_out, allowed.astype(F32), small, up_bias, qv_bias,
        w_qkv.reshape(LAYERS, 512, 768), w_out, w_up, w_down,
    )
    big = big.astype(F32)
    grad_down = big[:, 0:2].reshape(LAYERS, 1024, 512)
    grad_up = jnp.concatenate([big[:, 2], big[:, 3]], axis=2)
    value_part = jnp.concatenate([big[:, 5, 256:, :256], big[:, 5, 256:, 256:]], axis=1)
    grad_qkv = jnp.concatenate([big[:, 4], value_part], axis=2).reshape(LAYERS, 512, 3, COLS)
    grad_out_w = big[:, 5, :256]
    feature = sums[:16].reshape(LAYERS, 8, COLS)
    return (
        hout,
        gin,
        grad_qkv,
        sums[24:28].reshape(LAYERS, 2, COLS),
        grad_out_w,
        feature[:, 0],
        jnp.stack([feature[:, 1], feature[:, 3]], axis=1),
        jnp.stack([feature[:, 2], feature[:, 4]], axis=1),
        grad_up,
        sums[16:24].reshape(LAYERS, 1024),
        grad_down,
        feature[:, 5],
    )


def solution(mesh):
    tokens = P(("dp", "row"), "col")
    return jax.shard_map(
        shards,
        mesh=mesh,
        in_specs=(
            tokens, P(("dp", "row")), P(("dp", "row")), P(None, "row", None, "col"), P(None, None, "col"),
            P(None, "col", "row"), P(None, "col"), P(None, None, "col"), P(None, None, "col"),
            P(None, "row", "col"), P(None, "col"), P(None, "col", "row"), P(None, "col"), tokens,
        ),
        out_specs=(
            tokens, tokens, P(None, "row", None, "col"), P(None, None, "col"), P(None, "col", "row"),
            P(None, "col"), P(None, None, "col"), P(None, None, "col"), P(None, "row", "col"),
            P(None, "col"), P(None, "col", "row"), P(None, "col"),
        ),
        check_vma=False,
    )
```

```python
import functools

import jax
import jax.numpy as jnp
from jax import lax
from jax.experimental import pallas as pl
from jax.experimental.pallas import tpu as pltpu
from jax.sharding import PartitionSpec as P

D = 1024
HD = 64
LAYERS = 2
TOK = 256
OWN = 64
COLS = 256
HEADS_LOCAL = 4
SLABS = 6
EPSILON = 1e-05
MASKED = -1e30
SCALE = HD**-0.5
PARTS = ((0, 1, 2, 0), (0, 2, 3, 1), (1, 128, 512, 0), (2, 256, 640, 0), (2, 640, 1024, 1), (3, 128, 256, 0), (3, 256, 512, 1))
DIRECT = ((0, 0, 1), (1, 0, 128), (2, 0, 256), (3, 0, 128))
WEIGHT_ROWS = (512, 256, 512, 1024)
MESH = pl.DeviceIdType.MESH
BF = jnp.bfloat16
F32 = jnp.float32


def dot(a, b):
    return jnp.dot(a, b, preferred_element_type=F32)


def dot_nt(a, b):
    return lax.dot_general(a, b, (((1,), (1,)), ((), ())), preferred_element_type=F32)


def dot_tn(a, b):
    return lax.dot_general(a, b, (((0,), (0,)), ((), ())), preferred_element_type=F32)


def norm_back(upstream, normed, inverse, gain):
    scaled = upstream * gain
    mean_one = jnp.sum(scaled, axis=1, keepdims=True) / D
    mean_two = jnp.sum(scaled * normed, axis=1, keepdims=True) / D
    return inverse * (scaled - mean_one - normed * mean_two)


def kernel(
    hid, gout, seg, key, outb, gain, shift, downb, upb, qvb, wq, wo, wu, wd,
    hout, gin, gq, go, gu, gd, gsmall,
    mask, small, WQ, WO, WU, WD, PF, A2H, A2G, S, M, U, GS, GF, F1,
    STATE, MID, SEC, FIR, QKV, CTX, PR, DG, ACT, NRM, INV, LL, ML, GC,
    PS, XS, L1, L2, HS, HOB, GIB,
    G, R1, A1, R2, A2, R3, FB,
    SGF, SU, SQ, RC, SM, SZ, SY, SR,
    w_s, w_r, wd_s, wd_r, w_lsem, in_s, in_r, ag_s, ag_r, rs_s, rs_r, gr_s, gr_r, out_s, out_r, lsem, sm_s, sm_r,
):
    dp = lax.axis_index("dp")
    row = lax.axis_index("row")
    col = lax.axis_index("col")
    z, y = lax.div(dp, 4), lax.rem(dp, 4)
    xh, core = lax.div(col, 2), lax.rem(col, 2)
    col_core = xh * 2 + (1 - core)
    col_cross = (1 - xh) * 2 + core
    col_diag = (1 - xh) * 2 + (1 - core)
    core_dev = (dp, row, col_core)
    cross_dev = (dp, row, col_cross)
    row_dev = (dp, 1 - row, col)

    def col_dev(d):
        return (dp, row, lax.rem(col + d, 4))

    def axis_place(axis):
        return z if axis == 0 else y

    def axis_dev(axis, d):
        if axis == 0:
            return (lax.rem(z + d, 4) * 4 + y, row, col)
        return (z * 4 + lax.rem(y + d, 4), row, col)

    def chunk(j, rows=OWN):
        return pl.ds(pl.multiple_of(j * rows, rows), rows)

    def remote(src, dst, ssem, rsem, dev):
        return pltpu.make_async_remote_copy(
            src_ref=src, dst_ref=dst, send_sem=ssem, recv_sem=rsem, device_id=dev, device_id_type=MESH
        )

    barrier = pltpu.get_barrier_semaphore()
    for dev in [col_dev(1), col_dev(2), col_dev(3), row_dev] + [axis_dev(a, d) for a in (0, 1) for d in (1, 2, 3)]:
        pl.semaphore_signal(barrier, 1, device_id=dev, device_id_type=MESH)
    pl.semaphore_wait(barrier, 10)

    def in_copies(d):
        to = lax.rem(col + d, 4)
        dev = (dp, row, to)
        return [
            remote(hid.at[chunk(to)], A2H.at[:, chunk(col, COLS)], in_s.at[0, d - 1], in_r.at[0, d - 1], dev),
            remote(small, PF.at[:, chunk(col, COLS)], in_s.at[1, d - 1], in_r.at[1, d - 1], dev),
            remote(gout.at[chunk(to)], A2G.at[:, chunk(col, COLS)], in_s.at[2, d - 1], in_r.at[2, d - 1], dev),
        ]

    def in_arrivals(d):
        source = lax.rem(col + 4 - d, 4)
        return [
            remote(hid.at[chunk(col)], A2H.at[:, chunk(source, COLS)], in_s.at[0, d - 1], in_r.at[0, d - 1], col_dev(d)),
            remote(small, PF.at[:, chunk(source, COLS)], in_s.at[1, d - 1], in_r.at[1, d - 1], col_dev(d)),
            remote(gout.at[chunk(col)], A2G.at[:, chunk(source, COLS)], in_s.at[2, d - 1], in_r.at[2, d - 1], col_dev(d)),
        ]

    for l in range(LAYERS):
        rows = (outb[l : l + 1], gain[l, 0:1], shift[l, 0:1], gain[l, 1:2], shift[l, 1:2], downb[l : l + 1])
        for r in range(6):
            small[l * 8 + r : l * 8 + r + 1, :] = rows[r]
        small[l * 8 + 6 : l * 8 + 8, :] = jnp.zeros((2, COLS), F32)
    for d in (1, 2, 3):
        for c in in_copies(d)[:2]:
            c.start()

    pairs = ((wq, WQ), (wo, WO), (wu, WU), (wd, WD))

    def region(ref, n, lo, hi, rows):
        if n == 0:
            return ref.at[lo, rows, :]
        return ref.at[rows, pl.ds(lo, hi - lo)]

    def w_local(l, n):
        return pltpu.make_async_copy(pairs[n][0].at[l], pairs[n][1].at[l, row], w_lsem.at[l, n])

    def w_direct(l, n, which):
        rows = pl.ds(0, WEIGHT_ROWS[n])
        _, lo, hi = DIRECT[n]
        return remote(
            region(pairs[n][0].at[l], n, lo, hi, rows), region(pairs[n][1].at[l, which], n, lo, hi, rows),
            wd_s.at[l, n], wd_r.at[l, n], row_dev,
        )

    def part_axes(p):
        first = PARTS[p][3]
        return first, 1 - first

    def part_rows(p, a_place, b_place):
        piece = WEIGHT_ROWS[PARTS[p][0]] // 16
        return pl.ds(pl.multiple_of((b_place * 4 + a_place) * piece, piece), piece)

    def w_piece(l, p, which):
        n, lo, hi, _ = PARTS[p]
        first, second = part_axes(p)
        rows = part_rows(p, axis_place(first), axis_place(second))
        return remote(
            region(pairs[n][0].at[l], n, lo, hi, rows), region(pairs[n][1].at[l, which], n, lo, hi, rows),
            w_s.at[l, p, 0], w_r.at[l, p, 0], row_dev,
        )

    def w_one(l, p, d, place):
        n, lo, hi, _ = PARTS[p]
        first, second = part_axes(p)
        rows = part_rows(p, place, axis_place(second))
        ref = region(pairs[n][1].at[l, 1 - row], n, lo, hi, rows)
        return remote(ref, ref, w_s.at[l, p, d], w_r.at[l, p, d], axis_dev(first, d))

    def w_two(l, p, d, place):
        n, lo, hi, _ = PARTS[p]
        _, second = part_axes(p)
        block = WEIGHT_ROWS[n] // 4
        ref = region(pairs[n][1].at[l, 1 - row], n, lo, hi, chunk(place, block))
        return remote(ref, ref, w_s.at[l, p, 3 + d], w_r.at[l, p, 3 + d], axis_dev(second, d))

    def back(place, d):
        return lax.rem(place + 4 - d, 4)

    def w_step_one(l, p):
        w_piece(l, p, 1 - row).wait_recv()
        for d in (1, 2, 3):
            w_one(l, p, d, axis_place(part_axes(p)[0])).start()

    def w_step_two(l, p):
        first, second = part_axes(p)
        for d in (1, 2, 3):
            w_one(l, p, d, back(axis_place(first), d)).wait_recv()
        for d in (1, 2, 3):
            w_two(l, p, d, axis_place(second)).start()

    def w_wait(l, n):
        w_local(l, n).wait()
        w_direct(l, n, 1 - row).wait_recv()
        for p in range(len(PARTS)):
            if PARTS[p][0] == n:
                second = part_axes(p)[1]
                for d in (1, 2, 3):
                    w_two(l, p, d, back(axis_place(second), d)).wait_recv()

    def w_drain(l):
        for n in range(4):
            w_direct(l, n, row).wait_send()
        for p in range(len(PARTS)):
            first, second = part_axes(p)
            w_piece(l, p, row).wait_send()
            for d in (1, 2, 3):
                w_one(l, p, d, axis_place(first)).wait_send()
                w_two(l, p, d, axis_place(second)).wait_send()

    parts = range(len(PARTS))
    for p in parts:
        w_piece(0, p, row).start()
    w_direct(0, 0, row).start()
    for d in (1, 2, 3):
        in_copies(d)[2].start()
    for p in parts:
        w_piece(1, p, row).start()
    for l in range(LAYERS):
        for n in range(4):
            w_local(l, n).start()
            if l + n > 0:
                w_direct(l, n, row).start()
    for p in parts:
        w_step_one(0, p)

    seg_lanes = jnp.broadcast_to(seg[...].astype(F32), (TOK, TOK))
    key_lanes = jnp.broadcast_to(key[...].astype(F32), (TOK, TOK))
    same_place = lax.broadcasted_iota(jnp.int32, (TOK, TOK), 0) == lax.broadcasted_iota(jnp.int32, (TOK, TOK), 1)
    keep = jnp.where(same_place, 1.0, key_lanes)
    mask[...] = jnp.where(seg_lanes.T == seg_lanes, keep, 0.0)

    A2H[:, chunk(col, COLS)] = hid[chunk(col), :]
    A2G[:, chunk(col, COLS)] = gout[chunk(col), :]
    PF[:, chunk(col, COLS)] = small[...]
    for d in (1, 2, 3):
        for c in in_arrivals(d):
            c.wait_recv()
    S[...] = A2H[...].astype(F32)
    U[...] = A2G[...].astype(F32)
    w_step_two(0, 0)
    w_step_two(0, 1)

    def ag_send(k, X):
        out = []
        for p in (0, 1):
            rows = pl.ds(pl.multiple_of(col * OWN + p * 32, 32), 32)
            out.append(remote(X.at[rows], X.at[rows], ag_s.at[k, p], ag_r.at[k, p], cross_dev))
        out.append(remote(X.at[chunk(col)], X.at[chunk(col)], ag_s.at[k, 2], ag_r.at[k, 2], core_dev))
        return out

    def ag_forward(k, X, p):
        rows = pl.ds(pl.multiple_of(col_cross * OWN + p * 32, 32), 32)
        return remote(X.at[rows], X.at[rows], ag_s.at[k, 3 + p], ag_r.at[k, 3 + p], core_dev)

    def ag_start(k, X):
        for c in ag_send(k, X):
            c.start()

    def ag_finish(k, X):
        for p in (0, 1):
            rows = pl.ds(pl.multiple_of(col_cross * OWN + p * 32, 32), 32)
            remote(X.at[rows], X.at[rows], ag_s.at[k, p], ag_r.at[k, p], cross_dev).wait_recv()
            ag_forward(k, X, p).start()
        remote(X.at[chunk(col_core)], X.at[chunk(col_core)], ag_s.at[k, 2], ag_r.at[k, 2], core_dev).wait_recv()
        for p in (0, 1):
            rows = pl.ds(pl.multiple_of(col_diag * OWN + p * 32, 32), 32)
            remote(X.at[rows], X.at[rows], ag_s.at[k, 3 + p], ag_r.at[k, 3 + p], core_dev).wait_recv()

    def ag_drain(k, X):
        for c in ag_send(k, X):
            c.wait_send()
        for p in (0, 1):
            ag_forward(k, X, p).wait_send()

    def half(h):
        return pl.ds(h * 512, 512)

    def rs_first(k, par, h, t):
        to = (1 - xh) * 2 + (1 - core) if t == 0 else col_core
        return remote(
            PS.at[chunk(to), half(h)], L1.at[par, t, :, half(h)], rs_s.at[k, h * 3 + t], rs_r.at[k, h * 3 + t], core_dev
        )

    def rs_cross(k, par, h):
        return remote(XS.at[:, half(h)], L2.at[par, :, half(h)], rs_s.at[k, h * 3 + 2], rs_r.at[k, h * 3 + 2], cross_dev)

    def rs_send(k, par, h):
        for t in (0, 1):
            rs_first(k, par, h, t).start()

    def rs_mid(k, par, h):
        rs_first(k, par, h, 0).wait_recv()
        total = PS[chunk(col_cross), half(h)].astype(F32) + L1[par, 0, :, half(h)].astype(F32)
        XS[:, half(h)] = total.astype(BF)
        rs_cross(k, par, h).start()

    def rs_end(k, par, h):
        rs_first(k, par, h, 1).wait_recv()
        total = PS[chunk(col), half(h)].astype(F32) + L1[par, 1, :, half(h)].astype(F32)
        rs_cross(k, par, h).wait_recv()
        return total + L2[par, :, half(h)].astype(F32)

    def rs_drain(k, par):
        for h in (0, 1):
            for t in (0, 1):
                rs_first(k, par, h, t).wait_send()
            rs_cross(k, par, h).wait_send()

    def gr_one(l, s, d):
        axis = s % 2
        to = lax.rem(axis_place(axis) + d, 4)
        return remote(
            G.at[l, s, :, chunk(to, 128), :], R1.at[l, s, d - 1], gr_s.at[l, s, d - 1], gr_r.at[l, s, d - 1], axis_dev(axis, d)
        )

    def gr_two(l, s, d):
        axis = 1 - s % 2
        to = lax.rem(axis_place(axis) + d, 4)
        return remote(
            A1.at[l, s, :, chunk(to, 32), :], R2.at[l, s, d - 1], gr_s.at[l, s, 2 + d], gr_r.at[l, s, 2 + d], axis_dev(axis, d)
        )

    def gr_row(l, s):
        return remote(A2.at[l, s, 1 - row], R3.at[l, s], gr_s.at[l, s, 6], gr_r.at[l, s, 6], row_dev)

    def gr_four(l, s, d, place):
        axis = 1 - s % 2
        rows = FB.at[l, s, chunk(place, 32), :]
        return remote(rows, rows, gr_s.at[l, s, 6 + d], gr_r.at[l, s, 6 + d], axis_dev(axis, d))

    def places(l, s, place):
        if s < 2:
            return [(pl.ds(0, 128), pl.ds(0, 512), gd.at[l, pl.ds(pl.multiple_of(s * 512 + place * 128, 128), 128), :])]
        if s < 4:
            return [(pl.ds(0, 128), pl.ds(0, 512), gu.at[l, chunk(place, 128), pl.ds((s - 2) * 512, 512)])]
        if s == 4:
            return [(pl.ds(0, 128), pl.ds(j * COLS, COLS), gq.at[l, j, chunk(place, 128), :]) for j in (0, 1)]
        return [
            (pl.ds(0, 64), pl.ds(0, 512), go.at[l, chunk(place, 64), :]),
            (pl.ds(64, 64), pl.ds(0, COLS), gq.at[l, 2, chunk(place, 64), :]),
            (pl.ds(64, 64), pl.ds(COLS, COLS), gq.at[l, 2, pl.ds(pl.multiple_of(256 + place * 64, 64), 64), :]),
        ]

    def gr_five(l, s, d, place):
        axis = s % 2
        return [
            remote(
                FB.at[l, s, rows, lanes], to, gr_s.at[l, s, 6 + 3 * d + q + 1], gr_r.at[l, s, 6 + 3 * d + q + 1],
                axis_dev(axis, d),
            )
            for q, (rows, lanes, to) in enumerate(places(l, s, place))
        ]

    def gr_local(l, s):
        return [
            pltpu.make_async_copy(FB.at[l, s, rows, lanes], to, lsem.at[l, s, q])
            for q, (rows, lanes, to) in enumerate(places(l, s, axis_place(s % 2)))
        ]

    def t1(l, s):
        for d in (1, 2, 3):
            gr_one(l, s, d).start()

    def t2(l, s):
        for d in (1, 2, 3):
            gr_one(l, s, d).wait_recv()
        own = chunk(axis_place(s % 2), 128)
        for r in (0, 1):
            total = G[l, s, r, own, :].astype(F32)
            for d in (0, 1, 2):
                total = total + R1[l, s, d, r].astype(F32)
            A1[l, s, r] = total.astype(BF)
        for d in (1, 2, 3):
            gr_two(l, s, d).start()

    def t3(l, s):
        for d in (1, 2, 3):
            gr_two(l, s, d).wait_recv()
        own = chunk(axis_place(1 - s % 2), 32)
        for r in (0, 1):
            total = A1[l, s, r, own, :].astype(F32)
            for d in (0, 1, 2):
                total = total + R2[l, s, d, r].astype(F32)
            A2[l, s, r] = total.astype(BF)
        gr_row(l, s).start()

    def t4(l, s):
        gr_row(l, s).wait_recv()
        place = axis_place(1 - s % 2)
        FB[l, s, chunk(place, 32), :] = (A2[l, s, row].astype(F32) + R3[l, s].astype(F32)).astype(BF)
        for d in (1, 2, 3):
            gr_four(l, s, d, place).start()

    def t5(l, s):
        place = axis_place(1 - s % 2)
        for d in (1, 2, 3):
            gr_four(l, s, d, lax.rem(place + 4 - d, 4)).wait_recv()
        own = axis_place(s % 2)
        for d in (1, 2, 3):
            for c in gr_five(l, s, d, own):
                c.start()
        for c in gr_local(l, s):
            c.start()

    def t6(l, s):
        own = axis_place(s % 2)
        for d in (1, 2, 3):
            for c in gr_five(l, s, d, lax.rem(own + 4 - d, 4)):
                c.wait_recv()
        for c in gr_local(l, s):
            c.wait()
        place = axis_place(1 - s % 2)
        for d in (1, 2, 3):
            gr_one(l, s, d).wait_send()
            gr_two(l, s, d).wait_send()
            gr_four(l, s, d, place).wait_send()
            for c in gr_five(l, s, d, own):
                c.wait_send()
        gr_row(l, s).wait_send()

    def both(step, l, first):
        step(l, first)
        step(l, first + 1)

    def vec(l, r):
        return PF[pl.ds(l * 8 + r, 1), :]

    def norm_into(values, l, n, gain, shift):
        mean_row = jnp.sum(values, axis=1, keepdims=True) / D
        squares = jnp.sum(values * values, axis=1, keepdims=True) / D
        inverse = lax.rsqrt(squares - mean_row * mean_row + EPSILON)
        normed = (values - mean_row) * inverse
        NRM[l, n] = normed
        INV[l, n] = jnp.broadcast_to(inverse, (OWN, 128))
        return normed * gain + shift

    def forward(l, carry):
        X = STATE.at[l]
        X[chunk(col), :] = S[...].astype(BF)
        ag_start(l * 4, X)

        @pl.when(l == 0)
        def _():
            for p in parts[2:]:
                w_step_two(0, p)
            for p in parts:
                w_step_one(1, p)

        w_wait(l, 0)
        ag_finish(l * 4, X)
        for j in range(3):
            mixed = dot(STATE[l, :, :512], WQ[l, 0, j]) + dot(STATE[l, :, 512:], WQ[l, 1, j])
            if j != 1:
                mixed = mixed + qvb[l, j // 2 : j // 2 + 1, :]
            QKV[l, j] = mixed.astype(BF)
        ag_drain(l * 4, X)
        for h in range(HEADS_LOCAL):
            lanes = slice(h * HD, (h + 1) * HD)
            scores = dot_nt(QKV[l, 0, :, lanes], QKV[l, 1, :, lanes])
            scaled = jnp.where(mask[...] > 0.5, scores * SCALE, MASKED)
            raised = jnp.exp(scaled - jnp.max(scaled, axis=1, keepdims=True))
            probs = raised / jnp.sum(raised, axis=1, keepdims=True)
            PR[l, h] = probs
            CTX[l, :, lanes] = dot(probs.astype(BF), QKV[l, 2, :, lanes]).astype(BF)

        @pl.when(l == 0)
        def _():
            for p in parts:
                w_step_two(1, p)

        w_wait(l, 1)
        k = l * 4
        for h in (0, 1):
            PS[:, half(h)] = dot(CTX[l], WO[l, h]).astype(BF)
            rs_send(k, 0, h)
        rs_mid(k, 0, 0)
        rs_mid(k, 0, 1)
        for h in (0, 1):
            F1[:, half(h)] = S[:, half(h)] + rs_end(k, 0, h)
        rs_drain(k, 0)
        middle = norm_into(F1[...] + vec(l, 0), l, 0, vec(l, 1), vec(l, 2))
        M[...] = middle
        X = MID.at[l]
        X[chunk(col), :] = middle.astype(BF)
        ag_start(l * 4 + 1, X)
        w_wait(l, 2)
        ag_finish(l * 4 + 1, X)

        def lift(n, c):
            lanes = chunk(n, COLS)
            lifted = dot(MID[l, :, :512], WU[l, 0, :, lanes]) + dot(MID[l, :, 512:], WU[l, 1, :, lanes])
            lifted = lifted + upb[pl.ds(l, 1), lanes]
            phi = 0.5 * (1.0 + lax.erf(lifted * (0.5**0.5)))
            density = jnp.exp(-0.5 * lifted * lifted) * 0.3989422804014327
            DG[l, :, lanes] = phi + lifted * density
            ACT[l, :, lanes] = (lifted * phi).astype(BF)
            return c

        lax.fori_loop(0, 4, lift, 0)
        ag_drain(l * 4 + 1, X)
        w_wait(l, 3)
        k = l * 4 + 1
        for h in (0, 1):
            for q in (0, 1):
                lanes = pl.ds(h * 512 + q * 256, 256)
                PS[:, lanes] = dot(ACT[l], WD[l, h, :, pl.ds(q * 256, 256)]).astype(BF)
            rs_send(k, 1, h)
        rs_mid(k, 1, 0)
        rs_mid(k, 1, 1)
        for h in (0, 1):
            F1[:, half(h)] = M[:, half(h)] + rs_end(k, 1, h)
        rs_drain(k, 1)
        S[...] = norm_into(F1[...] + vec(l, 5), l, 1, vec(l, 3), vec(l, 4))
        return carry

    lax.fori_loop(0, LAYERS, forward, 0)

    def out_copies(n, d):
        buf = (HOB, GIB)[n]
        to = lax.rem(col + d, 4)
        return remote(
            HS.at[n, :, chunk(to, COLS)], buf.at[chunk(col)], out_s.at[n, d - 1], out_r.at[n, d - 1], (dp, row, to)
        )

    def out_arrivals(n, d):
        buf = (HOB, GIB)[n]
        source = lax.rem(col + 4 - d, 4)
        return remote(
            HS.at[n, :, chunk(col, COLS)], buf.at[chunk(source)], out_s.at[n, d - 1], out_r.at[n, d - 1], col_dev(d)
        )

    HS[0] = S[...].astype(BF)
    for d in (1, 2, 3):
        out_copies(0, d).start()
    HOB[chunk(col), :] = HS[0, :, chunk(col, COLS)]

    def backward(i, carry):
        l = LAYERS - 1 - i
        prev = l + 1
        upstream = U[...]
        normed = NRM[l, 1]
        SGF[l, 3:4, :] = jnp.sum(upstream * normed, axis=0, keepdims=True)
        SGF[l, 4:5, :] = jnp.sum(upstream, axis=0, keepdims=True)
        grad_second = norm_back(upstream, normed, INV[l, 1, :, :1], vec(l, 3))
        GS[...] = grad_second
        SGF[l, 5:6, :] = jnp.sum(grad_second, axis=0, keepdims=True)
        SEC[chunk(col), :] = grad_second.astype(BF)
        k = l * 4 + 2
        ag_start(k, SEC)

        @pl.when(i > 0)
        def _():
            both(t2, prev, 2)
            both(t3, prev, 0)

        ag_finish(k, SEC)

        def pull(n, c):
            lanes = chunk(n, COLS)
            grad_act = dot_nt(SEC[:, :512], WD[l, 0, lanes, :]) + dot_nt(SEC[:, 512:], WD[l, 1, lanes, :])
            grad_lifted = grad_act * DG[l, :, lanes]
            SU[l, :, lanes] = jnp.sum(grad_lifted, axis=0, keepdims=True)
            LL[:, lanes] = grad_lifted.astype(BF)
            return c

        lax.fori_loop(0, 4, pull, 0)
        for h in (0, 1):
            for q in (0, 1):
                lanes = pl.ds(h * 512 + q * 256, 256)
                PS[:, lanes] = dot_nt(LL[...], WU[l, h, pl.ds(q * 256, 256), :]).astype(BF)
            rs_send(k, 0, h)
        rs_mid(k, 0, 0)
        rs_mid(k, 0, 1)

        def down_grad(f, c):
            total = dot_tn(ACT[l, :, chunk(f, COLS)], SEC[...]).astype(BF)
            rows = chunk(lax.rem(f, 2), COLS)
            for r in (0, 1):
                G[l, lax.div(f, 2), r, rows, :] = total[:, r * 512 : (r + 1) * 512]
            return c

        lax.fori_loop(0, 4, down_grad, 0)
        both(t1, l, 0)
        ag_drain(k, SEC)

        @pl.when(i > 0)
        def _():
            both(t2, prev, 4)
            both(t3, prev, 2)
            both(t4, prev, 0)

        for h in (0, 1):
            GS[:, half(h)] = GS[:, half(h)] + rs_end(k, 0, h)
        rs_drain(k, 0)
        grad_middle = GS[...]
        normed = NRM[l, 0]
        SGF[l, 1:2, :] = jnp.sum(grad_middle * normed, axis=0, keepdims=True)
        SGF[l, 2:3, :] = jnp.sum(grad_middle, axis=0, keepdims=True)
        grad_first = norm_back(grad_middle, normed, INV[l, 0, :, :1], vec(l, 1))
        GF[...] = grad_first
        SGF[l, 0:1, :] = jnp.sum(grad_first, axis=0, keepdims=True)
        FIR[chunk(col), :] = grad_first.astype(BF)
        k = l * 4 + 3
        ag_start(k, FIR)

        def up_grad(n, c):
            total = dot_tn(MID[l, :, chunk(n, COLS)], LL[...]).astype(BF)
            rows = chunk(lax.rem(n, 2), COLS)
            for r in (0, 1):
                G[l, 2 + r, lax.div(n, 2), rows, :] = total[:, r * 512 : (r + 1) * 512]
            return c

        lax.fori_loop(0, 4, up_grad, 0)
        both(t1, l, 2)

        @pl.when(i > 0)
        def _():
            both(t3, prev, 4)
            both(t4, prev, 2)
            both(t5, prev, 0)

        ag_finish(k, FIR)
        GC[...] = (dot_nt(FIR[:, :512], WO[l, 0]) + dot_nt(FIR[:, 512:], WO[l, 1])).astype(BF)
        for h in range(HEADS_LOCAL):
            lanes = slice(h * HD, (h + 1) * HD)
            probs = PR[l, h]
            grad_probs = dot_nt(GC[:, lanes], QKV[l, 2, :, lanes])
            centre = jnp.sum(probs * grad_probs, axis=1, keepdims=True)
            grad_scores = (probs * (grad_probs - centre) * SCALE).astype(BF)
            grad_query = dot(grad_scores, QKV[l, 1, :, lanes])
            grad_key = dot_tn(grad_scores, QKV[l, 0, :, lanes])
            grad_value = dot_tn(probs.astype(BF), GC[:, lanes])
            SQ[l, 0:1, lanes] = jnp.sum(grad_query, axis=0, keepdims=True)
            SQ[l, 1:2, lanes] = jnp.sum(grad_value, axis=0, keepdims=True)
            ML[:, h * HD : (h + 1) * HD] = grad_query.astype(BF)
            ML[:, COLS + h * HD : COLS + (h + 1) * HD] = grad_key.astype(BF)
            ML[:, 2 * COLS + h * HD : 2 * COLS + (h + 1) * HD] = grad_value.astype(BF)
        for h in (0, 1):
            for q in (0, 1):
                lanes = pl.ds(h * 512 + q * 256, 256)
                PS[:, lanes] = sum(
                    dot_nt(ML[:, j * COLS : (j + 1) * COLS], WQ[l, h, j, pl.ds(q * 256, 256), :]) for j in range(3)
                ).astype(BF)
            rs_send(k, 1, h)
        rs_mid(k, 1, 0)
        rs_mid(k, 1, 1)
        total = dot_tn(CTX[l], FIR[...]).astype(BF)
        for r in (0, 1):
            for q in range(4):
                G[l, 5, r, q * 128 : q * 128 + 64, :] = total[q * 64 : (q + 1) * 64, r * 512 : (r + 1) * 512]

        def qkv_grad(r, c):
            for q in (0, 1):
                total = dot_tn(STATE[l, :, chunk(2 * r + q, COLS)], ML[...]).astype(BF)
                G[l, 4, r, q * 256 : (q + 1) * 256, :] = total[:, :512]
                for b in range(4):
                    G[l, 5, r, b * 128 + 64 : b * 128 + 128, q * 256 : (q + 1) * 256] = total[b * 64 : (b + 1) * 64, 512:]
            return c

        lax.fori_loop(0, 2, qkv_grad, 0)
        both(t1, l, 4)
        ag_drain(k, FIR)
        both(t2, l, 0)

        @pl.when(i > 0)
        def _():
            both(t4, prev, 4)
            both(t5, prev, 2)

        for h in (0, 1):
            U[:, half(h)] = GF[:, half(h)] + rs_end(k, 1, h)
        rs_drain(k, 1)
        return carry

    lax.fori_loop(0, LAYERS, backward, 0)

    HS[1] = U[...].astype(BF)
    for d in (1, 2, 3):
        out_copies(1, d).start()
    GIB[chunk(col), :] = HS[1, :, chunk(col, COLS)]

    def sc_copy(d):
        to = lax.rem(col + d, 4)
        return remote(SGF.at[:, :, chunk(to, COLS)], RC.at[d - 1], sm_s.at[0, d - 1], sm_r.at[0, d - 1], (dp, row, to))

    def sd_copy(axis, d, place):
        buf = (SZ, SY)[axis]
        return remote(
            buf.at[axis_place(axis)], buf.at[place], sm_s.at[1 + axis, d - 1], sm_r.at[1 + axis, d - 1], axis_dev(axis, d)
        )

    def sr_copy():
        return remote(SM, SR, sm_s.at[3, 0], sm_r.at[3, 0], row_dev)

    for d in (1, 2, 3):
        sc_copy(d).start()
    both(t2, 0, 2)
    both(t3, 0, 0)
    both(t5, 1, 4)
    for d in (1, 2, 3):
        sc_copy(d).wait_recv()
    feature = SGF[:, :, chunk(col, COLS)]
    for d in (0, 1, 2):
        feature = feature + RC[d]
    for l in range(LAYERS):
        SZ[z, 8 * l : 8 * l + 8, :] = feature[l]
        for q in range(4):
            SZ[z, 16 + 4 * l + q : 17 + 4 * l + q, :] = SU[l, :, q * COLS : (q + 1) * COLS]
        SZ[z, 24 + 2 * l : 26 + 2 * l, :] = SQ[l]
    SZ[z, 28:32, :] = jnp.zeros((4, COLS), F32)
    for d in (1, 2, 3):
        sd_copy(0, d, z).start()
    both(t2, 0, 4)
    both(t3, 0, 2)
    both(t4, 0, 0)
    for d in (1, 2, 3):
        sd_copy(0, d, lax.rem(z + 4 - d, 4)).wait_recv()
    SY[y] = SZ[0] + SZ[1] + SZ[2] + SZ[3]
    for d in (1, 2, 3):
        sd_copy(1, d, y).start()
    both(t3, 0, 4)
    both(t4, 0, 2)
    both(t5, 0, 0)
    for d in (1, 2, 3):
        sd_copy(1, d, lax.rem(y + 4 - d, 4)).wait_recv()
    SM[...] = SY[0] + SY[1] + SY[2] + SY[3]
    sr_copy().start()
    both(t4, 0, 4)
    both(t5, 0, 2)
    sr_copy().wait_recv()
    gsmall[...] = SM[...] + SR[...]
    both(t5, 0, 4)

    for n in (0, 1):
        for d in (1, 2, 3):
            out_arrivals(n, d).wait_recv()
    hout[...] = HOB[...]
    gin[...] = GIB[...]

    for d in (1, 2, 3):
        for c in in_copies(d):
            c.wait_send()
        for n in (0, 1):
            out_copies(n, d).wait_send()
        sc_copy(d).wait_send()
        sd_copy(0, d, z).wait_send()
        sd_copy(1, d, y).wait_send()
    sr_copy().wait_send()
    for l in range(LAYERS):
        w_drain(l)

    def finish(l, c):
        for s in range(SLABS):
            t6(l, s)
        return c

    lax.fori_loop(0, LAYERS, finish, 0)


def step_call(*args):
    vmem = pl.BlockSpec(memory_space=pltpu.VMEM)
    hbm = pl.BlockSpec(memory_space=pl.ANY)
    dma = pltpu.SemaphoreType.DMA
    V = pltpu.VMEM
    L = LAYERS
    scratch = [
        V((TOK, TOK), F32), V((16, COLS), F32),
        V((L, 2, 3, 512, COLS), BF), V((L, 2, 256, 512), BF), V((L, 2, 512, 1024), BF), V((L, 2, 1024, 512), BF),
        V((16, 1024), F32), V((OWN, D), BF), V((OWN, D), BF),
        V((OWN, D), F32), V((OWN, D), F32), V((OWN, D), F32), V((OWN, D), F32), V((OWN, D), F32), V((OWN, D), F32),
        V((L, TOK, D), BF), V((L, TOK, D), BF), V((TOK, D), BF), V((TOK, D), BF),
        V((L, 3, TOK, COLS), BF), V((L, TOK, COLS), BF), V((L, HEADS_LOCAL, TOK, TOK), F32),
        V((L, TOK, 1024), F32), V((L, TOK, 1024), BF), V((L, 2, OWN, D), F32), V((L, 2, OWN, 128), F32),
        V((TOK, 1024), BF), V((TOK, 768), BF), V((TOK, COLS), BF),
        V((TOK, D), BF), V((OWN, D), BF), V((2, 2, OWN, D), BF), V((2, OWN, D), BF),
        V((2, OWN, D), BF), V((TOK, COLS), BF), V((TOK, COLS), BF),
        V((L, SLABS, 2, 512, 512), BF), V((L, SLABS, 3, 2, 128, 512), BF), V((L, SLABS, 2, 128, 512), BF),
        V((L, SLABS, 3, 2, 32, 512), BF), V((L, SLABS, 2, 32, 512), BF), V((L, SLABS, 32, 512), BF),
        V((L, SLABS, 128, 512), BF),
        V((L, 8, D), F32), V((L, 1, 1024), F32), V((L, 2, COLS), F32), V((3, L, 8, COLS), F32),
        V((32, COLS), F32), V((4, 32, COLS), F32), V((4, 32, COLS), F32), V((32, COLS), F32),
        dma((L, 7, 7)), dma((L, 7, 7)), dma((L, 4)), dma((L, 4)), dma((L, 4)), dma((3, 3)), dma((3, 3)),
        dma((8, 5)), dma((8, 5)), dma((8, 6)), dma((8, 6)),
        dma((L, SLABS, 19)), dma((L, SLABS, 19)), dma((2, 3)), dma((2, 3)), dma((L, SLABS, 3)), dma((4, 3)), dma((4, 3)),
    ]
    return pl.pallas_call(
        kernel,
        out_shape=[
            jax.ShapeDtypeStruct((TOK, COLS), BF),
            jax.ShapeDtypeStruct((TOK, COLS), BF),
            jax.ShapeDtypeStruct((L, 3, 512, COLS), BF),
            jax.ShapeDtypeStruct((L, 256, 512), BF),
            jax.ShapeDtypeStruct((L, 512, 1024), BF),
            jax.ShapeDtypeStruct((L, 1024, 512), BF),
            jax.ShapeDtypeStruct((32, COLS), F32),
        ],
        in_specs=[vmem] * 10 + [hbm] * 4,
        out_specs=[vmem, vmem, hbm, hbm, hbm, hbm, vmem],
        scratch_shapes=scratch,
        compiler_params=pltpu.CompilerParams(
            collective_id=0, has_side_effects=True, vmem_limit_bytes=63 * 2**20
        ),
        name="encoder_step",
    )(*args)


def split_small(hout, gin, sums, out_h, out_g, qvb, outb, gain, shift, upb, downb):
    out_h[...] = hout[...]
    out_g[...] = gin[...]
    for l in range(LAYERS):
        outb[l : l + 1, :] = sums[8 * l : 8 * l + 1, :]
        for n in (0, 1):
            gain[l, n : n + 1, :] = sums[8 * l + 1 + 2 * n : 8 * l + 2 + 2 * n, :]
            shift[l, n : n + 1, :] = sums[8 * l + 2 + 2 * n : 8 * l + 3 + 2 * n, :]
        downb[l : l + 1, :] = sums[8 * l + 5 : 8 * l + 6, :]
        for q in range(4):
            upb[l : l + 1, q * COLS : (q + 1) * COLS] = sums[16 + 4 * l + q : 17 + 4 * l + q, :]
        qvb[l] = sums[24 + 2 * l : 26 + 2 * l, :]


def split_call(hout, gin, sums):
    vmem = pl.BlockSpec(memory_space=pltpu.VMEM)
    shapes = ((LAYERS, 2, COLS), (LAYERS, COLS), (LAYERS, 2, COLS), (LAYERS, 2, COLS), (LAYERS, 1024), (LAYERS, COLS))
    return pl.pallas_call(
        split_small,
        out_shape=[jax.ShapeDtypeStruct((TOK, COLS), BF)] * 2 + [jax.ShapeDtypeStruct(d, F32) for d in shapes],
        in_specs=[vmem] * 3,
        out_specs=[vmem] * 8,
        name="split_small",
    )(hout, gin, sums)


def shards(
    hidden_in, seg_ids, key_mask, w_qkv, qv_bias, w_out, out_bias, ln_gain, ln_shift,
    w_up, up_bias, w_down, down_bias, grad_out,
):
    hout, gin, grad_qkv, grad_out_w, grad_up, grad_down, sums = step_call(
        hidden_in, grad_out, seg_ids.reshape(1, TOK), key_mask.reshape(1, TOK), out_bias, ln_gain, ln_shift, down_bias,
        up_bias, qv_bias, w_qkv.transpose(0, 2, 1, 3), w_out, w_up, w_down,
    )
    hout, gin, qvb, outb, gain, shift, upb, downb = split_call(hout, gin, sums)
    return (
        hout,
        gin,
        grad_qkv.astype(F32).transpose(0, 2, 1, 3),
        qvb,
        grad_out_w.astype(F32),
        outb,
        gain,
        shift,
        grad_up.astype(F32),
        upb,
        grad_down.astype(F32),
        downb,
    )


def solution(mesh):
    tokens = P(("dp", "row"), "col")
    return jax.shard_map(
        shards,
        mesh=mesh,
        in_specs=(
            tokens, P(("dp", "row")), P(("dp", "row")), P(None, "row", None, "col"), P(None, None, "col"),
            P(None, "col", "row"), P(None, "col"), P(None, None, "col"), P(None, None, "col"),
            P(None, "row", "col"), P(None, "col"), P(None, "col", "row"), P(None, "col"), tokens,
        ),
        out_specs=(
            tokens, tokens, P(None, "row", None, "col"), P(None, None, "col"), P(None, "col", "row"),
            P(None, "col"), P(None, None, "col"), P(None, None, "col"), P(None, "row", "col"),
            P(None, "col"), P(None, "col", "row"), P(None, "col"),
        ),
        check_vma=False,
    )
```

```python
import functools

import jax
import jax.numpy as jnp
from jax import lax
from jax.experimental import pallas as pl
from jax.experimental.pallas import tpu as pltpu
from jax.sharding import PartitionSpec as P

D = 1024
HD = 64
LAYERS = 2
TOK = 256
OWN = 64
COLS = 256
HEADS_LOCAL = 4
SLABS = 6
EPSILON = 1e-05
MASKED = -1e30
SCALE = HD**-0.5
PARTS = ((0, 1, 2, 0), (0, 2, 3, 1), (1, 0, 512, 0), (2, 0, 512, 0), (2, 512, 1024, 1), (3, 0, 256, 0), (3, 256, 512, 1))
WEIGHT_ROWS = (512, 256, 512, 1024)
MESH = pl.DeviceIdType.MESH
BF = jnp.bfloat16
F32 = jnp.float32


def dot(a, b):
    return jnp.dot(a, b, preferred_element_type=F32)


def dot_nt(a, b):
    return lax.dot_general(a, b, (((1,), (1,)), ((), ())), preferred_element_type=F32)


def dot_tn(a, b):
    return lax.dot_general(a, b, (((0,), (0,)), ((), ())), preferred_element_type=F32)


def norm_back(upstream, normed, inverse, gain):
    scaled = upstream * gain
    mean_one = jnp.sum(scaled, axis=1, keepdims=True) / D
    mean_two = jnp.sum(scaled * normed, axis=1, keepdims=True) / D
    return inverse * (scaled - mean_one - normed * mean_two)


def kernel(
    hid, gout, seg, key, outb, gain, shift, downb, upb, qvb, wq, wo, wu, wd,
    hout, gin, gq, go, gu, gd, gsmall,
    mask, small, WQ, WO, WU, WD, PF, A2H, A2G, S, M, U, GS, GF, F1,
    STATE, MID, SEC, FIR, QKV, CTX, PR, DG, ACT, NRM, INV, LL, ML, GC,
    PS, XS, L1, L2, HS, HOB, GIB,
    G, RL, R1, A1, R2, A2, R3, FB,
    SGF, SU, SQ, RC, SM, SZ, SY, SR,
    w_s, w_r, w_rb, wd_s, wd_r, w_lsem, in_s, in_r, ag_s, ag_r, rs_s, rs_r, gr_s, gr_r, out_s, out_r, lsem, sm_s, sm_r,
):
    dp = lax.axis_index("dp")
    row = lax.axis_index("row")
    col = lax.axis_index("col")
    z, y = lax.div(dp, 4), lax.rem(dp, 4)
    xh, core = lax.div(col, 2), lax.rem(col, 2)
    col_core = xh * 2 + (1 - core)
    col_cross = (1 - xh) * 2 + core
    col_diag = (1 - xh) * 2 + (1 - core)
    core_dev = (dp, row, col_core)
    cross_dev = (dp, row, col_cross)
    row_dev = (dp, 1 - row, col)

    def col_dev(d):
        return (dp, row, lax.rem(col + d, 4))

    def axis_place(axis):
        return z if axis == 0 else y

    def axis_dev(axis, d):
        if axis == 0:
            return (lax.rem(z + d, 4) * 4 + y, row, col)
        return (z * 4 + lax.rem(y + d, 4), row, col)

    def chunk(j, rows=OWN):
        return pl.ds(pl.multiple_of(j * rows, rows), rows)

    def remote(src, dst, ssem, rsem, dev):
        return pltpu.make_async_remote_copy(
            src_ref=src, dst_ref=dst, send_sem=ssem, recv_sem=rsem, device_id=dev, device_id_type=MESH
        )

    def arrived(ref, sem):
        pltpu.make_async_copy(ref, ref, sem).wait()

    barrier = pltpu.get_barrier_semaphore()
    for dev in [col_dev(1), col_dev(2), col_dev(3), row_dev] + [axis_dev(a, d) for a in (0, 1) for d in (1, 2, 3)]:
        pl.semaphore_signal(barrier, 1, device_id=dev, device_id_type=MESH)
    pl.semaphore_wait(barrier, 10)

    def in_copies(d):
        to = lax.rem(col + d, 4)
        dev = (dp, row, to)
        return [
            remote(hid.at[chunk(to)], A2H.at[:, chunk(col, COLS)], in_s.at[0], in_r.at[0], dev),
            remote(small, PF.at[:, chunk(col, COLS)], in_s.at[1], in_r.at[1], dev),
            remote(gout.at[chunk(to)], A2G.at[:, chunk(col, COLS)], in_s.at[2], in_r.at[2], dev),
        ]

    for l in range(LAYERS):
        rows = (outb[l : l + 1], gain[l, 0:1], shift[l, 0:1], gain[l, 1:2], shift[l, 1:2], downb[l : l + 1])
        for r in range(6):
            small[l * 8 + r : l * 8 + r + 1, :] = rows[r]
        small[l * 8 + 6 : l * 8 + 8, :] = jnp.zeros((2, COLS), F32)
    for d in (1, 2, 3):
        for c in in_copies(d)[:2]:
            c.start()

    pairs = ((wq, WQ), (wo, WO), (wu, WU), (wd, WD))

    def region(ref, n, lo, hi, rows):
        if n == 0:
            return ref.at[lo, rows, :]
        return ref.at[rows, pl.ds(lo, hi - lo)]

    def w_local(l, n):
        return pltpu.make_async_copy(pairs[n][0].at[l], pairs[n][1].at[l, row], w_lsem.at[l, n])

    def w_direct(l, which):
        return remote(wq.at[l, 0], WQ.at[l, which, 0], wd_s.at[l], wd_r.at[l], row_dev)

    def part_axes(p):
        first = PARTS[p][3]
        return first, 1 - first

    def part_rows(p, a_place, b_place):
        piece = WEIGHT_ROWS[PARTS[p][0]] // 16
        return pl.ds(pl.multiple_of((b_place * 4 + a_place) * piece, piece), piece)

    def w_piece(l, p, which):
        n, lo, hi, _ = PARTS[p]
        first, second = part_axes(p)
        rows = part_rows(p, axis_place(first), axis_place(second))
        return remote(
            region(pairs[n][0].at[l], n, lo, hi, rows), region(pairs[n][1].at[l, which], n, lo, hi, rows),
            w_s.at[l, 0], w_r.at[l, p, 0], row_dev,
        )

    def w_one(l, p, d, place):
        n, lo, hi, _ = PARTS[p]
        first, second = part_axes(p)
        rows = part_rows(p, place, axis_place(second))
        ref = region(pairs[n][1].at[l, 1 - row], n, lo, hi, rows)
        return remote(ref, ref, w_s.at[l, 1], w_r.at[l, p, 1], axis_dev(first, d))

    def w_two(l, p, d, place):
        n, lo, hi, _ = PARTS[p]
        _, second = part_axes(p)
        block = WEIGHT_ROWS[n] // 4
        ref = region(pairs[n][1].at[l, 1 - row], n, lo, hi, chunk(place, block))
        return remote(ref, ref, w_s.at[l, 2], w_rb.at[l, n], axis_dev(second, d))

    def w_step_one(l, p):
        w_piece(l, p, 1 - row).wait_recv()
        for d in (1, 2, 3):
            w_one(l, p, d, axis_place(part_axes(p)[0])).start()

    def three_pieces(l, p):
        n, lo, hi, _ = PARTS[p]
        piece = WEIGHT_ROWS[n] // 16
        return region(pairs[n][1].at[l, 1 - row], n, lo, hi, pl.ds(0, 3 * piece))

    def w_step_two(l, p):
        second = part_axes(p)[1]
        arrived(three_pieces(l, p), w_r.at[l, p, 1])
        for d in (1, 2, 3):
            w_two(l, p, d, axis_place(second)).start()

    def w_wait(l, n):
        w_local(l, n).wait()
        rows = WEIGHT_ROWS[n] * 3 // 4
        if n == 0:
            w_direct(l, 1 - row).wait_recv()
            arrived(WQ.at[l, 1 - row, pl.ds(0, 2), pl.ds(0, rows), :], w_rb.at[l, n])
        else:
            arrived(pairs[n][1].at[l, 1 - row, pl.ds(0, rows), :], w_rb.at[l, n])

    def w_drain(l):
        w_direct(l, row).wait_send()
        arrived(WU.at[0, 0, pl.ds(0, 176), pl.ds(0, 512)], w_s.at[l, 0])
        arrived(WQ.at[0, :, :, pl.ds(0, 176), :], w_s.at[l, 1])
        arrived(WQ.at[:, :, :, pl.ds(0, 352), :], w_s.at[l, 2])

    parts = range(len(PARTS))
    for p in parts:
        w_piece(0, p, row).start()
    w_direct(0, row).start()
    for n in range(4):
        w_local(0, n).start()
    for p in parts:
        w_step_one(0, p)
    for d in (1, 2, 3):
        in_copies(d)[2].start()
    for n in range(4):
        w_local(1, n).start()

    seg_lanes = jnp.broadcast_to(seg[...].astype(F32), (TOK, TOK))
    key_lanes = jnp.broadcast_to(key[...].astype(F32), (TOK, TOK))
    same_place = lax.broadcasted_iota(jnp.int32, (TOK, TOK), 0) == lax.broadcasted_iota(jnp.int32, (TOK, TOK), 1)
    keep = jnp.where(same_place, 1.0, key_lanes)
    mask[...] = jnp.where(seg_lanes.T == seg_lanes, keep, 0.0)

    A2H[:, chunk(col, COLS)] = hid[chunk(col), :]
    A2G[:, chunk(col, COLS)] = gout[chunk(col), :]
    PF[:, chunk(col, COLS)] = small[...]
    arrived(A2H.at[:, pl.ds(0, 3 * COLS)], in_r.at[0])
    arrived(PF.at[:, pl.ds(0, 3 * COLS)], in_r.at[1])
    arrived(A2G.at[:, pl.ds(0, 3 * COLS)], in_r.at[2])
    S[...] = A2H[...].astype(F32)
    U[...] = A2G[...].astype(F32)
    w_step_two(0, 0)
    w_step_two(0, 1)

    def ag_rows(owner, p):
        return pl.ds(pl.multiple_of(owner * OWN + p * 32, 32), 32)

    def ag_send(X):
        out = []
        for p in (0, 1):
            rows = ag_rows(col, p)
            out.append(remote(X.at[rows], X.at[rows], ag_s.at[0], ag_r.at[p], cross_dev))
        out.append(remote(X.at[chunk(col)], X.at[chunk(col)], ag_s.at[0], ag_r.at[2], core_dev))
        return out

    def ag_start(X):
        for c in ag_send(X):
            c.start()

    def ag_finish(X):
        for p in (0, 1):
            rows = ag_rows(col_cross, p)
            arrived(X.at[rows], ag_r.at[p])
            remote(X.at[rows], X.at[rows], ag_s.at[0], ag_r.at[3], core_dev).start()
        arrived(X.at[chunk(col_core)], ag_r.at[2])
        arrived(X.at[chunk(col_diag)], ag_r.at[3])

    def ag_drain(X):
        arrived(X.at[pl.ds(0, 3 * OWN)], ag_s.at[0])

    def half(h):
        return pl.ds(h * 512, 512)

    def rs_first(par, h, t):
        to = (1 - xh) * 2 + (1 - core) if t == 0 else col_core
        return remote(
            PS.at[chunk(to), half(h)], L1.at[par, t, :, half(h)], rs_s.at[0], rs_r.at[h * 3 + t], core_dev
        )

    def rs_cross(par, h):
        return remote(XS.at[:, half(h)], L2.at[par, :, half(h)], rs_s.at[0], rs_r.at[h * 3 + 2], cross_dev)

    def rs_send(par, h):
        for t in (0, 1):
            rs_first(par, h, t).start()

    def rs_mid(par, h):
        rs_first(par, h, 0).wait_recv()
        total = PS[chunk(col_cross), half(h)].astype(F32) + L1[par, 0, :, half(h)].astype(F32)
        XS[:, half(h)] = total.astype(BF)
        rs_cross(par, h).start()

    def rs_end(par, h):
        rs_first(par, h, 1).wait_recv()
        total = PS[chunk(col), half(h)].astype(F32) + L1[par, 1, :, half(h)].astype(F32)
        rs_cross(par, h).wait_recv()
        return total + L2[par, :, half(h)].astype(F32)

    def rs_drain():
        arrived(PS.at[pl.ds(0, 3 * OWN)], rs_s.at[0])

    first_half, second_half = pl.ds(0, 256), pl.ds(256, 256)

    def gr_block(l, s, d, lanes):
        return G.at[l, s, :, chunk(lax.rem(axis_place(s % 2) + d, 4), 128), lanes]

    def gr_relay(l, s, side):
        lanes, d = ((first_half, 1), (second_half, 3))[side]
        return remote(gr_block(l, s, 2, lanes), RL.at[l, s, side], gr_s.at[l, 0], gr_r.at[l, s, 0], axis_dev(s % 2, d))

    def gr_one(l, s, side, lanes):
        d = (1, 3)[side]
        return remote(
            gr_block(l, s, d, lanes), R1.at[l, s, side, :, :, lanes], gr_s.at[l, 1], gr_r.at[l, s, 1], axis_dev(s % 2, d)
        )

    def gr_two(l, s, d):
        axis = 1 - s % 2
        to = lax.rem(axis_place(axis) + d, 4)
        return remote(A1.at[l, s, :, chunk(to, 32), :], R2.at[l, s, d - 1], gr_s.at[l, 2], gr_r.at[l, s, 2], axis_dev(axis, d))

    def gr_row(l, s):
        return remote(A2.at[l, s, 1 - row], R3.at[l, s], gr_s.at[l, 3], gr_r.at[l, s, 3], row_dev)

    def gr_four(l, s, d, place):
        rows = FB.at[l, s, chunk(place, 32), :]
        return remote(rows, rows, gr_s.at[l, 4], gr_r.at[l, s, 4], axis_dev(1 - s % 2, d))

    def places(l, s, place):
        every = pl.ds(0, 512)
        if s < 4:
            out = []
            for q in (0, 1):
                if s < 2:
                    to = gd.at[l, pl.ds(pl.multiple_of(s * 512 + place * 128 + q * 64, 64), 64), :]
                else:
                    to = gu.at[l, pl.ds(pl.multiple_of(place * 128 + q * 64, 64), 64), pl.ds((s - 2) * 512, 512)]
                out.append([(pl.ds(q * 64, 64), every, to)])
            return out
        if s == 4:
            return [[(pl.ds(0, 128), pl.ds(j * COLS, COLS), gq.at[l, j, chunk(place, 128), :])] for j in (0, 1)]
        lower = pl.ds(64, 64)
        return [
            [(pl.ds(0, 64), every, go.at[l, chunk(place, 64), :])],
            [
                (lower, pl.ds(0, COLS), gq.at[l, 2, chunk(place, 64), :]),
                (lower, pl.ds(COLS, COLS), gq.at[l, 2, pl.ds(pl.multiple_of(256 + place * 64, 64), 64), :]),
            ],
        ]

    def gr_five(l, s, d):
        first, second = places(l, s, axis_place(s % 2))
        return [
            remote(FB.at[l, s, rows, lanes], to, gr_s.at[l, 5], gr_r.at[l, s, 5], axis_dev(s % 2, d))
            for rows, lanes, to in first + second
        ]

    def gr_six(l, s):
        out = []
        for side, (source, d) in enumerate(((3, 1), (1, 3))):
            place = lax.rem(axis_place(s % 2) + source, 4)
            for _, _, to in places(l, s, place)[side]:
                out.append(remote(to, to, gr_s.at[l, 6], gr_r.at[l, s, 6], axis_dev(s % 2, d)))
        return out

    def gr_local(l, s):
        first, second = places(l, s, axis_place(s % 2))
        return [pltpu.make_async_copy(FB.at[l, s, rows, lanes], to, lsem.at[l]) for rows, lanes, to in first + second]

    def t1(l, s):
        gr_relay(l, s, 0).start()
        gr_relay(l, s, 1).start()
        gr_one(l, s, 0, second_half).start()
        gr_one(l, s, 1, first_half).start()

    def t1b(l, s):
        arrived(RL.at[l, s], gr_r.at[l, s, 0])
        for side, lanes in ((0, first_half), (1, second_half)):
            rows = chunk(lax.rem(axis_place(s % 2) + (1, 3)[side], 4), 128)
            for r in (0, 1):
                total = G[l, s, r, rows, lanes].astype(F32) + RL[l, s, side, r].astype(F32)
                G[l, s, r, rows, lanes] = total.astype(BF)
            gr_one(l, s, side, lanes).start()

    def t2(l, s):
        arrived(R1.at[l, s], gr_r.at[l, s, 1])
        own = chunk(axis_place(s % 2), 128)
        for r in (0, 1):
            total = G[l, s, r, own, :].astype(F32)
            for side in (0, 1):
                total = total + R1[l, s, side, r].astype(F32)
            A1[l, s, r] = total.astype(BF)
        for d in (1, 2, 3):
            gr_two(l, s, d).start()

    def t3(l, s):
        arrived(R2.at[l, s], gr_r.at[l, s, 2])
        own = chunk(axis_place(1 - s % 2), 32)
        for r in (0, 1):
            total = A1[l, s, r, own, :].astype(F32)
            for d in (0, 1, 2):
                total = total + R2[l, s, d, r].astype(F32)
            A2[l, s, r] = total.astype(BF)
        gr_row(l, s).start()

    def t4(l, s):
        arrived(R3.at[l, s], gr_r.at[l, s, 3])
        place = axis_place(1 - s % 2)
        FB[l, s, chunk(place, 32), :] = (A2[l, s, row].astype(F32) + R3[l, s].astype(F32)).astype(BF)
        for d in (1, 2, 3):
            gr_four(l, s, d, place).start()

    def t5(l, s):
        arrived(FB.at[l, s, pl.ds(0, 96), :], gr_r.at[l, s, 4])
        for d in (1, 3):
            for c in gr_five(l, s, d):
                c.start()
        for c in gr_local(l, s):
            c.start()

    def t5b(l, s):
        arrived(R1.at[l, s, 0], gr_r.at[l, s, 5])
        for c in gr_six(l, s):
            c.start()

    def t6(l, s):
        arrived(FB.at[l, s], gr_r.at[l, s, 6])

    def gr_drain(l):
        arrived(FB.at[l], lsem.at[l])
        arrived(RL.at[l], gr_s.at[l, 0])
        arrived(R1.at[l], gr_s.at[l, 1])
        arrived(R2.at[l], gr_s.at[l, 2])
        arrived(R3.at[l], gr_s.at[l, 3])
        arrived(FB.at[l, :, pl.ds(0, 96), :], gr_s.at[l, 4])
        arrived(R1.at[l, :, 0], gr_s.at[l, 5])
        arrived(FB.at[l], gr_s.at[l, 6])

    def both(step, l, first):
        step(l, first)
        step(l, first + 1)

    def vec(l, r):
        return PF[pl.ds(l * 8 + r, 1), :]

    def norm_into(values, l, n, gain, shift):
        mean_row = jnp.sum(values, axis=1, keepdims=True) / D
        squares = jnp.sum(values * values, axis=1, keepdims=True) / D
        inverse = lax.rsqrt(squares - mean_row * mean_row + EPSILON)
        normed = (values - mean_row) * inverse
        NRM[l, n] = normed
        INV[l, n] = jnp.broadcast_to(inverse, (OWN, 128))
        return normed * gain + shift

    def forward(l, carry):
        X = STATE.at[l]
        X[chunk(col), :] = S[...].astype(BF)
        ag_start(X)

        @pl.when(l == 0)
        def _():
            for p in parts[2:]:
                w_step_two(0, p)
            for p in parts:
                w_piece(1, p, row).start()
            w_direct(1, row).start()

        w_wait(l, 0)
        ag_finish(X)
        for j in range(3):
            mixed = dot(STATE[l, :, :512], WQ[l, 0, j]) + dot(STATE[l, :, 512:], WQ[l, 1, j])
            if j != 1:
                mixed = mixed + qvb[l, j // 2 : j // 2 + 1, :]
            QKV[l, j] = mixed.astype(BF)
        ag_drain(X)

        @pl.when(l == 0)
        def _():
            for p in parts:
                w_step_one(1, p)

        for h in range(HEADS_LOCAL):
            lanes = slice(h * HD, (h + 1) * HD)
            scores = dot_nt(QKV[l, 0, :, lanes], QKV[l, 1, :, lanes])
            scaled = jnp.where(mask[...] > 0.5, scores * SCALE, MASKED)
            raised = jnp.exp(scaled - jnp.max(scaled, axis=1, keepdims=True))
            probs = raised / jnp.sum(raised, axis=1, keepdims=True)
            PR[l, h] = probs
            CTX[l, :, lanes] = dot(probs.astype(BF), QKV[l, 2, :, lanes]).astype(BF)

        @pl.when(l == 0)
        def _():
            for p in parts:
                w_step_two(1, p)

        w_wait(l, 1)
        for h in (0, 1):
            PS[:, half(h)] = dot(CTX[l], WO[l, h]).astype(BF)
            rs_send(0, h)
        rs_mid(0, 0)
        rs_mid(0, 1)
        for h in (0, 1):
            F1[:, half(h)] = S[:, half(h)] + rs_end(0, h)
        rs_drain()
        middle = norm_into(F1[...] + vec(l, 0), l, 0, vec(l, 1), vec(l, 2))
        M[...] = middle
        X = MID.at[l]
        X[chunk(col), :] = middle.astype(BF)
        ag_start(X)
        w_wait(l, 2)
        ag_finish(X)

        def lift(n, c):
            lanes = chunk(n, COLS)
            lifted = dot(MID[l, :, :512], WU[l, 0, :, lanes]) + dot(MID[l, :, 512:], WU[l, 1, :, lanes])
            lifted = lifted + upb[pl.ds(l, 1), lanes]
            phi = 0.5 * (1.0 + lax.erf(lifted * (0.5**0.5)))
            density = jnp.exp(-0.5 * lifted * lifted) * 0.3989422804014327
            DG[l, :, lanes] = phi + lifted * density
            ACT[l, :, lanes] = (lifted * phi).astype(BF)
            return c

        lax.fori_loop(0, 4, lift, 0)
        ag_drain(X)
        w_wait(l, 3)
        for h in (0, 1):
            for q in (0, 1):
                lanes = pl.ds(h * 512 + q * 256, 256)
                PS[:, lanes] = dot(ACT[l], WD[l, h, :, pl.ds(q * 256, 256)]).astype(BF)
            rs_send(1, h)
        rs_mid(1, 0)
        rs_mid(1, 1)
        for h in (0, 1):
            F1[:, half(h)] = M[:, half(h)] + rs_end(1, h)
        rs_drain()
        S[...] = norm_into(F1[...] + vec(l, 5), l, 1, vec(l, 3), vec(l, 4))
        return carry

    lax.fori_loop(0, LAYERS, forward, 0)

    def out_copies(n, d):
        buf = (HOB, GIB)[n]
        to = lax.rem(col + d, 4)
        return remote(
            HS.at[n, :, chunk(to, COLS)], buf.at[chunk(col)], out_s.at[n], out_r.at[n], (dp, row, to)
        )

    HS[0] = S[...].astype(BF)
    for d in (1, 2, 3):
        out_copies(0, d).start()
    HOB[chunk(col), :] = HS[0, :, chunk(col, COLS)]

    def backward(i, carry):
        l = LAYERS - 1 - i
        prev = l + 1
        upstream = U[...]
        normed = NRM[l, 1]
        SGF[l, 3:4, :] = jnp.sum(upstream * normed, axis=0, keepdims=True)
        SGF[l, 4:5, :] = jnp.sum(upstream, axis=0, keepdims=True)
        grad_second = norm_back(upstream, normed, INV[l, 1, :, :1], vec(l, 3))
        GS[...] = grad_second
        SGF[l, 5:6, :] = jnp.sum(grad_second, axis=0, keepdims=True)
        SEC[chunk(col), :] = grad_second.astype(BF)
        ag_start(SEC)

        @pl.when(i > 0)
        def _():
            both(t2, prev, 2)
            both(t3, prev, 0)
            both(t1b, prev, 4)

        ag_finish(SEC)

        def pull(n, c):
            lanes = chunk(n, COLS)
            grad_act = dot_nt(SEC[:, :512], WD[l, 0, lanes, :]) + dot_nt(SEC[:, 512:], WD[l, 1, lanes, :])
            grad_lifted = grad_act * DG[l, :, lanes]
            SU[l, :, lanes] = jnp.sum(grad_lifted, axis=0, keepdims=True)
            LL[:, lanes] = grad_lifted.astype(BF)
            return c

        lax.fori_loop(0, 4, pull, 0)
        for h in (0, 1):
            for q in (0, 1):
                lanes = pl.ds(h * 512 + q * 256, 256)
                PS[:, lanes] = dot_nt(LL[...], WU[l, h, pl.ds(q * 256, 256), :]).astype(BF)
            rs_send(0, h)
        rs_mid(0, 0)
        rs_mid(0, 1)

        def down_grad(f, c):
            total = dot_tn(ACT[l, :, chunk(f, COLS)], SEC[...]).astype(BF)
            rows = chunk(lax.rem(f, 2), COLS)
            for r in (0, 1):
                G[l, lax.div(f, 2), r, rows, :] = total[:, r * 512 : (r + 1) * 512]
            return c

        lax.fori_loop(0, 4, down_grad, 0)
        both(t1, l, 0)
        ag_drain(SEC)

        @pl.when(i > 0)
        def _():
            both(t4, prev, 0)
            both(t3, prev, 2)
            both(t2, prev, 4)

        for h in (0, 1):
            GS[:, half(h)] = GS[:, half(h)] + rs_end(0, h)
        rs_drain()
        grad_middle = GS[...]
        normed = NRM[l, 0]
        SGF[l, 1:2, :] = jnp.sum(grad_middle * normed, axis=0, keepdims=True)
        SGF[l, 2:3, :] = jnp.sum(grad_middle, axis=0, keepdims=True)
        grad_first = norm_back(grad_middle, normed, INV[l, 0, :, :1], vec(l, 1))
        GF[...] = grad_first
        SGF[l, 0:1, :] = jnp.sum(grad_first, axis=0, keepdims=True)
        FIR[chunk(col), :] = grad_first.astype(BF)
        ag_start(FIR)

        def up_grad(n, c):
            total = dot_tn(MID[l, :, chunk(n, COLS)], LL[...]).astype(BF)
            rows = chunk(lax.rem(n, 2), COLS)
            for r in (0, 1):
                G[l, 2 + r, lax.div(n, 2), rows, :] = total[:, r * 512 : (r + 1) * 512]
            return c

        lax.fori_loop(0, 4, up_grad, 0)
        both(t1, l, 2)

        @pl.when(i > 0)
        def _():
            both(t5, prev, 0)
            both(t4, prev, 2)
            both(t3, prev, 4)

        both(t1b, l, 0)

        ag_finish(FIR)
        GC[...] = (dot_nt(FIR[:, :512], WO[l, 0]) + dot_nt(FIR[:, 512:], WO[l, 1])).astype(BF)
        for h in range(HEADS_LOCAL):
            lanes = slice(h * HD, (h + 1) * HD)
            probs = PR[l, h]
            grad_probs = dot_nt(GC[:, lanes], QKV[l, 2, :, lanes])
            centre = jnp.sum(probs * grad_probs, axis=1, keepdims=True)
            grad_scores = (probs * (grad_probs - centre) * SCALE).astype(BF)
            grad_query = dot(grad_scores, QKV[l, 1, :, lanes])
            grad_key = dot_tn(grad_scores, QKV[l, 0, :, lanes])
            grad_value = dot_tn(probs.astype(BF), GC[:, lanes])
            SQ[l, 0:1, lanes] = jnp.sum(grad_query, axis=0, keepdims=True)
            SQ[l, 1:2, lanes] = jnp.sum(grad_value, axis=0, keepdims=True)
            ML[:, h * HD : (h + 1) * HD] = grad_query.astype(BF)
            ML[:, COLS + h * HD : COLS + (h + 1) * HD] = grad_key.astype(BF)
            ML[:, 2 * COLS + h * HD : 2 * COLS + (h + 1) * HD] = grad_value.astype(BF)
        for h in (0, 1):
            for q in (0, 1):
                lanes = pl.ds(h * 512 + q * 256, 256)
                PS[:, lanes] = sum(
                    dot_nt(ML[:, j * COLS : (j + 1) * COLS], WQ[l, h, j, pl.ds(q * 256, 256), :]) for j in range(3)
                ).astype(BF)
            rs_send(1, h)
        rs_mid(1, 0)
        rs_mid(1, 1)
        total = dot_tn(CTX[l], FIR[...]).astype(BF)
        for r in (0, 1):
            for q in range(4):
                G[l, 5, r, q * 128 : q * 128 + 64, :] = total[q * 64 : (q + 1) * 64, r * 512 : (r + 1) * 512]

        def qkv_grad(r, c):
            for q in (0, 1):
                total = dot_tn(STATE[l, :, chunk(2 * r + q, COLS)], ML[...]).astype(BF)
                G[l, 4, r, q * 256 : (q + 1) * 256, :] = total[:, :512]
                for b in range(4):
                    G[l, 5, r, b * 128 + 64 : b * 128 + 128, q * 256 : (q + 1) * 256] = total[b * 64 : (b + 1) * 64, 512:]
            return c

        lax.fori_loop(0, 2, qkv_grad, 0)
        both(t1, l, 4)
        ag_drain(FIR)
        both(t1b, l, 2)
        both(t2, l, 0)

        @pl.when(i > 0)
        def _():
            both(t5, prev, 2)
            both(t4, prev, 4)
            both(t5b, prev, 0)

        for h in (0, 1):
            U[:, half(h)] = GF[:, half(h)] + rs_end(1, h)
        rs_drain()
        return carry

    lax.fori_loop(0, LAYERS, backward, 0)

    HS[1] = U[...].astype(BF)
    for d in (1, 2, 3):
        out_copies(1, d).start()
    GIB[chunk(col), :] = HS[1, :, chunk(col, COLS)]

    def sc_copy(d):
        to = lax.rem(col + d, 4)
        return remote(SGF.at[:, :, chunk(to, COLS)], RC.at[d - 1], sm_s.at[0], sm_r.at[0], (dp, row, to))

    def sd_copy(axis, d, place):
        buf = (SZ, SY)[axis]
        return remote(
            buf.at[axis_place(axis)], buf.at[place], sm_s.at[1 + axis], sm_r.at[1 + axis], axis_dev(axis, d)
        )

    def sr_copy():
        return remote(SM, SR, sm_s.at[3], sm_r.at[3], row_dev)

    for d in (1, 2, 3):
        sc_copy(d).start()
    both(t2, 0, 2)
    both(t5b, 1, 2)
    both(t5, 1, 4)
    both(t3, 0, 0)
    both(t1b, 0, 4)
    arrived(RC, sm_r.at[0])
    feature = SGF[:, :, chunk(col, COLS)]
    for d in (0, 1, 2):
        feature = feature + RC[d]
    for l in range(LAYERS):
        SZ[z, 8 * l : 8 * l + 8, :] = feature[l]
        for q in range(4):
            SZ[z, 16 + 4 * l + q : 17 + 4 * l + q, :] = SU[l, :, q * COLS : (q + 1) * COLS]
        SZ[z, 24 + 2 * l : 26 + 2 * l, :] = SQ[l]
    SZ[z, 28:32, :] = jnp.zeros((4, COLS), F32)
    for d in (1, 2, 3):
        sd_copy(0, d, z).start()
    both(t4, 0, 0)
    both(t3, 0, 2)
    both(t2, 0, 4)
    both(t5b, 1, 4)
    arrived(SZ.at[pl.ds(0, 3)], sm_r.at[1])
    SY[y] = SZ[0] + SZ[1] + SZ[2] + SZ[3]
    for d in (1, 2, 3):
        sd_copy(1, d, y).start()
    both(t5, 0, 0)
    both(t4, 0, 2)
    both(t3, 0, 4)
    arrived(SY.at[pl.ds(0, 3)], sm_r.at[2])
    SM[...] = SY[0] + SY[1] + SY[2] + SY[3]
    sr_copy().start()
    both(t5b, 0, 0)
    both(t5, 0, 2)
    both(t4, 0, 4)
    sr_copy().wait_recv()
    gsmall[...] = SM[...] + SR[...]
    both(t5b, 0, 2)
    both(t5, 0, 4)
    for n in (0, 1):
        buf = (HOB, GIB)[n]
        arrived(buf.at[pl.ds(0, 3 * OWN)], out_r.at[n])
    hout[...] = HOB[...]
    gin[...] = GIB[...]
    both(t5b, 0, 4)

    arrived(A2H.at[:, pl.ds(0, 3 * COLS)], in_s.at[0])
    arrived(PF.at[:, pl.ds(0, 3 * COLS)], in_s.at[1])
    arrived(A2G.at[:, pl.ds(0, 3 * COLS)], in_s.at[2])
    for n in (0, 1):
        arrived(HOB.at[pl.ds(0, 3 * OWN)], out_s.at[n])
    arrived(RC, sm_s.at[0])
    arrived(SZ.at[pl.ds(0, 3)], sm_s.at[1])
    arrived(SY.at[pl.ds(0, 3)], sm_s.at[2])
    sr_copy().wait_send()

    def finish(l, c):
        w_drain(l)
        for s in range(SLABS):
            t6(l, s)
        gr_drain(l)
        return c

    lax.fori_loop(0, LAYERS, finish, 0)


def step_call(*args):
    vmem = pl.BlockSpec(memory_space=pltpu.VMEM)
    hbm = pl.BlockSpec(memory_space=pl.ANY)
    dma = pltpu.SemaphoreType.DMA
    V = pltpu.VMEM
    L = LAYERS
    scratch = [
        V((TOK, TOK), F32), V((16, COLS), F32),
        V((L, 2, 3, 512, COLS), BF), V((L, 2, 256, 512), BF), V((L, 2, 512, 1024), BF), V((L, 2, 1024, 512), BF),
        V((16, 1024), F32), V((OWN, D), BF), V((OWN, D), BF),
        V((OWN, D), F32), V((OWN, D), F32), V((OWN, D), F32), V((OWN, D), F32), V((OWN, D), F32), V((OWN, D), F32),
        V((L, TOK, D), BF), V((L, TOK, D), BF), V((TOK, D), BF), V((TOK, D), BF),
        V((L, 3, TOK, COLS), BF), V((L, TOK, COLS), BF), V((L, HEADS_LOCAL, TOK, TOK), F32),
        V((L, TOK, 1024), F32), V((L, TOK, 1024), BF), V((L, 2, OWN, D), F32), V((L, 2, OWN, 128), F32),
        V((TOK, 1024), BF), V((TOK, 768), BF), V((TOK, COLS), BF),
        V((TOK, D), BF), V((OWN, D), BF), V((2, 2, OWN, D), BF), V((2, OWN, D), BF),
        V((2, OWN, D), BF), V((TOK, COLS), BF), V((TOK, COLS), BF),
        V((L, SLABS, 2, 512, 512), BF), V((L, SLABS, 2, 2, 128, 256), BF),
        V((L, SLABS, 2, 2, 128, 512), BF), V((L, SLABS, 2, 128, 512), BF),
        V((L, SLABS, 3, 2, 32, 512), BF), V((L, SLABS, 2, 32, 512), BF), V((L, SLABS, 32, 512), BF),
        V((L, SLABS, 128, 512), BF),
        V((L, 8, D), F32), V((L, 1, 1024), F32), V((L, 2, COLS), F32), V((3, L, 8, COLS), F32),
        V((32, COLS), F32), V((4, 32, COLS), F32), V((4, 32, COLS), F32), V((32, COLS), F32),
        dma((L, 3)), dma((L, 7, 2)), dma((L, 4)), dma((L,)), dma((L,)), dma((L, 4)), dma((3,)), dma((3,)),
        dma((1,)), dma((4,)), dma((1,)), dma((6,)),
        dma((L, 7)), dma((L, SLABS, 7)), dma((2,)), dma((2,)), dma((L,)), dma((4,)), dma((4,)),
    ]
    return pl.pallas_call(
        kernel,
        out_shape=[
            jax.ShapeDtypeStruct((TOK, COLS), BF),
            jax.ShapeDtypeStruct((TOK, COLS), BF),
            jax.ShapeDtypeStruct((L, 3, 512, COLS), BF),
            jax.ShapeDtypeStruct((L, 256, 512), BF),
            jax.ShapeDtypeStruct((L, 512, 1024), BF),
            jax.ShapeDtypeStruct((L, 1024, 512), BF),
            jax.ShapeDtypeStruct((32, COLS), F32),
        ],
        in_specs=[vmem] * 10 + [hbm] * 4,
        out_specs=[vmem, vmem, hbm, hbm, hbm, hbm, vmem],
        scratch_shapes=scratch,
        compiler_params=pltpu.CompilerParams(
            collective_id=0, has_side_effects=True, vmem_limit_bytes=63 * 2**20
        ),
        name="encoder_step",
    )(*args)


def split_small(hout, gin, sums, out_h, out_g, qvb, outb, gain, shift, upb, downb):
    out_h[...] = hout[...]
    out_g[...] = gin[...]
    for l in range(LAYERS):
        outb[l : l + 1, :] = sums[8 * l : 8 * l + 1, :]
        for n in (0, 1):
            gain[l, n : n + 1, :] = sums[8 * l + 1 + 2 * n : 8 * l + 2 + 2 * n, :]
            shift[l, n : n + 1, :] = sums[8 * l + 2 + 2 * n : 8 * l + 3 + 2 * n, :]
        downb[l : l + 1, :] = sums[8 * l + 5 : 8 * l + 6, :]
        for q in range(4):
            upb[l : l + 1, q * COLS : (q + 1) * COLS] = sums[16 + 4 * l + q : 17 + 4 * l + q, :]
        qvb[l] = sums[24 + 2 * l : 26 + 2 * l, :]


def split_call(hout, gin, sums):
    vmem = pl.BlockSpec(memory_space=pltpu.VMEM)
    shapes = ((LAYERS, 2, COLS), (LAYERS, COLS), (LAYERS, 2, COLS), (LAYERS, 2, COLS), (LAYERS, 1024), (LAYERS, COLS))
    return pl.pallas_call(
        split_small,
        out_shape=[jax.ShapeDtypeStruct((TOK, COLS), BF)] * 2 + [jax.ShapeDtypeStruct(d, F32) for d in shapes],
        in_specs=[vmem] * 3,
        out_specs=[vmem] * 8,
        name="split_small",
    )(hout, gin, sums)


def shards(
    hidden_in, seg_ids, key_mask, w_qkv, qv_bias, w_out, out_bias, ln_gain, ln_shift,
    w_up, up_bias, w_down, down_bias, grad_out,
):
    hout, gin, grad_qkv, grad_out_w, grad_up, grad_down, sums = step_call(
        hidden_in, grad_out, seg_ids.reshape(1, TOK), key_mask.reshape(1, TOK), out_bias, ln_gain, ln_shift, down_bias,
        up_bias, qv_bias, w_qkv.transpose(0, 2, 1, 3), w_out, w_up, w_down,
    )
    hout, gin, qvb, outb, gain, shift, upb, downb = split_call(hout, gin, sums)
    return (
        hout,
        gin,
        grad_qkv.astype(F32).transpose(0, 2, 1, 3),
        qvb,
        grad_out_w.astype(F32),
        outb,
        gain,
        shift,
        grad_up.astype(F32),
        upb,
        grad_down.astype(F32),
        downb,
    )


def solution(mesh):
    tokens = P(("dp", "row"), "col")
    return jax.shard_map(
        shards,
        mesh=mesh,
        in_specs=(
            tokens, P(("dp", "row")), P(("dp", "row")), P(None, "row", None, "col"), P(None, None, "col"),
            P(None, "col", "row"), P(None, "col"), P(None, None, "col"), P(None, None, "col"),
            P(None, "row", "col"), P(None, "col"), P(None, "col", "row"), P(None, "col"), tokens,
        ),
        out_specs=(
            tokens, tokens, P(None, "row", None, "col"), P(None, None, "col"), P(None, "col", "row"),
            P(None, "col"), P(None, None, "col"), P(None, None, "col"), P(None, "row", "col"),
            P(None, "col"), P(None, "col", "row"), P(None, "col"),
        ),
        check_vma=False,
    )
```

```python
import functools

import jax
import jax.numpy as jnp
from jax import lax
from jax.experimental import pallas as pl
from jax.experimental.pallas import tpu as pltpu
from jax.sharding import PartitionSpec as P

D = 1024
HD = 64
LAYERS = 2
TOK = 256
OWN = 64
COLS = 256
HEADS_LOCAL = 4
SLABS = 6
EPSILON = 1e-05
MASKED = -1e30
SCALE = HD**-0.5
PARTS = (
    (0, 0, 1, 0), (0, 1, 2, 1), (0, 2, 3, 0), (1, 0, 512, 1), (2, 0, 512, 0), (2, 512, 1024, 1), (3, 0, 256, 0), (3, 256, 512, 1),
)
WEIGHT_ROWS = (512, 256, 512, 1024)
MESH = pl.DeviceIdType.MESH
BF = jnp.bfloat16
F32 = jnp.float32


def dot(a, b):
    return jnp.dot(a, b, preferred_element_type=F32)


def dot_nt(a, b):
    return lax.dot_general(a, b, (((1,), (1,)), ((), ())), preferred_element_type=F32)


def dot_tn(a, b):
    return lax.dot_general(a, b, (((0,), (0,)), ((), ())), preferred_element_type=F32)


def norm_back(upstream, normed, inverse, gain):
    scaled = upstream * gain
    mean_one = jnp.sum(scaled, axis=1, keepdims=True) / D
    mean_two = jnp.sum(scaled * normed, axis=1, keepdims=True) / D
    return inverse * (scaled - mean_one - normed * mean_two)


def kernel(
    hid, gout, seg, key, outb, gain, shift, downb, upb, qvb, wq, wo, wu, wd,
    hout, gin, gq, go, gu, gd, gsmall,
    mask, small, WQ, WO, WU, WD, PF, A2G, S, M, U, GS, GF, F1,
    STATE, MID, SEC, FIR, QKV, CTX, PR, DG, ACT, NRM, INV, LL, ML, GC,
    PS, XS, L1, L2, HS, HOB, GIB,
    G, RL, R1, A1, R2, A2, R3, FB,
    SGF, SU, SQ, RC, SM, SZ, SY, SR,
    w_s, w_r, w_rb, w_lsem, in_s, in_r, ag_s, ag_r, rs_s, rs_r, gr_s, gr_r, out_s, out_r, lsem, sm_s, sm_r,
):
    dp = lax.axis_index("dp")
    row = lax.axis_index("row")
    col = lax.axis_index("col")
    z, y = lax.div(dp, 4), lax.rem(dp, 4)
    xh, core = lax.div(col, 2), lax.rem(col, 2)
    col_core = xh * 2 + (1 - core)
    col_cross = (1 - xh) * 2 + core
    col_diag = (1 - xh) * 2 + (1 - core)
    core_dev = (dp, row, col_core)
    cross_dev = (dp, row, col_cross)
    row_dev = (dp, 1 - row, col)

    def col_dev(d):
        return (dp, row, lax.rem(col + d, 4))

    def axis_place(axis):
        return z if axis == 0 else y

    def axis_dev(axis, d):
        if axis == 0:
            return (lax.rem(z + d, 4) * 4 + y, row, col)
        return (z * 4 + lax.rem(y + d, 4), row, col)

    def chunk(j, rows=OWN):
        return pl.ds(pl.multiple_of(j * rows, rows), rows)

    def remote(src, dst, ssem, rsem, dev):
        return pltpu.make_async_remote_copy(
            src_ref=src, dst_ref=dst, send_sem=ssem, recv_sem=rsem, device_id=dev, device_id_type=MESH
        )

    def arrived(ref, sem):
        pltpu.make_async_copy(ref, ref, sem).wait()

    barrier = pltpu.get_barrier_semaphore()
    for dev in [col_dev(1), col_dev(2), col_dev(3), row_dev] + [axis_dev(a, d) for a in (0, 1) for d in (1, 2, 3)]:
        pl.semaphore_signal(barrier, 1, device_id=dev, device_id_type=MESH)
    pl.semaphore_wait(barrier, 10)

    def in_copies(d):
        to = lax.rem(col + d, 4)
        dev = (dp, row, to)
        return [
            remote(small, PF.at[:, chunk(col, COLS)], in_s.at[0], in_r.at[0], dev),
            remote(gout.at[chunk(to)], A2G.at[:, chunk(col, COLS)], in_s.at[1], in_r.at[1], dev),
        ]

    def hid_block(owner, p):
        return STATE.at[0, pl.ds(p * 128, 128), chunk(owner, COLS)]

    for p in (0, 1):
        remote(hid.at[pl.ds(p * 128, 128)], hid_block(col, p), ag_s.at[0], ag_r.at[p], cross_dev).start()
    remote(hid, STATE.at[0, :, chunk(col, COLS)], ag_s.at[0], ag_r.at[2], core_dev).start()

    for l in range(LAYERS):
        rows = (outb[l : l + 1], gain[l, 0:1], shift[l, 0:1], gain[l, 1:2], shift[l, 1:2], downb[l : l + 1])
        for r in range(6):
            small[l * 8 + r : l * 8 + r + 1, :] = rows[r]
        small[l * 8 + 6 : l * 8 + 8, :] = jnp.zeros((2, COLS), F32)
    for d in (1, 2, 3):
        in_copies(d)[0].start()

    pairs = ((wq, WQ), (wo, WO), (wu, WU), (wd, WD))

    def region(ref, n, lo, hi, rows):
        if n == 0:
            return ref.at[lo, rows, :]
        return ref.at[rows, pl.ds(lo, hi - lo)]

    def w_local(l, n):
        return pltpu.make_async_copy(pairs[n][0].at[l], pairs[n][1].at[l, row], w_lsem.at[l, n])

    def part_axes(p):
        first = PARTS[p][3]
        return first, 1 - first

    def part_rows(p, a_place, b_place):
        piece = WEIGHT_ROWS[PARTS[p][0]] // 16
        return pl.ds(pl.multiple_of((b_place * 4 + a_place) * piece, piece), piece)

    def w_piece(l, p, which):
        n, lo, hi, _ = PARTS[p]
        first, second = part_axes(p)
        rows = part_rows(p, axis_place(first), axis_place(second))
        return remote(
            region(pairs[n][0].at[l], n, lo, hi, rows), region(pairs[n][1].at[l, which], n, lo, hi, rows),
            w_s.at[l, 0], w_r.at[l, p, 0], row_dev,
        )

    def w_one(l, p, d, place):
        n, lo, hi, _ = PARTS[p]
        first, second = part_axes(p)
        rows = part_rows(p, place, axis_place(second))
        ref = region(pairs[n][1].at[l, 1 - row], n, lo, hi, rows)
        return remote(ref, ref, w_s.at[l, 1], w_r.at[l, p, 1], axis_dev(first, d))

    def w_two(l, p, d, place):
        n, lo, hi, _ = PARTS[p]
        _, second = part_axes(p)
        block = WEIGHT_ROWS[n] // 4
        ref = region(pairs[n][1].at[l, 1 - row], n, lo, hi, chunk(place, block))
        return remote(ref, ref, w_s.at[l, 2], w_rb.at[l, n], axis_dev(second, d))

    def w_step_one(l, p):
        w_piece(l, p, 1 - row).wait_recv()
        for d in (1, 2, 3):
            w_one(l, p, d, axis_place(part_axes(p)[0])).start()

    def three_pieces(l, p):
        n, lo, hi, _ = PARTS[p]
        piece = WEIGHT_ROWS[n] // 16
        return region(pairs[n][1].at[l, 1 - row], n, lo, hi, pl.ds(0, 3 * piece))

    def w_step_two(l, p):
        second = part_axes(p)[1]
        arrived(three_pieces(l, p), w_r.at[l, p, 1])
        for d in (1, 2, 3):
            w_two(l, p, d, axis_place(second)).start()

    def w_wait(l, n):
        w_local(l, n).wait()
        rows = WEIGHT_ROWS[n] * 3 // 4
        if n == 0:
            arrived(WQ.at[l, 1 - row, :, pl.ds(0, rows), :], w_rb.at[l, n])
        else:
            arrived(pairs[n][1].at[l, 1 - row, pl.ds(0, rows), :], w_rb.at[l, n])

    def w_drain(l):
        arrived(WU.at[0, 0, pl.ds(0, 192), pl.ds(0, 512)], w_s.at[l, 0])
        arrived(WQ.at[0, :, :, pl.ds(0, 192), :], w_s.at[l, 1])
        arrived(WQ.at[:, :, :, pl.ds(0, 384), :], w_s.at[l, 2])

    parts = range(len(PARTS))
    for p in parts:
        w_piece(0, p, row).start()
    for n in range(4):
        w_local(0, n).start()
    for p in parts:
        w_step_one(0, p)
    for d in (1, 2, 3):
        in_copies(d)[1].start()
    for n in range(4):
        w_local(1, n).start()

    seg_lanes = jnp.broadcast_to(seg[...].astype(F32), (TOK, TOK))
    key_lanes = jnp.broadcast_to(key[...].astype(F32), (TOK, TOK))
    same_place = lax.broadcasted_iota(jnp.int32, (TOK, TOK), 0) == lax.broadcasted_iota(jnp.int32, (TOK, TOK), 1)
    keep = jnp.where(same_place, 1.0, key_lanes)
    mask[...] = jnp.where(seg_lanes.T == seg_lanes, keep, 0.0)

    A2G[:, chunk(col, COLS)] = gout[chunk(col), :]
    PF[:, chunk(col, COLS)] = small[...]
    STATE[0, :, chunk(col, COLS)] = hid[...]
    for p in parts[:3]:
        w_step_two(0, p)
    for p in (0, 1):
        arrived(hid_block(col_cross, p), ag_r.at[p])
        remote(hid_block(col_cross, p), hid_block(col_cross, p), ag_s.at[0], ag_r.at[3], core_dev).start()
    for p in parts[3:]:
        w_step_two(0, p)
    arrived(STATE.at[0, :, chunk(col_core, COLS)], ag_r.at[2])
    arrived(STATE.at[0, :, chunk(col_diag, COLS)], ag_r.at[3])
    S[...] = STATE[0, chunk(col), :].astype(F32)
    arrived(PF.at[:, pl.ds(0, 3 * COLS)], in_r.at[0])
    arrived(A2G.at[:, pl.ds(0, 3 * COLS)], in_r.at[1])
    U[...] = A2G[...].astype(F32)

    def ag_rows(owner, p):
        return pl.ds(pl.multiple_of(owner * OWN + p * 32, 32), 32)

    def ag_send(X):
        out = []
        for p in (0, 1):
            rows = ag_rows(col, p)
            out.append(remote(X.at[rows], X.at[rows], ag_s.at[0], ag_r.at[p], cross_dev))
        out.append(remote(X.at[chunk(col)], X.at[chunk(col)], ag_s.at[0], ag_r.at[2], core_dev))
        return out

    def ag_start(X):
        for c in ag_send(X):
            c.start()

    def ag_finish(X):
        for p in (0, 1):
            rows = ag_rows(col_cross, p)
            arrived(X.at[rows], ag_r.at[p])
            remote(X.at[rows], X.at[rows], ag_s.at[0], ag_r.at[3], core_dev).start()
        arrived(X.at[chunk(col_core)], ag_r.at[2])
        arrived(X.at[chunk(col_diag)], ag_r.at[3])

    def ag_drain(X):
        arrived(X.at[pl.ds(0, 3 * OWN)], ag_s.at[0])

    def half(h):
        return pl.ds(h * 512, 512)

    def rs_first(par, h, t):
        to = (1 - xh) * 2 + (1 - core) if t == 0 else col_core
        return remote(
            PS.at[chunk(to), half(h)], L1.at[par, t, :, half(h)], rs_s.at[0], rs_r.at[h * 3 + t], core_dev
        )

    def rs_cross(par, h):
        return remote(XS.at[:, half(h)], L2.at[par, :, half(h)], rs_s.at[0], rs_r.at[h * 3 + 2], cross_dev)

    def rs_send(par, h):
        for t in (0, 1):
            rs_first(par, h, t).start()

    def rs_mid(par, h):
        rs_first(par, h, 0).wait_recv()
        total = PS[chunk(col_cross), half(h)].astype(F32) + L1[par, 0, :, half(h)].astype(F32)
        XS[:, half(h)] = total.astype(BF)
        rs_cross(par, h).start()

    def rs_end(par, h):
        rs_first(par, h, 1).wait_recv()
        total = PS[chunk(col), half(h)].astype(F32) + L1[par, 1, :, half(h)].astype(F32)
        rs_cross(par, h).wait_recv()
        return total + L2[par, :, half(h)].astype(F32)

    def rs_drain():
        arrived(PS.at[pl.ds(0, 3 * OWN)], rs_s.at[0])

    first_half, second_half = pl.ds(0, 256), pl.ds(256, 256)

    def gr_block(l, s, d, lanes):
        return G.at[l, s, :, chunk(lax.rem(axis_place(s % 2) + d, 4), 128), lanes]

    def gr_relay(l, s, side):
        lanes, d = ((first_half, 1), (second_half, 3))[side]
        return remote(gr_block(l, s, 2, lanes), RL.at[l, s, side], gr_s.at[l, 0], gr_r.at[l, s, 0], axis_dev(s % 2, d))

    def gr_one(l, s, side, lanes):
        d = (1, 3)[side]
        return remote(
            gr_block(l, s, d, lanes), R1.at[l, s, side, :, :, lanes], gr_s.at[l, 1], gr_r.at[l, s, 1], axis_dev(s % 2, d)
        )

    def gr_two(l, s, d):
        axis = 1 - s % 2
        to = lax.rem(axis_place(axis) + d, 4)
        return remote(A1.at[l, s, :, chunk(to, 32), :], R2.at[l, s, d - 1], gr_s.at[l, 2], gr_r.at[l, s, 2], axis_dev(axis, d))

    def gr_row(l, s):
        return remote(A2.at[l, s, 1 - row], R3.at[l, s], gr_s.at[l, 3], gr_r.at[l, s, 3], row_dev)

    def gr_four(l, s, d, place):
        rows = FB.at[l, s, chunk(place, 32), :]
        return remote(rows, rows, gr_s.at[l, 4], gr_r.at[l, s, 4], axis_dev(1 - s % 2, d))

    def places(l, s, place):
        every = pl.ds(0, 512)
        if s < 4:
            out = []
            for q in (0, 1):
                if s < 2:
                    to = gd.at[l, pl.ds(pl.multiple_of(s * 512 + place * 128 + q * 64, 64), 64), :]
                else:
                    to = gu.at[l, pl.ds(pl.multiple_of(place * 128 + q * 64, 64), 64), pl.ds((s - 2) * 512, 512)]
                out.append([(pl.ds(q * 64, 64), every, to)])
            return out
        if s == 4:
            return [[(pl.ds(0, 128), pl.ds(j * COLS, COLS), gq.at[l, j, chunk(place, 128), :])] for j in (0, 1)]
        lower = pl.ds(64, 64)
        return [
            [(pl.ds(0, 64), every, go.at[l, chunk(place, 64), :])],
            [
                (lower, pl.ds(0, COLS), gq.at[l, 2, chunk(place, 64), :]),
                (lower, pl.ds(COLS, COLS), gq.at[l, 2, pl.ds(pl.multiple_of(256 + place * 64, 64), 64), :]),
            ],
        ]

    def gr_five(l, s, d):
        first, second = places(l, s, axis_place(s % 2))
        return [
            remote(FB.at[l, s, rows, lanes], to, gr_s.at[l, 5], gr_r.at[l, s, 5], axis_dev(s % 2, d))
            for rows, lanes, to in first + second
        ]

    def gr_six(l, s):
        out = []
        for side, (source, d) in enumerate(((3, 1), (1, 3))):
            place = lax.rem(axis_place(s % 2) + source, 4)
            for _, _, to in places(l, s, place)[side]:
                out.append(remote(to, to, gr_s.at[l, 6], gr_r.at[l, s, 6], axis_dev(s % 2, d)))
        return out

    def gr_local(l, s):
        first, second = places(l, s, axis_place(s % 2))
        return [pltpu.make_async_copy(FB.at[l, s, rows, lanes], to, lsem.at[l]) for rows, lanes, to in first + second]

    def t1(l, s):
        gr_relay(l, s, 0).start()
        gr_relay(l, s, 1).start()
        gr_one(l, s, 0, second_half).start()
        gr_one(l, s, 1, first_half).start()

    def t1b(l, s):
        arrived(RL.at[l, s], gr_r.at[l, s, 0])
        for side, lanes in ((0, first_half), (1, second_half)):
            rows = chunk(lax.rem(axis_place(s % 2) + (1, 3)[side], 4), 128)
            for r in (0, 1):
                total = G[l, s, r, rows, lanes].astype(F32) + RL[l, s, side, r].astype(F32)
                G[l, s, r, rows, lanes] = total.astype(BF)
            gr_one(l, s, side, lanes).start()

    def t2(l, s):
        arrived(R1.at[l, s], gr_r.at[l, s, 1])
        own = chunk(axis_place(s % 2), 128)
        for r in (0, 1):
            total = G[l, s, r, own, :].astype(F32)
            for side in (0, 1):
                total = total + R1[l, s, side, r].astype(F32)
            A1[l, s, r] = total.astype(BF)
        for d in (1, 2, 3):
            gr_two(l, s, d).start()

    def t3(l, s):
        arrived(R2.at[l, s], gr_r.at[l, s, 2])
        own = chunk(axis_place(1 - s % 2), 32)
        for r in (0, 1):
            total = A1[l, s, r, own, :].astype(F32)
            for d in (0, 1, 2):
                total = total + R2[l, s, d, r].astype(F32)
            A2[l, s, r] = total.astype(BF)
        gr_row(l, s).start()

    def t4(l, s):
        arrived(R3.at[l, s], gr_r.at[l, s, 3])
        place = axis_place(1 - s % 2)
        FB[l, s, chunk(place, 32), :] = (A2[l, s, row].astype(F32) + R3[l, s].astype(F32)).astype(BF)
        for d in (1, 2, 3):
            gr_four(l, s, d, place).start()

    def t5(l, s):
        arrived(FB.at[l, s, pl.ds(0, 96), :], gr_r.at[l, s, 4])
        for d in (1, 3):
            for c in gr_five(l, s, d):
                c.start()
        for c in gr_local(l, s):
            c.start()

    def t5b(l, s):
        arrived(R1.at[l, s, 0], gr_r.at[l, s, 5])
        for c in gr_six(l, s):
            c.start()

    def t6(l, s):
        arrived(FB.at[l, s], gr_r.at[l, s, 6])

    def gr_drain(l):
        arrived(FB.at[l], lsem.at[l])
        arrived(RL.at[l], gr_s.at[l, 0])
        arrived(R1.at[l], gr_s.at[l, 1])
        arrived(R2.at[l], gr_s.at[l, 2])
        arrived(R3.at[l], gr_s.at[l, 3])
        arrived(FB.at[l, :, pl.ds(0, 96), :], gr_s.at[l, 4])
        arrived(R1.at[l, :, 0], gr_s.at[l, 5])
        arrived(FB.at[l], gr_s.at[l, 6])

    def both(step, l, first):
        step(l, first)
        step(l, first + 1)

    def vec(l, r):
        return PF[pl.ds(l * 8 + r, 1), :]

    def norm_into(values, l, n, gain, shift):
        mean_row = jnp.sum(values, axis=1, keepdims=True) / D
        squares = jnp.sum(values * values, axis=1, keepdims=True) / D
        inverse = lax.rsqrt(squares - mean_row * mean_row + EPSILON)
        normed = (values - mean_row) * inverse
        NRM[l, n] = normed
        INV[l, n] = jnp.broadcast_to(inverse, (OWN, 128))
        return normed * gain + shift

    def forward(l, carry):
        X = STATE.at[l]

        @pl.when(l > 0)
        def _():
            X[chunk(col), :] = S[...].astype(BF)
            ag_start(X)

        w_wait(l, 0)

        @pl.when(l > 0)
        def _():
            ag_finish(X)

        for j in range(3):
            mixed = dot(STATE[l, :, :512], WQ[l, 0, j]) + dot(STATE[l, :, 512:], WQ[l, 1, j])
            if j != 1:
                mixed = mixed + qvb[l, j // 2 : j // 2 + 1, :]
            QKV[l, j] = mixed.astype(BF)
        ag_drain(X)

        @pl.when(l == 0)
        def _():
            for p in parts:
                w_piece(1, p, row).start()

        for h in range(HEADS_LOCAL):
            lanes = slice(h * HD, (h + 1) * HD)
            scores = dot_nt(QKV[l, 0, :, lanes], QKV[l, 1, :, lanes])
            scaled = jnp.where(mask[...] > 0.5, scores * SCALE, MASKED)
            raised = jnp.exp(scaled - jnp.max(scaled, axis=1, keepdims=True))
            probs = raised / jnp.sum(raised, axis=1, keepdims=True)
            PR[l, h] = probs
            CTX[l, :, lanes] = dot(probs.astype(BF), QKV[l, 2, :, lanes]).astype(BF)
        w_wait(l, 1)
        for h in (0, 1):
            PS[:, half(h)] = dot(CTX[l], WO[l, h]).astype(BF)
            rs_send(0, h)
        rs_mid(0, 0)
        rs_mid(0, 1)
        for h in (0, 1):
            F1[:, half(h)] = S[:, half(h)] + rs_end(0, h)
        rs_drain()
        middle = norm_into(F1[...] + vec(l, 0), l, 0, vec(l, 1), vec(l, 2))
        M[...] = middle
        X = MID.at[l]
        X[chunk(col), :] = middle.astype(BF)
        ag_start(X)

        @pl.when(l == 0)
        def _():
            for p in parts:
                w_step_one(1, p)

        w_wait(l, 2)
        ag_finish(X)

        def lift(n, c):
            lanes = chunk(n, COLS)
            lifted = dot(MID[l, :, :512], WU[l, 0, :, lanes]) + dot(MID[l, :, 512:], WU[l, 1, :, lanes])
            lifted = lifted + upb[pl.ds(l, 1), lanes]
            phi = 0.5 * (1.0 + lax.erf(lifted * (0.5**0.5)))
            density = jnp.exp(-0.5 * lifted * lifted) * 0.3989422804014327
            DG[l, :, lanes] = phi + lifted * density
            ACT[l, :, lanes] = (lifted * phi).astype(BF)
            return c

        lax.fori_loop(0, 4, lift, 0)
        ag_drain(X)

        @pl.when(l == 0)
        def _():
            for p in parts:
                w_step_two(1, p)

        w_wait(l, 3)
        for h in (0, 1):
            for q in (0, 1):
                lanes = pl.ds(h * 512 + q * 256, 256)
                PS[:, lanes] = dot(ACT[l], WD[l, h, :, pl.ds(q * 256, 256)]).astype(BF)
            rs_send(1, h)
        rs_mid(1, 0)
        rs_mid(1, 1)
        for h in (0, 1):
            F1[:, half(h)] = M[:, half(h)] + rs_end(1, h)
        rs_drain()
        S[...] = norm_into(F1[...] + vec(l, 5), l, 1, vec(l, 3), vec(l, 4))
        return carry

    lax.fori_loop(0, LAYERS, forward, 0)

    def out_copies(n, d):
        buf = (HOB, GIB)[n]
        to = lax.rem(col + d, 4)
        return remote(
            HS.at[n, :, chunk(to, COLS)], buf.at[chunk(col)], out_s.at[n], out_r.at[n], (dp, row, to)
        )

    HS[0] = S[...].astype(BF)
    for d in (1, 2, 3):
        out_copies(0, d).start()
    HOB[chunk(col), :] = HS[0, :, chunk(col, COLS)]

    def backward(i, carry):
        l = LAYERS - 1 - i
        prev = l + 1
        upstream = U[...]
        normed = NRM[l, 1]
        SGF[l, 3:4, :] = jnp.sum(upstream * normed, axis=0, keepdims=True)
        SGF[l, 4:5, :] = jnp.sum(upstream, axis=0, keepdims=True)
        grad_second = norm_back(upstream, normed, INV[l, 1, :, :1], vec(l, 3))
        GS[...] = grad_second
        SGF[l, 5:6, :] = jnp.sum(grad_second, axis=0, keepdims=True)
        SEC[chunk(col), :] = grad_second.astype(BF)
        ag_start(SEC)

        @pl.when(i > 0)
        def _():
            both(t2, prev, 2)
            both(t3, prev, 0)
            both(t1b, prev, 4)

        ag_finish(SEC)

        def pull(n, c):
            lanes = chunk(n, COLS)
            grad_act = dot_nt(SEC[:, :512], WD[l, 0, lanes, :]) + dot_nt(SEC[:, 512:], WD[l, 1, lanes, :])
            grad_lifted = grad_act * DG[l, :, lanes]
            SU[l, :, lanes] = jnp.sum(grad_lifted, axis=0, keepdims=True)
            LL[:, lanes] = grad_lifted.astype(BF)
            return c

        lax.fori_loop(0, 4, pull, 0)
        for h in (0, 1):
            for q in (0, 1):
                lanes = pl.ds(h * 512 + q * 256, 256)
                PS[:, lanes] = dot_nt(LL[...], WU[l, h, pl.ds(q * 256, 256), :]).astype(BF)
            rs_send(0, h)
        rs_mid(0, 0)
        rs_mid(0, 1)

        def down_grad(f, c):
            total = dot_tn(ACT[l, :, chunk(f, COLS)], SEC[...]).astype(BF)
            rows = chunk(lax.rem(f, 2), COLS)
            for r in (0, 1):
                G[l, lax.div(f, 2), r, rows, :] = total[:, r * 512 : (r + 1) * 512]
            return c

        lax.fori_loop(0, 4, down_grad, 0)
        both(t1, l, 0)
        ag_drain(SEC)

        @pl.when(i > 0)
        def _():
            both(t4, prev, 0)
            both(t3, prev, 2)
            both(t2, prev, 4)

        for h in (0, 1):
            GS[:, half(h)] = GS[:, half(h)] + rs_end(0, h)
        rs_drain()
        grad_middle = GS[...]
        normed = NRM[l, 0]
        SGF[l, 1:2, :] = jnp.sum(grad_middle * normed, axis=0, keepdims=True)
        SGF[l, 2:3, :] = jnp.sum(grad_middle, axis=0, keepdims=True)
        grad_first = norm_back(grad_middle, normed, INV[l, 0, :, :1], vec(l, 1))
        GF[...] = grad_first
        SGF[l, 0:1, :] = jnp.sum(grad_first, axis=0, keepdims=True)
        FIR[chunk(col), :] = grad_first.astype(BF)
        ag_start(FIR)

        def up_grad(n, c):
            total = dot_tn(MID[l, :, chunk(n, COLS)], LL[...]).astype(BF)
            rows = chunk(lax.rem(n, 2), COLS)
            for r in (0, 1):
                G[l, 2 + r, lax.div(n, 2), rows, :] = total[:, r * 512 : (r + 1) * 512]
            return c

        lax.fori_loop(0, 4, up_grad, 0)
        both(t1, l, 2)

        @pl.when(i > 0)
        def _():
            both(t5, prev, 0)
            both(t4, prev, 2)
            both(t3, prev, 4)

        both(t1b, l, 0)

        ag_finish(FIR)
        GC[...] = (dot_nt(FIR[:, :512], WO[l, 0]) + dot_nt(FIR[:, 512:], WO[l, 1])).astype(BF)
        for h in range(HEADS_LOCAL):
            lanes = slice(h * HD, (h + 1) * HD)
            probs = PR[l, h]
            grad_probs = dot_nt(GC[:, lanes], QKV[l, 2, :, lanes])
            centre = jnp.sum(probs * grad_probs, axis=1, keepdims=True)
            grad_scores = (probs * (grad_probs - centre) * SCALE).astype(BF)
            grad_query = dot(grad_scores, QKV[l, 1, :, lanes])
            grad_key = dot_tn(grad_scores, QKV[l, 0, :, lanes])
            grad_value = dot_tn(probs.astype(BF), GC[:, lanes])
            SQ[l, 0:1, lanes] = jnp.sum(grad_query, axis=0, keepdims=True)
            SQ[l, 1:2, lanes] = jnp.sum(grad_value, axis=0, keepdims=True)
            ML[:, h * HD : (h + 1) * HD] = grad_query.astype(BF)
            ML[:, COLS + h * HD : COLS + (h + 1) * HD] = grad_key.astype(BF)
            ML[:, 2 * COLS + h * HD : 2 * COLS + (h + 1) * HD] = grad_value.astype(BF)
        for h in (0, 1):
            for q in (0, 1):
                lanes = pl.ds(h * 512 + q * 256, 256)
                PS[:, lanes] = sum(
                    dot_nt(ML[:, j * COLS : (j + 1) * COLS], WQ[l, h, j, pl.ds(q * 256, 256), :]) for j in range(3)
                ).astype(BF)
            rs_send(1, h)
        rs_mid(1, 0)
        rs_mid(1, 1)
        total = dot_tn(CTX[l], FIR[...]).astype(BF)
        for r in (0, 1):
            for q in range(4):
                G[l, 5, r, q * 128 : q * 128 + 64, :] = total[q * 64 : (q + 1) * 64, r * 512 : (r + 1) * 512]

        def qkv_grad(r, c):
            for q in (0, 1):
                total = dot_tn(STATE[l, :, chunk(2 * r + q, COLS)], ML[...]).astype(BF)
                G[l, 4, r, q * 256 : (q + 1) * 256, :] = total[:, :512]
                for b in range(4):
                    G[l, 5, r, b * 128 + 64 : b * 128 + 128, q * 256 : (q + 1) * 256] = total[b * 64 : (b + 1) * 64, 512:]
            return c

        lax.fori_loop(0, 2, qkv_grad, 0)
        both(t1, l, 4)
        ag_drain(FIR)
        both(t1b, l, 2)
        both(t2, l, 0)

        @pl.when(i > 0)
        def _():
            both(t5, prev, 2)
            both(t4, prev, 4)
            both(t5b, prev, 0)

        for h in (0, 1):
            U[:, half(h)] = GF[:, half(h)] + rs_end(1, h)
        rs_drain()
        return carry

    lax.fori_loop(0, LAYERS, backward, 0)

    HS[1] = U[...].astype(BF)
    for d in (1, 2, 3):
        out_copies(1, d).start()
    GIB[chunk(col), :] = HS[1, :, chunk(col, COLS)]

    def sc_copy(d):
        to = lax.rem(col + d, 4)
        return remote(SGF.at[:, :, chunk(to, COLS)], RC.at[d - 1], sm_s.at[0], sm_r.at[0], (dp, row, to))

    def sd_copy(axis, d, place):
        buf = (SZ, SY)[axis]
        return remote(
            buf.at[axis_place(axis)], buf.at[place], sm_s.at[1 + axis], sm_r.at[1 + axis], axis_dev(axis, d)
        )

    def sr_copy():
        return remote(SM, SR, sm_s.at[3], sm_r.at[3], row_dev)

    for d in (1, 2, 3):
        sc_copy(d).start()
    both(t2, 0, 2)
    both(t5b, 1, 2)
    both(t5, 1, 4)
    both(t3, 0, 0)
    both(t1b, 0, 4)
    arrived(RC, sm_r.at[0])
    feature = SGF[:, :, chunk(col, COLS)]
    for d in (0, 1, 2):
        feature = feature + RC[d]
    for l in range(LAYERS):
        SZ[z, 8 * l : 8 * l + 8, :] = feature[l]
        for q in range(4):
            SZ[z, 16 + 4 * l + q : 17 + 4 * l + q, :] = SU[l, :, q * COLS : (q + 1) * COLS]
        SZ[z, 24 + 2 * l : 26 + 2 * l, :] = SQ[l]
    SZ[z, 28:32, :] = jnp.zeros((4, COLS), F32)
    for d in (1, 2, 3):
        sd_copy(0, d, z).start()
    both(t4, 0, 0)
    both(t3, 0, 2)
    both(t2, 0, 4)
    both(t5b, 1, 4)
    arrived(SZ.at[pl.ds(0, 3)], sm_r.at[1])
    SY[y] = SZ[0] + SZ[1] + SZ[2] + SZ[3]
    for d in (1, 2, 3):
        sd_copy(1, d, y).start()
    both(t5, 0, 0)
    both(t4, 0, 2)
    both(t3, 0, 4)
    arrived(SY.at[pl.ds(0, 3)], sm_r.at[2])
    SM[...] = SY[0] + SY[1] + SY[2] + SY[3]
    sr_copy().start()
    both(t5b, 0, 0)
    both(t5, 0, 2)
    both(t4, 0, 4)
    sr_copy().wait_recv()
    gsmall[...] = SM[...] + SR[...]
    both(t5b, 0, 2)
    both(t5, 0, 4)
    for n in (0, 1):
        buf = (HOB, GIB)[n]
        arrived(buf.at[pl.ds(0, 3 * OWN)], out_r.at[n])
    hout[...] = HOB[...]
    gin[...] = GIB[...]
    both(t5b, 0, 4)

    arrived(PF.at[:, pl.ds(0, 3 * COLS)], in_s.at[0])
    arrived(A2G.at[:, pl.ds(0, 3 * COLS)], in_s.at[1])
    for n in (0, 1):
        arrived(HOB.at[pl.ds(0, 3 * OWN)], out_s.at[n])
    arrived(RC, sm_s.at[0])
    arrived(SZ.at[pl.ds(0, 3)], sm_s.at[1])
    arrived(SY.at[pl.ds(0, 3)], sm_s.at[2])
    sr_copy().wait_send()

    def finish(l, c):
        w_drain(l)
        for s in range(SLABS):
            t6(l, s)
        gr_drain(l)
        return c

    lax.fori_loop(0, LAYERS, finish, 0)


def step_call(*args):
    vmem = pl.BlockSpec(memory_space=pltpu.VMEM)
    hbm = pl.BlockSpec(memory_space=pl.ANY)
    dma = pltpu.SemaphoreType.DMA
    V = pltpu.VMEM
    L = LAYERS
    scratch = [
        V((TOK, TOK), F32), V((16, COLS), F32),
        V((L, 2, 3, 512, COLS), BF), V((L, 2, 256, 512), BF), V((L, 2, 512, 1024), BF), V((L, 2, 1024, 512), BF),
        V((16, 1024), F32), V((OWN, D), BF),
        V((OWN, D), F32), V((OWN, D), F32), V((OWN, D), F32), V((OWN, D), F32), V((OWN, D), F32), V((OWN, D), F32),
        V((L, TOK, D), BF), V((L, TOK, D), BF), V((TOK, D), BF), V((TOK, D), BF),
        V((L, 3, TOK, COLS), BF), V((L, TOK, COLS), BF), V((L, HEADS_LOCAL, TOK, TOK), F32),
        V((L, TOK, 1024), F32), V((L, TOK, 1024), BF), V((L, 2, OWN, D), F32), V((L, 2, OWN, 128), F32),
        V((TOK, 1024), BF), V((TOK, 768), BF), V((TOK, COLS), BF),
        V((TOK, D), BF), V((OWN, D), BF), V((2, 2, OWN, D), BF), V((2, OWN, D), BF),
        V((2, OWN, D), BF), V((TOK, COLS), BF), V((TOK, COLS), BF),
        V((L, SLABS, 2, 512, 512), BF), V((L, SLABS, 2, 2, 128, 256), BF),
        V((L, SLABS, 2, 2, 128, 512), BF), V((L, SLABS, 2, 128, 512), BF),
        V((L, SLABS, 3, 2, 32, 512), BF), V((L, SLABS, 2, 32, 512), BF), V((L, SLABS, 32, 512), BF),
        V((L, SLABS, 128, 512), BF),
        V((L, 8, D), F32), V((L, 1, 1024), F32), V((L, 2, COLS), F32), V((3, L, 8, COLS), F32),
        V((32, COLS), F32), V((4, 32, COLS), F32), V((4, 32, COLS), F32), V((32, COLS), F32),
        dma((L, 3)), dma((L, len(PARTS), 2)), dma((L, 4)), dma((L, 4)), dma((2,)), dma((2,)),
        dma((1,)), dma((4,)), dma((1,)), dma((6,)),
        dma((L, 7)), dma((L, SLABS, 7)), dma((2,)), dma((2,)), dma((L,)), dma((4,)), dma((4,)),
    ]
    return pl.pallas_call(
        kernel,
        out_shape=[
            jax.ShapeDtypeStruct((TOK, COLS), BF),
            jax.ShapeDtypeStruct((TOK, COLS), BF),
            jax.ShapeDtypeStruct((L, 3, 512, COLS), BF),
            jax.ShapeDtypeStruct((L, 256, 512), BF),
            jax.ShapeDtypeStruct((L, 512, 1024), BF),
            jax.ShapeDtypeStruct((L, 1024, 512), BF),
            jax.ShapeDtypeStruct((32, COLS), F32),
        ],
        in_specs=[vmem] * 10 + [hbm] * 4,
        out_specs=[vmem, vmem, hbm, hbm, hbm, hbm, vmem],
        scratch_shapes=scratch,
        compiler_params=pltpu.CompilerParams(
            collective_id=0, has_side_effects=True, vmem_limit_bytes=63 * 2**20
        ),
        name="encoder_step",
    )(*args)


def finish_kernel(
    hout, gin, sums, gq, go, gu, gd,
    out_h, out_g, qvb, outb, gain, shift, upb, downb, fq, fo, fu, fd,
    low, high, low_q, high_q, in_sem, out_sem,
):
    blocks = []
    for l in range(LAYERS):
        for j in range(3):
            blocks.append((gq.at[l, j], fq.at[l, j], low_q.at[l * 3 + j], high_q.at[l * 3 + j]))
    n = 0
    for l in range(LAYERS):
        places = [(gd, fd, (l, pl.ds(q * 256, 256))) for q in range(4)] + [(go, fo, (l,))]
        places += [(gu, fu, (l, pl.ds(q * 256, 256), pl.ds(h * 512, 512))) for q in range(2) for h in range(2)]
        for src, dst, where in places:
            blocks.append((src.at[where], dst.at[where], low.at[n], high.at[n]))
            n += 1
    for k, (src, _, here, _) in enumerate(blocks):
        pltpu.make_async_copy(src, here, in_sem.at[k]).start()
    out_h[...] = hout[...]
    out_g[...] = gin[...]
    for l in range(LAYERS):
        outb[l : l + 1, :] = sums[8 * l : 8 * l + 1, :]
        for n in (0, 1):
            gain[l, n : n + 1, :] = sums[8 * l + 1 + 2 * n : 8 * l + 2 + 2 * n, :]
            shift[l, n : n + 1, :] = sums[8 * l + 2 + 2 * n : 8 * l + 3 + 2 * n, :]
        downb[l : l + 1, :] = sums[8 * l + 5 : 8 * l + 6, :]
        for q in range(4):
            upb[l : l + 1, q * COLS : (q + 1) * COLS] = sums[16 + 4 * l + q : 17 + 4 * l + q, :]
        qvb[l] = sums[24 + 2 * l : 26 + 2 * l, :]
    for k, (src, dst, here, wide) in enumerate(blocks):
        pltpu.make_async_copy(src, here, in_sem.at[k]).wait()
        wide[...] = here[...].astype(F32)
        pltpu.make_async_copy(wide, dst, out_sem.at[k]).start()
    for k, (_, dst, _, wide) in enumerate(blocks):
        pltpu.make_async_copy(wide, dst, out_sem.at[k]).wait()


def finish_call(*args):
    vmem = pl.BlockSpec(memory_space=pltpu.VMEM)
    hbm = pl.BlockSpec(memory_space=pl.ANY)
    L = LAYERS
    small = ((L, 2, COLS), (L, COLS), (L, 2, COLS), (L, 2, COLS), (L, 1024), (L, COLS))
    large = ((L, 3, 512, COLS), (L, 256, 512), (L, 512, 1024), (L, 1024, 512))
    return pl.pallas_call(
        finish_kernel,
        out_shape=[jax.ShapeDtypeStruct((TOK, COLS), BF)] * 2 + [jax.ShapeDtypeStruct(d, F32) for d in small + large],
        in_specs=[vmem] * 3 + [hbm] * 4,
        out_specs=[vmem] * 8 + [hbm] * 4,
        scratch_shapes=[
            pltpu.VMEM((9 * L, 256, 512), BF), pltpu.VMEM((9 * L, 256, 512), F32),
            pltpu.VMEM((3 * L, 512, COLS), BF), pltpu.VMEM((3 * L, 512, COLS), F32),
            pltpu.SemaphoreType.DMA((12 * L,)), pltpu.SemaphoreType.DMA((12 * L,)),
        ],
        compiler_params=pltpu.CompilerParams(vmem_limit_bytes=32 * 2**20),
        name="finish",
    )(*args)


def shards(
    hidden_in, seg_ids, key_mask, w_qkv, qv_bias, w_out, out_bias, ln_gain, ln_shift,
    w_up, up_bias, w_down, down_bias, grad_out,
):
    hout, gin, grad_qkv, grad_out_w, grad_up, grad_down, sums = step_call(
        hidden_in, grad_out, seg_ids.reshape(1, TOK), key_mask.reshape(1, TOK), out_bias, ln_gain, ln_shift, down_bias,
        up_bias, qv_bias, w_qkv.transpose(0, 2, 1, 3), w_out, w_up, w_down,
    )
    hout, gin, qvb, outb, gain, shift, upb, downb, grad_qkv, grad_out_w, grad_up, grad_down = finish_call(
        hout, gin, sums, grad_qkv, grad_out_w, grad_up, grad_down
    )
    return (
        hout, gin, grad_qkv.transpose(0, 2, 1, 3), qvb, grad_out_w, outb, gain, shift, grad_up, upb, grad_down, downb,
    )


def solution(mesh):
    tokens = P(("dp", "row"), "col")
    return jax.shard_map(
        shards,
        mesh=mesh,
        in_specs=(
            tokens, P(("dp", "row")), P(("dp", "row")), P(None, "row", None, "col"), P(None, None, "col"),
            P(None, "col", "row"), P(None, "col"), P(None, None, "col"), P(None, None, "col"),
            P(None, "row", "col"), P(None, "col"), P(None, "col", "row"), P(None, "col"), tokens,
        ),
        out_specs=(
            tokens, tokens, P(None, "row", None, "col"), P(None, None, "col"), P(None, "col", "row"),
            P(None, "col"), P(None, None, "col"), P(None, None, "col"), P(None, "row", "col"),
            P(None, "col"), P(None, "col", "row"), P(None, "col"),
        ),
        check_vma=False,
    )
```

```python
import functools

import jax
import jax.numpy as jnp
from jax import lax
from jax.experimental import pallas as pl
from jax.experimental.pallas import tpu as pltpu
from jax.sharding import PartitionSpec as P

D = 1024
HD = 64
LAYERS = 2
TOK = 256
OWN = 64
COLS = 256
HEADS_LOCAL = 4
SLABS = 6
EPSILON = 1e-05
MASKED = -1e30
SCALE = HD**-0.5
PARTS = (
    (0, 0, 1, 0), (0, 1, 2, 1), (0, 2, 3, 0), (1, 0, 512, 1), (2, 0, 512, 0), (2, 512, 1024, 1), (3, 0, 256, 0), (3, 256, 512, 1),
)
WEIGHT_ROWS = (512, 256, 512, 1024)
MESH = pl.DeviceIdType.MESH
BF = jnp.bfloat16
F32 = jnp.float32


def dot(a, b):
    return jnp.dot(a, b, preferred_element_type=F32)


def dot_nt(a, b):
    return lax.dot_general(a, b, (((1,), (1,)), ((), ())), preferred_element_type=F32)


def dot_tn(a, b):
    return lax.dot_general(a, b, (((0,), (0,)), ((), ())), preferred_element_type=F32)


def norm_back(upstream, normed, inverse, gain):
    scaled = upstream * gain
    mean_one = jnp.sum(scaled, axis=1, keepdims=True) / D
    mean_two = jnp.sum(scaled * normed, axis=1, keepdims=True) / D
    return inverse * (scaled - mean_one - normed * mean_two)


def kernel(
    hid, gout, seg, key, outb, gain, shift, downb, upb, qvb, wq, wo, wu, wd,
    hout, gin, gq, go, gu, gd, gsmall,
    mask, small, WQ, WO, WU, WD, PF, A2G, S, M, U, GS, GF, F1,
    STATE, MID, SEC, FIR, QKV, CTX, PR, DG, ACT, NRM, INV, LL, ML, GC,
    PS, XS, L1, L2, HS, HOB, GIB,
    G, RL, R1, A1, R2, A2, R3, FB,
    SGF, SU, SQ, RC, SM, SZ, SY, SR,
    w_s, w_r, w_rb, w_lsem, in_s, in_r, ag_s, ag_r, rs_s, rs_r, gr_s, gr_r, out_s, out_r, lsem, sm_s, sm_r,
):
    dp = lax.axis_index("dp")
    row = lax.axis_index("row")
    col = lax.axis_index("col")
    z, y = lax.div(dp, 4), lax.rem(dp, 4)
    xh, core = lax.div(col, 2), lax.rem(col, 2)
    col_core = xh * 2 + (1 - core)
    col_cross = (1 - xh) * 2 + core
    col_diag = (1 - xh) * 2 + (1 - core)
    core_dev = (dp, row, col_core)
    cross_dev = (dp, row, col_cross)
    row_dev = (dp, 1 - row, col)

    def col_dev(d):
        return (dp, row, lax.rem(col + d, 4))

    def axis_place(axis):
        return z if axis == 0 else y

    def axis_dev(axis, d):
        if axis == 0:
            return (lax.rem(z + d, 4) * 4 + y, row, col)
        return (z * 4 + lax.rem(y + d, 4), row, col)

    def chunk(j, rows=OWN):
        return pl.ds(pl.multiple_of(j * rows, rows), rows)

    def remote(src, dst, ssem, rsem, dev):
        return pltpu.make_async_remote_copy(
            src_ref=src, dst_ref=dst, send_sem=ssem, recv_sem=rsem, device_id=dev, device_id_type=MESH
        )

    def arrived(ref, sem):
        pltpu.make_async_copy(ref, ref, sem).wait()

    barrier = pltpu.get_barrier_semaphore()
    for dev in [col_dev(1), col_dev(2), col_dev(3), row_dev] + [axis_dev(a, d) for a in (0, 1) for d in (1, 2, 3)]:
        pl.semaphore_signal(barrier, 1, device_id=dev, device_id_type=MESH)
    pl.semaphore_wait(barrier, 10)

    def in_copies(d):
        to = lax.rem(col + d, 4)
        dev = (dp, row, to)
        return [
            remote(small, PF.at[:, chunk(col, COLS)], in_s.at[0], in_r.at[0], dev),
            remote(gout.at[chunk(to)], A2G.at[:, chunk(col, COLS)], in_s.at[1], in_r.at[1], dev),
        ]

    def hid_block(owner, p):
        return STATE.at[0, pl.ds(p * 128, 128), chunk(owner, COLS)]

    pairs = ((wq, WQ), (wo, WO), (wu, WU), (wd, WD))

    def region(ref, n, lo, hi, rows):
        if n == 0:
            return ref.at[lo, rows, :]
        return ref.at[rows, pl.ds(lo, hi - lo)]

    def w_local(l, n):
        return pltpu.make_async_copy(pairs[n][0].at[l], pairs[n][1].at[l, row], w_lsem.at[l, n])

    def part_axes(p):
        first = PARTS[p][3]
        return first, 1 - first

    def part_rows(p, a_place, b_place):
        piece = WEIGHT_ROWS[PARTS[p][0]] // 16
        return pl.ds(pl.multiple_of((b_place * 4 + a_place) * piece, piece), piece)

    def w_piece(l, p, which):
        n, lo, hi, _ = PARTS[p]
        first, second = part_axes(p)
        rows = part_rows(p, axis_place(first), axis_place(second))
        return remote(
            region(pairs[n][0].at[l], n, lo, hi, rows), region(pairs[n][1].at[l, which], n, lo, hi, rows),
            w_s.at[l, 0], w_r.at[l, p, 0], row_dev,
        )

    def w_one(l, p, d, place):
        n, lo, hi, _ = PARTS[p]
        first, second = part_axes(p)
        rows = part_rows(p, place, axis_place(second))
        ref = region(pairs[n][1].at[l, 1 - row], n, lo, hi, rows)
        return remote(ref, ref, w_s.at[l, 1], w_r.at[l, p, 1], axis_dev(first, d))

    def w_two(l, p, d, place):
        n, lo, hi, _ = PARTS[p]
        _, second = part_axes(p)
        block = WEIGHT_ROWS[n] // 4
        ref = region(pairs[n][1].at[l, 1 - row], n, lo, hi, chunk(place, block))
        return remote(ref, ref, w_s.at[l, 2], w_rb.at[l, n], axis_dev(second, d))

    def w_step_one(l, p):
        w_piece(l, p, 1 - row).wait_recv()
        for d in (1, 2, 3):
            w_one(l, p, d, axis_place(part_axes(p)[0])).start()

    def three_pieces(l, p):
        n, lo, hi, _ = PARTS[p]
        piece = WEIGHT_ROWS[n] // 16
        return region(pairs[n][1].at[l, 1 - row], n, lo, hi, pl.ds(0, 3 * piece))

    def w_step_two(l, p):
        second = part_axes(p)[1]
        arrived(three_pieces(l, p), w_r.at[l, p, 1])
        for d in (1, 2, 3):
            w_two(l, p, d, axis_place(second)).start()

    def w_wait(l, n):
        w_local(l, n).wait()
        rows = WEIGHT_ROWS[n] * 3 // 4
        if n == 0:
            arrived(WQ.at[l, 1 - row, :, pl.ds(0, rows), :], w_rb.at[l, n])
        else:
            arrived(pairs[n][1].at[l, 1 - row, pl.ds(0, rows), :], w_rb.at[l, n])

    def w_drain(l):
        arrived(WU.at[0, 0, pl.ds(0, 192), pl.ds(0, 512)], w_s.at[l, 0])
        arrived(WQ.at[0, :, :, pl.ds(0, 192), :], w_s.at[l, 1])
        arrived(WQ.at[:, :, :, pl.ds(0, 384), :], w_s.at[l, 2])

    parts = range(len(PARTS))
    for p in parts[:3]:
        w_piece(0, p, row).start()
    for p in (0, 1):
        remote(hid.at[pl.ds(p * 128, 128)], hid_block(col, p), ag_s.at[0], ag_r.at[p], cross_dev).start()
    remote(hid, STATE.at[0, :, chunk(col, COLS)], ag_s.at[0], ag_r.at[2], core_dev).start()
    for p in parts[3:]:
        w_piece(0, p, row).start()
    for n in range(4):
        w_local(0, n).start()
    for l in range(LAYERS):
        rows = (outb[l : l + 1], gain[l, 0:1], shift[l, 0:1], gain[l, 1:2], shift[l, 1:2], downb[l : l + 1])
        for r in range(6):
            small[l * 8 + r : l * 8 + r + 1, :] = rows[r]
        small[l * 8 + 6 : l * 8 + 8, :] = jnp.zeros((2, COLS), F32)
    for d in (1, 2, 3):
        in_copies(d)[0].start()
    for p in parts[:3]:
        w_step_one(0, p)

    seg_lanes = jnp.broadcast_to(seg[...].astype(F32), (TOK, TOK))
    key_lanes = jnp.broadcast_to(key[...].astype(F32), (TOK, TOK))
    same_place = lax.broadcasted_iota(jnp.int32, (TOK, TOK), 0) == lax.broadcasted_iota(jnp.int32, (TOK, TOK), 1)
    keep = jnp.where(same_place, 1.0, key_lanes)
    mask[...] = jnp.where(seg_lanes.T == seg_lanes, keep, 0.0)

    A2G[:, chunk(col, COLS)] = gout[chunk(col), :]
    PF[:, chunk(col, COLS)] = small[...]
    STATE[0, :, chunk(col, COLS)] = hid[...]
    for p in parts[:3]:
        w_step_two(0, p)
    for p in parts[3:]:
        w_step_one(0, p)
    for d in (1, 2, 3):
        in_copies(d)[1].start()
    for n in range(4):
        w_local(1, n).start()
    for p in (0, 1):
        arrived(hid_block(col_cross, p), ag_r.at[p])
        remote(hid_block(col_cross, p), hid_block(col_cross, p), ag_s.at[0], ag_r.at[3], core_dev).start()
    for p in parts[3:]:
        w_step_two(0, p)
    arrived(STATE.at[0, :, chunk(col_core, COLS)], ag_r.at[2])
    arrived(STATE.at[0, :, chunk(col_diag, COLS)], ag_r.at[3])
    S[...] = STATE[0, chunk(col), :].astype(F32)
    arrived(PF.at[:, pl.ds(0, 3 * COLS)], in_r.at[0])
    arrived(A2G.at[:, pl.ds(0, 3 * COLS)], in_r.at[1])
    U[...] = A2G[...].astype(F32)

    def ag_rows(owner, p):
        return pl.ds(pl.multiple_of(owner * OWN + p * 32, 32), 32)

    def ag_send(X):
        out = []
        for p in (0, 1):
            rows = ag_rows(col, p)
            out.append(remote(X.at[rows], X.at[rows], ag_s.at[0], ag_r.at[p], cross_dev))
        out.append(remote(X.at[chunk(col)], X.at[chunk(col)], ag_s.at[0], ag_r.at[2], core_dev))
        return out

    def ag_start(X):
        for c in ag_send(X):
            c.start()

    def ag_near(X):
        arrived(X.at[chunk(col_core)], ag_r.at[2])

    def ag_far(X):
        for p in (0, 1):
            rows = ag_rows(col_cross, p)
            arrived(X.at[rows], ag_r.at[p])
            remote(X.at[rows], X.at[rows], ag_s.at[0], ag_r.at[3], core_dev).start()
        arrived(X.at[chunk(col_diag)], ag_r.at[3])

    def ag_finish(X):
        ag_far(X)
        ag_near(X)

    near_rows, far_rows = chunk(xh, 2 * OWN), chunk(1 - xh, 2 * OWN)

    def ag_drain(X):
        arrived(X.at[pl.ds(0, 3 * OWN)], ag_s.at[0])

    def half(h):
        return pl.ds(h * 512, 512)

    def rs_first(par, h, t):
        to = (1 - xh) * 2 + (1 - core) if t == 0 else col_core
        return remote(
            PS.at[chunk(to), half(h)], L1.at[par, t, :, half(h)], rs_s.at[0], rs_r.at[h * 3 + t], core_dev
        )

    def rs_cross(par, h):
        return remote(XS.at[:, half(h)], L2.at[par, :, half(h)], rs_s.at[0], rs_r.at[h * 3 + 2], cross_dev)

    def rs_send(par, h):
        for t in (0, 1):
            rs_first(par, h, t).start()

    def rs_send_rows(par, t):
        for h in (0, 1):
            rs_first(par, h, t).start()

    def rs_mid(par, h):
        rs_first(par, h, 0).wait_recv()
        total = PS[chunk(col_cross), half(h)].astype(F32) + L1[par, 0, :, half(h)].astype(F32)
        XS[:, half(h)] = total.astype(BF)
        rs_cross(par, h).start()

    def rs_end(par, h):
        rs_first(par, h, 1).wait_recv()
        total = PS[chunk(col), half(h)].astype(F32) + L1[par, 1, :, half(h)].astype(F32)
        rs_cross(par, h).wait_recv()
        return total + L2[par, :, half(h)].astype(F32)

    def rs_drain():
        arrived(PS.at[pl.ds(0, 3 * OWN)], rs_s.at[0])

    first_half, second_half = pl.ds(0, 256), pl.ds(256, 256)

    def gr_block(l, s, d, lanes):
        return G.at[l, s, :, chunk(lax.rem(axis_place(s % 2) + d, 4), 128), lanes]

    def gr_relay(l, s, side):
        lanes, d = ((first_half, 1), (second_half, 3))[side]
        return remote(gr_block(l, s, 2, lanes), RL.at[l, s, side], gr_s.at[l, 0], gr_r.at[l, s, 0], axis_dev(s % 2, d))

    def gr_one(l, s, side, lanes):
        d = (1, 3)[side]
        return remote(
            gr_block(l, s, d, lanes), R1.at[l, s, side, :, :, lanes], gr_s.at[l, 1], gr_r.at[l, s, 1], axis_dev(s % 2, d)
        )

    def gr_two(l, s, d):
        axis = 1 - s % 2
        to = lax.rem(axis_place(axis) + d, 4)
        return remote(A1.at[l, s, :, chunk(to, 32), :], R2.at[l, s, d - 1], gr_s.at[l, 2], gr_r.at[l, s, 2], axis_dev(axis, d))

    def gr_row(l, s):
        return remote(A2.at[l, s, 1 - row], R3.at[l, s], gr_s.at[l, 3], gr_r.at[l, s, 3], row_dev)

    def gr_four(l, s, d, place):
        rows = FB.at[l, s, chunk(place, 32), :]
        return remote(rows, rows, gr_s.at[l, 4], gr_r.at[l, s, 4], axis_dev(1 - s % 2, d))

    def places(l, s, place):
        every = pl.ds(0, 512)
        if s < 4:
            out = []
            for q in (0, 1):
                if s < 2:
                    to = gd.at[l, pl.ds(pl.multiple_of(s * 512 + place * 128 + q * 64, 64), 64), :]
                else:
                    to = gu.at[l, pl.ds(pl.multiple_of(place * 128 + q * 64, 64), 64), pl.ds((s - 2) * 512, 512)]
                out.append([(pl.ds(q * 64, 64), every, to)])
            return out
        if s == 4:
            return [[(pl.ds(0, 128), pl.ds(j * COLS, COLS), gq.at[l, j, chunk(place, 128), :])] for j in (0, 1)]
        lower = pl.ds(64, 64)
        return [
            [(pl.ds(0, 64), every, go.at[l, chunk(place, 64), :])],
            [
                (lower, pl.ds(0, COLS), gq.at[l, 2, chunk(place, 64), :]),
                (lower, pl.ds(COLS, COLS), gq.at[l, 2, pl.ds(pl.multiple_of(256 + place * 64, 64), 64), :]),
            ],
        ]

    def gr_five(l, s, d):
        first, second = places(l, s, axis_place(s % 2))
        return [
            remote(FB.at[l, s, rows, lanes], to, gr_s.at[l, 5], gr_r.at[l, s, 5], axis_dev(s % 2, d))
            for rows, lanes, to in first + second
        ]

    def gr_six(l, s):
        out = []
        for side, (source, d) in enumerate(((3, 1), (1, 3))):
            place = lax.rem(axis_place(s % 2) + source, 4)
            for _, _, to in places(l, s, place)[side]:
                out.append(remote(to, to, gr_s.at[l, 6], gr_r.at[l, s, 6], axis_dev(s % 2, d)))
        return out

    def gr_local(l, s):
        first, second = places(l, s, axis_place(s % 2))
        return [pltpu.make_async_copy(FB.at[l, s, rows, lanes], to, lsem.at[l]) for rows, lanes, to in first + second]

    def t1(l, s):
        gr_relay(l, s, 0).start()
        gr_relay(l, s, 1).start()
        gr_one(l, s, 0, second_half).start()
        gr_one(l, s, 1, first_half).start()

    def t1b(l, s):
        arrived(RL.at[l, s], gr_r.at[l, s, 0])
        for side, lanes in ((0, first_half), (1, second_half)):
            rows = chunk(lax.rem(axis_place(s % 2) + (1, 3)[side], 4), 128)
            for r in (0, 1):
                total = G[l, s, r, rows, lanes].astype(F32) + RL[l, s, side, r].astype(F32)
                G[l, s, r, rows, lanes] = total.astype(BF)
            gr_one(l, s, side, lanes).start()

    def t2(l, s):
        arrived(R1.at[l, s], gr_r.at[l, s, 1])
        own = chunk(axis_place(s % 2), 128)
        for r in (0, 1):
            total = G[l, s, r, own, :].astype(F32)
            for side in (0, 1):
                total = total + R1[l, s, side, r].astype(F32)
            A1[l, s, r] = total.astype(BF)
        for d in (1, 2, 3):
            gr_two(l, s, d).start()

    def t3(l, s):
        arrived(R2.at[l, s], gr_r.at[l, s, 2])
        own = chunk(axis_place(1 - s % 2), 32)
        for r in (0, 1):
            total = A1[l, s, r, own, :].astype(F32)
            for d in (0, 1, 2):
                total = total + R2[l, s, d, r].astype(F32)
            A2[l, s, r] = total.astype(BF)
        gr_row(l, s).start()

    def t4(l, s):
        arrived(R3.at[l, s], gr_r.at[l, s, 3])
        place = axis_place(1 - s % 2)
        FB[l, s, chunk(place, 32), :] = (A2[l, s, row].astype(F32) + R3[l, s].astype(F32)).astype(BF)
        for d in (1, 2, 3):
            gr_four(l, s, d, place).start()

    def t5(l, s):
        arrived(FB.at[l, s, pl.ds(0, 96), :], gr_r.at[l, s, 4])
        for d in (1, 3):
            for c in gr_five(l, s, d):
                c.start()
        for c in gr_local(l, s):
            c.start()

    def t5b(l, s):
        arrived(R1.at[l, s, 0], gr_r.at[l, s, 5])
        for c in gr_six(l, s):
            c.start()

    def t6(l, s):
        arrived(FB.at[l, s], gr_r.at[l, s, 6])

    def gr_drain(l):
        arrived(FB.at[l], lsem.at[l])
        arrived(RL.at[l], gr_s.at[l, 0])
        arrived(R1.at[l], gr_s.at[l, 1])
        arrived(R2.at[l], gr_s.at[l, 2])
        arrived(R3.at[l], gr_s.at[l, 3])
        arrived(FB.at[l, :, pl.ds(0, 96), :], gr_s.at[l, 4])
        arrived(R1.at[l, :, 0], gr_s.at[l, 5])
        arrived(FB.at[l], gr_s.at[l, 6])

    def both(step, l, first):
        step(l, first)
        step(l, first + 1)

    def vec(l, r):
        return PF[pl.ds(l * 8 + r, 1), :]

    def norm_into(values, l, n, gain, shift):
        mean_row = jnp.sum(values, axis=1, keepdims=True) / D
        squares = jnp.sum(values * values, axis=1, keepdims=True) / D
        inverse = lax.rsqrt(squares - mean_row * mean_row + EPSILON)
        normed = (values - mean_row) * inverse
        NRM[l, n] = normed
        INV[l, n] = jnp.broadcast_to(inverse, (OWN, 128))
        return normed * gain + shift

    def forward(l, carry):
        X = STATE.at[l]

        @pl.when(l > 0)
        def _():
            X[chunk(col), :] = S[...].astype(BF)
            ag_start(X)

        w_wait(l, 0)

        def project(rows):
            for j in range(3):
                mixed = dot(STATE[l, rows, :512], WQ[l, 0, j]) + dot(STATE[l, rows, 512:], WQ[l, 1, j])
                if j != 1:
                    mixed = mixed + qvb[l, j // 2 : j // 2 + 1, :]
                QKV[l, j, rows, :] = mixed.astype(BF)

        @pl.when(l > 0)
        def _():
            ag_near(X)

        project(near_rows)

        @pl.when(l > 0)
        def _():
            ag_far(X)

        project(far_rows)
        ag_drain(X)

        @pl.when(l == 0)
        def _():
            for p in parts:
                w_piece(1, p, row).start()

        for h in range(HEADS_LOCAL):
            lanes = slice(h * HD, (h + 1) * HD)
            scores = dot_nt(QKV[l, 0, :, lanes], QKV[l, 1, :, lanes])
            scaled = jnp.where(mask[...] > 0.5, scores * SCALE, MASKED)
            raised = jnp.exp(scaled - jnp.max(scaled, axis=1, keepdims=True))
            probs = raised / jnp.sum(raised, axis=1, keepdims=True)
            PR[l, h] = probs
            CTX[l, :, lanes] = dot(probs.astype(BF), QKV[l, 2, :, lanes]).astype(BF)
        w_wait(l, 1)
        for t, rows in ((0, far_rows), (1, near_rows)):
            for h in (0, 1):
                PS[rows, half(h)] = dot(CTX[l, rows, :], WO[l, h]).astype(BF)
            rs_send_rows(0, t)
        rs_mid(0, 0)
        rs_mid(0, 1)
        for h in (0, 1):
            F1[:, half(h)] = S[:, half(h)] + rs_end(0, h)
        rs_drain()
        middle = norm_into(F1[...] + vec(l, 0), l, 0, vec(l, 1), vec(l, 2))
        M[...] = middle
        X = MID.at[l]
        X[chunk(col), :] = middle.astype(BF)
        ag_start(X)

        @pl.when(l == 0)
        def _():
            for p in parts:
                w_step_one(1, p)

        w_wait(l, 2)

        def lift_rows(rows):
            def lift(n, c):
                lanes = chunk(n, COLS)
                lifted = dot(MID[l, rows, :512], WU[l, 0, :, lanes]) + dot(MID[l, rows, 512:], WU[l, 1, :, lanes])
                lifted = lifted + upb[pl.ds(l, 1), lanes]
                phi = 0.5 * (1.0 + lax.erf(lifted * (0.5**0.5)))
                density = jnp.exp(-0.5 * lifted * lifted) * 0.3989422804014327
                DG[l, rows, lanes] = phi + lifted * density
                ACT[l, rows, lanes] = (lifted * phi).astype(BF)
                return c

            lax.fori_loop(0, 4, lift, 0)

        ag_near(X)
        lift_rows(near_rows)
        ag_far(X)
        lift_rows(far_rows)
        ag_drain(X)

        @pl.when(l == 0)
        def _():
            for p in parts:
                w_step_two(1, p)

        w_wait(l, 3)
        for t, rows in ((0, far_rows), (1, near_rows)):
            for h in (0, 1):
                for q in (0, 1):
                    lanes = pl.ds(h * 512 + q * 256, 256)
                    PS[rows, lanes] = dot(ACT[l, rows, :], WD[l, h, :, pl.ds(q * 256, 256)]).astype(BF)
            rs_send_rows(1, t)
        rs_mid(1, 0)
        rs_mid(1, 1)
        for h in (0, 1):
            F1[:, half(h)] = M[:, half(h)] + rs_end(1, h)
        rs_drain()
        S[...] = norm_into(F1[...] + vec(l, 5), l, 1, vec(l, 3), vec(l, 4))
        return carry

    lax.fori_loop(0, LAYERS, forward, 0)

    def out_copies(n, d):
        buf = (HOB, GIB)[n]
        to = lax.rem(col + d, 4)
        return remote(
            HS.at[n, :, chunk(to, COLS)], buf.at[chunk(col)], out_s.at[n], out_r.at[n], (dp, row, to)
        )

    HS[0] = S[...].astype(BF)
    for d in (1, 2, 3):
        out_copies(0, d).start()
    HOB[chunk(col), :] = HS[0, :, chunk(col, COLS)]

    def backward(i, carry):
        l = LAYERS - 1 - i
        prev = l + 1
        upstream = U[...]
        normed = NRM[l, 1]
        SGF[l, 3:4, :] = jnp.sum(upstream * normed, axis=0, keepdims=True)
        SGF[l, 4:5, :] = jnp.sum(upstream, axis=0, keepdims=True)
        grad_second = norm_back(upstream, normed, INV[l, 1, :, :1], vec(l, 3))
        GS[...] = grad_second
        SGF[l, 5:6, :] = jnp.sum(grad_second, axis=0, keepdims=True)
        SEC[chunk(col), :] = grad_second.astype(BF)
        ag_start(SEC)

        @pl.when(i > 0)
        def _():
            both(t4, prev, 0)
            both(t3, prev, 2)

        ag_finish(SEC)

        def down_grad(f, c):
            total = dot_tn(ACT[l, :, chunk(f, COLS)], SEC[...]).astype(BF)
            rows = chunk(lax.rem(f, 2), COLS)
            for r in (0, 1):
                G[l, lax.div(f, 2), r, rows, :] = total[:, r * 512 : (r + 1) * 512]
            return c

        lax.fori_loop(0, 4, down_grad, 0)
        both(t1, l, 0)

        def pull(n, c):
            lanes = chunk(n, COLS)
            grad_act = dot_nt(SEC[:, :512], WD[l, 0, lanes, :]) + dot_nt(SEC[:, 512:], WD[l, 1, lanes, :])
            grad_lifted = grad_act * DG[l, :, lanes]
            SU[l, :, lanes] = jnp.sum(grad_lifted, axis=0, keepdims=True)
            LL[:, lanes] = grad_lifted.astype(BF)
            return c

        lax.fori_loop(0, 4, pull, 0)
        ag_drain(SEC)

        @pl.when(i > 0)
        def _():
            both(t2, prev, 4)

        for h in (0, 1):
            for q in (0, 1):
                lanes = pl.ds(h * 512 + q * 256, 256)
                PS[:, lanes] = dot_nt(LL[...], WU[l, h, pl.ds(q * 256, 256), :]).astype(BF)
            rs_send(0, h)
        rs_mid(0, 0)
        rs_mid(0, 1)

        def up_grad(n, c):
            total = dot_tn(MID[l, :, chunk(n, COLS)], LL[...]).astype(BF)
            rows = chunk(lax.rem(n, 2), COLS)
            for r in (0, 1):
                G[l, 2 + r, lax.div(n, 2), rows, :] = total[:, r * 512 : (r + 1) * 512]
            return c

        lax.fori_loop(0, 4, up_grad, 0)
        both(t1, l, 2)

        both(t1b, l, 0)

        @pl.when(i > 0)
        def _():
            both(t4, prev, 2)
            both(t3, prev, 4)


        for h in (0, 1):
            GS[:, half(h)] = GS[:, half(h)] + rs_end(0, h)
        rs_drain()
        grad_middle = GS[...]
        normed = NRM[l, 0]
        SGF[l, 1:2, :] = jnp.sum(grad_middle * normed, axis=0, keepdims=True)
        SGF[l, 2:3, :] = jnp.sum(grad_middle, axis=0, keepdims=True)
        grad_first = norm_back(grad_middle, normed, INV[l, 0, :, :1], vec(l, 1))
        GF[...] = grad_first
        SGF[l, 0:1, :] = jnp.sum(grad_first, axis=0, keepdims=True)
        FIR[chunk(col), :] = grad_first.astype(BF)
        ag_start(FIR)

        @pl.when(i > 0)
        def _():
            both(t4, prev, 4)

        ag_finish(FIR)
        GC[...] = (dot_nt(FIR[:, :512], WO[l, 0]) + dot_nt(FIR[:, 512:], WO[l, 1])).astype(BF)
        for h in range(HEADS_LOCAL):
            lanes = slice(h * HD, (h + 1) * HD)
            probs = PR[l, h]
            grad_probs = dot_nt(GC[:, lanes], QKV[l, 2, :, lanes])
            centre = jnp.sum(probs * grad_probs, axis=1, keepdims=True)
            grad_scores = (probs * (grad_probs - centre) * SCALE).astype(BF)
            grad_query = dot(grad_scores, QKV[l, 1, :, lanes])
            grad_key = dot_tn(grad_scores, QKV[l, 0, :, lanes])
            grad_value = dot_tn(probs.astype(BF), GC[:, lanes])
            SQ[l, 0:1, lanes] = jnp.sum(grad_query, axis=0, keepdims=True)
            SQ[l, 1:2, lanes] = jnp.sum(grad_value, axis=0, keepdims=True)
            ML[:, h * HD : (h + 1) * HD] = grad_query.astype(BF)
            ML[:, COLS + h * HD : COLS + (h + 1) * HD] = grad_key.astype(BF)
            ML[:, 2 * COLS + h * HD : 2 * COLS + (h + 1) * HD] = grad_value.astype(BF)
        ag_drain(FIR)
        total = dot_tn(CTX[l], FIR[...]).astype(BF)
        for r in (0, 1):
            for q in range(4):
                G[l, 5, r, q * 128 : q * 128 + 64, :] = total[q * 64 : (q + 1) * 64, r * 512 : (r + 1) * 512]

        def qkv_grad(r, c):
            for q in (0, 1):
                total = dot_tn(STATE[l, :, chunk(2 * r + q, COLS)], ML[...]).astype(BF)
                G[l, 4, r, q * 256 : (q + 1) * 256, :] = total[:, :512]
                for b in range(4):
                    G[l, 5, r, b * 128 + 64 : b * 128 + 128, q * 256 : (q + 1) * 256] = total[b * 64 : (b + 1) * 64, 512:]
            return c

        lax.fori_loop(0, 2, qkv_grad, 0)
        both(t1, l, 4)
        both(t1b, l, 2)
        both(t2, l, 0)

        for h in (0, 1):
            for q in (0, 1):
                lanes = pl.ds(h * 512 + q * 256, 256)
                PS[:, lanes] = sum(
                    dot_nt(ML[:, j * COLS : (j + 1) * COLS], WQ[l, h, j, pl.ds(q * 256, 256), :]) for j in range(3)
                ).astype(BF)
            rs_send(1, h)
        rs_mid(1, 0)
        rs_mid(1, 1)
        both(t3, l, 0)
        both(t2, l, 2)
        both(t1b, l, 4)

        for h in (0, 1):
            U[:, half(h)] = GF[:, half(h)] + rs_end(1, h)
        rs_drain()
        return carry

    lax.fori_loop(0, LAYERS, backward, 0)

    HS[1] = U[...].astype(BF)
    for d in (1, 2, 3):
        out_copies(1, d).start()
    GIB[chunk(col), :] = HS[1, :, chunk(col, COLS)]

    def sc_copy(d):
        to = lax.rem(col + d, 4)
        return remote(SGF.at[:, :, chunk(to, COLS)], RC.at[d - 1], sm_s.at[0], sm_r.at[0], (dp, row, to))

    def sd_copy(axis, d, place):
        buf = (SZ, SY)[axis]
        return remote(
            buf.at[axis_place(axis)], buf.at[place], sm_s.at[1 + axis], sm_r.at[1 + axis], axis_dev(axis, d)
        )

    def sr_copy():
        return remote(SM, SR, sm_s.at[3], sm_r.at[3], row_dev)

    for d in (1, 2, 3):
        sc_copy(d).start()
    both(t5, 1, 0)
    both(t5, 1, 2)
    both(t4, 0, 0)
    both(t3, 0, 2)
    both(t2, 0, 4)
    both(t5, 1, 4)
    arrived(RC, sm_r.at[0])
    feature = SGF[:, :, chunk(col, COLS)]
    for d in (0, 1, 2):
        feature = feature + RC[d]
    for l in range(LAYERS):
        SZ[z, 8 * l : 8 * l + 8, :] = feature[l]
        for q in range(4):
            SZ[z, 16 + 4 * l + q : 17 + 4 * l + q, :] = SU[l, :, q * COLS : (q + 1) * COLS]
        SZ[z, 24 + 2 * l : 26 + 2 * l, :] = SQ[l]
    SZ[z, 28:32, :] = jnp.zeros((4, COLS), F32)
    for d in (1, 2, 3):
        sd_copy(0, d, z).start()
    both(t3, 0, 4)
    both(t4, 0, 2)
    both(t5, 0, 0)
    both(t5b, 1, 0)
    both(t5b, 1, 2)
    arrived(SZ.at[pl.ds(0, 3)], sm_r.at[1])
    SY[y] = SZ[0] + SZ[1] + SZ[2] + SZ[3]
    for d in (1, 2, 3):
        sd_copy(1, d, y).start()
    both(t4, 0, 4)
    both(t5, 0, 2)
    both(t5b, 1, 4)
    arrived(SY.at[pl.ds(0, 3)], sm_r.at[2])
    SM[...] = SY[0] + SY[1] + SY[2] + SY[3]
    sr_copy().start()
    both(t5, 0, 4)
    both(t5b, 0, 0)
    both(t5b, 0, 2)
    sr_copy().wait_recv()
    gsmall[...] = SM[...] + SR[...]
    for n in (0, 1):
        buf = (HOB, GIB)[n]
        arrived(buf.at[pl.ds(0, 3 * OWN)], out_r.at[n])
    hout[...] = HOB[...]
    gin[...] = GIB[...]
    both(t5b, 0, 4)

    arrived(PF.at[:, pl.ds(0, 3 * COLS)], in_s.at[0])
    arrived(A2G.at[:, pl.ds(0, 3 * COLS)], in_s.at[1])
    for n in (0, 1):
        arrived(HOB.at[pl.ds(0, 3 * OWN)], out_s.at[n])
    arrived(RC, sm_s.at[0])
    arrived(SZ.at[pl.ds(0, 3)], sm_s.at[1])
    arrived(SY.at[pl.ds(0, 3)], sm_s.at[2])
    sr_copy().wait_send()

    def finish(l, c):
        w_drain(l)
        for s in range(SLABS):
            t6(l, s)
        gr_drain(l)
        return c

    lax.fori_loop(0, LAYERS, finish, 0)


def step_call(*args):
    vmem = pl.BlockSpec(memory_space=pltpu.VMEM)
    hbm = pl.BlockSpec(memory_space=pl.ANY)
    dma = pltpu.SemaphoreType.DMA
    V = pltpu.VMEM
    L = LAYERS
    scratch = [
        V((TOK, TOK), F32), V((16, COLS), F32),
        V((L, 2, 3, 512, COLS), BF), V((L, 2, 256, 512), BF), V((L, 2, 512, 1024), BF), V((L, 2, 1024, 512), BF),
        V((16, 1024), F32), V((OWN, D), BF),
        V((OWN, D), F32), V((OWN, D), F32), V((OWN, D), F32), V((OWN, D), F32), V((OWN, D), F32), V((OWN, D), F32),
        V((L, TOK, D), BF), V((L, TOK, D), BF), V((TOK, D), BF), V((TOK, D), BF),
        V((L, 3, TOK, COLS), BF), V((L, TOK, COLS), BF), V((L, HEADS_LOCAL, TOK, TOK), F32),
        V((L, TOK, 1024), F32), V((L, TOK, 1024), BF), V((L, 2, OWN, D), F32), V((L, 2, OWN, 128), F32),
        V((TOK, 1024), BF), V((TOK, 768), BF), V((TOK, COLS), BF),
        V((TOK, D), BF), V((OWN, D), BF), V((2, 2, OWN, D), BF), V((2, OWN, D), BF),
        V((2, OWN, D), BF), V((TOK, COLS), BF), V((TOK, COLS), BF),
        V((L, SLABS, 2, 512, 512), BF), V((L, SLABS, 2, 2, 128, 256), BF),
        V((L, SLABS, 2, 2, 128, 512), BF), V((L, SLABS, 2, 128, 512), BF),
        V((L, SLABS, 3, 2, 32, 512), BF), V((L, SLABS, 2, 32, 512), BF), V((L, SLABS, 32, 512), BF),
        V((L, SLABS, 128, 512), BF),
        V((L, 8, D), F32), V((L, 1, 1024), F32), V((L, 2, COLS), F32), V((3, L, 8, COLS), F32),
        V((32, COLS), F32), V((4, 32, COLS), F32), V((4, 32, COLS), F32), V((32, COLS), F32),
        dma((L, 3)), dma((L, len(PARTS), 2)), dma((L, 4)), dma((L, 4)), dma((2,)), dma((2,)),
        dma((1,)), dma((4,)), dma((1,)), dma((6,)),
        dma((L, 7)), dma((L, SLABS, 7)), dma((2,)), dma((2,)), dma((L,)), dma((4,)), dma((4,)),
    ]
    return pl.pallas_call(
        kernel,
        out_shape=[
            jax.ShapeDtypeStruct((TOK, COLS), BF),
            jax.ShapeDtypeStruct((TOK, COLS), BF),
            jax.ShapeDtypeStruct((L, 3, 512, COLS), BF),
            jax.ShapeDtypeStruct((L, 256, 512), BF),
            jax.ShapeDtypeStruct((L, 512, 1024), BF),
            jax.ShapeDtypeStruct((L, 1024, 512), BF),
            jax.ShapeDtypeStruct((32, COLS), F32),
        ],
        in_specs=[vmem] * 10 + [hbm] * 4,
        out_specs=[vmem, vmem, hbm, hbm, hbm, hbm, vmem],
        scratch_shapes=scratch,
        compiler_params=pltpu.CompilerParams(
            collective_id=0, has_side_effects=True, vmem_limit_bytes=63 * 2**20
        ),
        name="encoder_step",
    )(*args)


def finish_kernel(
    hout, gin, sums, gq, go, gu, gd,
    out_h, out_g, qvb, outb, gain, shift, upb, downb, fq, fo, fu, fd,
    low, high, low_q, high_q, in_sem, out_sem,
):
    blocks = []
    for l in range(LAYERS):
        for j in range(3):
            blocks.append((gq.at[l, j], fq.at[l, j], low_q.at[l * 3 + j], high_q.at[l * 3 + j]))
    n = 0
    for l in range(LAYERS):
        places = [(gd, fd, (l, pl.ds(q * 256, 256))) for q in range(4)] + [(go, fo, (l,))]
        places += [(gu, fu, (l, pl.ds(q * 256, 256), pl.ds(h * 512, 512))) for q in range(2) for h in range(2)]
        for src, dst, where in places:
            blocks.append((src.at[where], dst.at[where], low.at[n], high.at[n]))
            n += 1
    for k, (src, _, here, _) in enumerate(blocks):
        pltpu.make_async_copy(src, here, in_sem.at[k]).start()
    out_h[...] = hout[...]
    out_g[...] = gin[...]
    for l in range(LAYERS):
        outb[l : l + 1, :] = sums[8 * l : 8 * l + 1, :]
        for n in (0, 1):
            gain[l, n : n + 1, :] = sums[8 * l + 1 + 2 * n : 8 * l + 2 + 2 * n, :]
            shift[l, n : n + 1, :] = sums[8 * l + 2 + 2 * n : 8 * l + 3 + 2 * n, :]
        downb[l : l + 1, :] = sums[8 * l + 5 : 8 * l + 6, :]
        for q in range(4):
            upb[l : l + 1, q * COLS : (q + 1) * COLS] = sums[16 + 4 * l + q : 17 + 4 * l + q, :]
        qvb[l] = sums[24 + 2 * l : 26 + 2 * l, :]
    for k, (src, dst, here, wide) in enumerate(blocks):
        pltpu.make_async_copy(src, here, in_sem.at[k]).wait()
        wide[...] = here[...].astype(F32)
        pltpu.make_async_copy(wide, dst, out_sem.at[k]).start()
    for k, (_, dst, _, wide) in enumerate(blocks):
        pltpu.make_async_copy(wide, dst, out_sem.at[k]).wait()


def finish_call(*args):
    vmem = pl.BlockSpec(memory_space=pltpu.VMEM)
    hbm = pl.BlockSpec(memory_space=pl.ANY)
    L = LAYERS
    small = ((L, 2, COLS), (L, COLS), (L, 2, COLS), (L, 2, COLS), (L, 1024), (L, COLS))
    large = ((L, 3, 512, COLS), (L, 256, 512), (L, 512, 1024), (L, 1024, 512))
    return pl.pallas_call(
        finish_kernel,
        out_shape=[jax.ShapeDtypeStruct((TOK, COLS), BF)] * 2 + [jax.ShapeDtypeStruct(d, F32) for d in small + large],
        in_specs=[vmem] * 3 + [hbm] * 4,
        out_specs=[vmem] * 8 + [hbm] * 4,
        scratch_shapes=[
            pltpu.VMEM((9 * L, 256, 512), BF), pltpu.VMEM((9 * L, 256, 512), F32),
            pltpu.VMEM((3 * L, 512, COLS), BF), pltpu.VMEM((3 * L, 512, COLS), F32),
            pltpu.SemaphoreType.DMA((12 * L,)), pltpu.SemaphoreType.DMA((12 * L,)),
        ],
        compiler_params=pltpu.CompilerParams(vmem_limit_bytes=32 * 2**20),
        name="finish",
    )(*args)


def shards(
    hidden_in, seg_ids, key_mask, w_qkv, qv_bias, w_out, out_bias, ln_gain, ln_shift,
    w_up, up_bias, w_down, down_bias, grad_out,
):
    hout, gin, grad_qkv, grad_out_w, grad_up, grad_down, sums = step_call(
        hidden_in, grad_out, seg_ids.reshape(1, TOK), key_mask.reshape(1, TOK), out_bias, ln_gain, ln_shift, down_bias,
        up_bias, qv_bias, w_qkv.transpose(0, 2, 1, 3), w_out, w_up, w_down,
    )
    hout, gin, qvb, outb, gain, shift, upb, downb, grad_qkv, grad_out_w, grad_up, grad_down = finish_call(
        hout, gin, sums, grad_qkv, grad_out_w, grad_up, grad_down
    )
    return (
        hout, gin, grad_qkv.transpose(0, 2, 1, 3), qvb, grad_out_w, outb, gain, shift, grad_up, upb, grad_down, downb,
    )


def solution(mesh):
    tokens = P(("dp", "row"), "col")
    return jax.shard_map(
        shards,
        mesh=mesh,
        in_specs=(
            tokens, P(("dp", "row")), P(("dp", "row")), P(None, "row", None, "col"), P(None, None, "col"),
            P(None, "col", "row"), P(None, "col"), P(None, None, "col"), P(None, None, "col"),
            P(None, "row", "col"), P(None, "col"), P(None, "col", "row"), P(None, "col"), tokens,
        ),
        out_specs=(
            tokens, tokens, P(None, "row", None, "col"), P(None, None, "col"), P(None, "col", "row"),
            P(None, "col"), P(None, None, "col"), P(None, None, "col"), P(None, "row", "col"),
            P(None, "col"), P(None, "col", "row"), P(None, "col"),
        ),
        check_vma=False,
    )
```

```python
import functools

import jax
import jax.numpy as jnp
from jax import lax
from jax.experimental import pallas as pl
from jax.experimental.pallas import tpu as pltpu
from jax.sharding import PartitionSpec as P

D = 1024
HD = 64
LAYERS = 2
TOK = 256
OWN = 64
COLS = 256
HEADS_LOCAL = 4
SLABS = 6
EPSILON = 1e-05
MASKED = -1e30
SCALE = HD**-0.5
PARTS = (
    (0, 0, 1, 0), (0, 1, 2, 1), (0, 2, 3, 0), (1, 0, 512, 1), (2, 0, 512, 0), (2, 512, 1024, 1), (3, 0, 256, 0), (3, 256, 512, 1),
)
WEIGHT_ROWS = (512, 256, 512, 1024)
MESH = pl.DeviceIdType.MESH
BF = jnp.bfloat16
F32 = jnp.float32


def dot(a, b):
    return jnp.dot(a, b, preferred_element_type=F32)


def dot_nt(a, b):
    return lax.dot_general(a, b, (((1,), (1,)), ((), ())), preferred_element_type=F32)


def dot_tn(a, b):
    return lax.dot_general(a, b, (((0,), (0,)), ((), ())), preferred_element_type=F32)


def norm_back(upstream, normed, inverse, gain):
    scaled = upstream * gain
    mean_one = jnp.sum(scaled, axis=1, keepdims=True) / D
    mean_two = jnp.sum(scaled * normed, axis=1, keepdims=True) / D
    return inverse * (scaled - mean_one - normed * mean_two)


def kernel(
    hid, gout, seg, key, outb, gain, shift, downb, upb, qvb, wq, wo, wu, wd,
    hout, gin, gq, go, gu, gd, gsmall,
    mask, small, WQ, WO, WU, WD, PF, A2G, S, M, U, GS, GF, F1,
    STATE, MID, SEC, FIR, QKV, CTX, PR, DG, ACT, NRM, INV, LL, ML, GC,
    PS, XS, L1, L2, HS, HOB, GIB,
    G, RL, R1, A1, R2, A2, R3, FB,
    SGF, SU, SQ, RC, SM, SZ, SY, SR,
    w_s, w_r, w_rb, w_lsem, in_s, in_r, ag_s, ag_r, rs_s, rs_r, gr_s, gr_r, out_s, out_r, lsem, sm_s, sm_r,
):
    dp = lax.axis_index("dp")
    row = lax.axis_index("row")
    col = lax.axis_index("col")
    z, y = lax.div(dp, 4), lax.rem(dp, 4)
    xh, core = lax.div(col, 2), lax.rem(col, 2)
    col_core = xh * 2 + (1 - core)
    col_cross = (1 - xh) * 2 + core
    col_diag = (1 - xh) * 2 + (1 - core)
    core_dev = (dp, row, col_core)
    cross_dev = (dp, row, col_cross)
    row_dev = (dp, 1 - row, col)

    def col_dev(d):
        return (dp, row, lax.rem(col + d, 4))

    def axis_place(axis):
        return z if axis == 0 else y

    def axis_dev(axis, d):
        if axis == 0:
            return (lax.rem(z + d, 4) * 4 + y, row, col)
        return (z * 4 + lax.rem(y + d, 4), row, col)

    def chunk(j, rows=OWN):
        return pl.ds(pl.multiple_of(j * rows, rows), rows)

    def remote(src, dst, ssem, rsem, dev):
        return pltpu.make_async_remote_copy(
            src_ref=src, dst_ref=dst, send_sem=ssem, recv_sem=rsem, device_id=dev, device_id_type=MESH
        )

    def arrived(ref, sem):
        pltpu.make_async_copy(ref, ref, sem).wait()

    barrier = pltpu.get_barrier_semaphore()
    for dev in [col_dev(1), col_dev(2), col_dev(3), row_dev] + [axis_dev(a, d) for a in (0, 1) for d in (1, 2, 3)]:
        pl.semaphore_signal(barrier, 1, device_id=dev, device_id_type=MESH)
    pl.semaphore_wait(barrier, 10)

    def in_copies(d):
        to = lax.rem(col + d, 4)
        dev = (dp, row, to)
        return [
            remote(small, PF.at[:, chunk(col, COLS)], in_s.at[0], in_r.at[0], dev),
            remote(gout.at[chunk(to)], A2G.at[:, chunk(col, COLS)], in_s.at[1], in_r.at[1], dev),
        ]

    def hid_block(owner, p):
        return STATE.at[0, pl.ds(p * 128, 128), chunk(owner, COLS)]

    pairs = ((wq, WQ), (wo, WO), (wu, WU), (wd, WD))

    def region(ref, n, lo, hi, rows):
        if n == 0:
            return ref.at[lo, rows, :]
        return ref.at[rows, pl.ds(lo, hi - lo)]

    def w_local(l, n):
        return pltpu.make_async_copy(pairs[n][0].at[l], pairs[n][1].at[l, row], w_lsem.at[l, n])

    def part_axes(p):
        first = PARTS[p][3]
        return first, 1 - first

    def part_rows(p, a_place, b_place):
        piece = WEIGHT_ROWS[PARTS[p][0]] // 16
        return pl.ds(pl.multiple_of((b_place * 4 + a_place) * piece, piece), piece)

    def w_piece(l, p, which):
        n, lo, hi, _ = PARTS[p]
        first, second = part_axes(p)
        rows = part_rows(p, axis_place(first), axis_place(second))
        return remote(
            region(pairs[n][0].at[l], n, lo, hi, rows), region(pairs[n][1].at[l, which], n, lo, hi, rows),
            w_s.at[l, 0], w_r.at[l, p, 0], row_dev,
        )

    def w_one(l, p, d, place):
        n, lo, hi, _ = PARTS[p]
        first, second = part_axes(p)
        rows = part_rows(p, place, axis_place(second))
        ref = region(pairs[n][1].at[l, 1 - row], n, lo, hi, rows)
        return remote(ref, ref, w_s.at[l, 1], w_r.at[l, p, 1], axis_dev(first, d))

    def w_two(l, p, d, place):
        n, lo, hi, _ = PARTS[p]
        _, second = part_axes(p)
        block = WEIGHT_ROWS[n] // 4
        ref = region(pairs[n][1].at[l, 1 - row], n, lo, hi, chunk(place, block))
        return remote(ref, ref, w_s.at[l, 2], w_rb.at[l, n], axis_dev(second, d))

    def w_step_one(l, p):
        w_piece(l, p, 1 - row).wait_recv()
        for d in (1, 2, 3):
            w_one(l, p, d, axis_place(part_axes(p)[0])).start()

    def three_pieces(l, p):
        n, lo, hi, _ = PARTS[p]
        piece = WEIGHT_ROWS[n] // 16
        return region(pairs[n][1].at[l, 1 - row], n, lo, hi, pl.ds(0, 3 * piece))

    def w_step_two(l, p):
        second = part_axes(p)[1]
        arrived(three_pieces(l, p), w_r.at[l, p, 1])
        for d in (1, 2, 3):
            w_two(l, p, d, axis_place(second)).start()

    def w_wait(l, n):
        w_local(l, n).wait()
        rows = WEIGHT_ROWS[n] * 3 // 4
        if n == 0:
            arrived(WQ.at[l, 1 - row, :, pl.ds(0, rows), :], w_rb.at[l, n])
        else:
            arrived(pairs[n][1].at[l, 1 - row, pl.ds(0, rows), :], w_rb.at[l, n])

    def w_drain(l):
        arrived(WU.at[0, 0, pl.ds(0, 192), pl.ds(0, 512)], w_s.at[l, 0])
        arrived(WQ.at[0, :, :, pl.ds(0, 192), :], w_s.at[l, 1])
        arrived(WQ.at[:, :, :, pl.ds(0, 384), :], w_s.at[l, 2])

    parts = range(len(PARTS))
    for p in parts[:3]:
        w_piece(0, p, row).start()
    for p in (0, 1):
        remote(hid.at[pl.ds(p * 128, 128)], hid_block(col, p), ag_s.at[0], ag_r.at[p], cross_dev).start()
    remote(hid, STATE.at[0, :, chunk(col, COLS)], ag_s.at[0], ag_r.at[2], core_dev).start()
    for p in parts[3:]:
        w_piece(0, p, row).start()
    for n in range(4):
        w_local(0, n).start()
    for l in range(LAYERS):
        rows = (outb[l : l + 1], gain[l, 0:1], shift[l, 0:1], gain[l, 1:2], shift[l, 1:2], downb[l : l + 1])
        for r in range(6):
            small[l * 8 + r : l * 8 + r + 1, :] = rows[r]
        small[l * 8 + 6 : l * 8 + 8, :] = jnp.zeros((2, COLS), F32)
    for d in (1, 2, 3):
        in_copies(d)[0].start()
    for p in parts[:3]:
        w_step_one(0, p)

    seg_lanes = jnp.broadcast_to(seg[...].astype(F32), (TOK, TOK))
    key_lanes = jnp.broadcast_to(key[...].astype(F32), (TOK, TOK))
    same_place = lax.broadcasted_iota(jnp.int32, (TOK, TOK), 0) == lax.broadcasted_iota(jnp.int32, (TOK, TOK), 1)
    keep = jnp.where(same_place, 1.0, key_lanes)
    mask[...] = jnp.where(seg_lanes.T == seg_lanes, keep, 0.0)

    A2G[:, chunk(col, COLS)] = gout[chunk(col), :]
    PF[:, chunk(col, COLS)] = small[...]
    STATE[0, :, chunk(col, COLS)] = hid[...]
    for p in parts[:3]:
        w_step_two(0, p)
    for p in parts[3:]:
        w_step_one(0, p)
    for d in (1, 2, 3):
        in_copies(d)[1].start()
    for n in range(4):
        w_local(1, n).start()
    for p in (0, 1):
        arrived(hid_block(col_cross, p), ag_r.at[p])
        remote(hid_block(col_cross, p), hid_block(col_cross, p), ag_s.at[0], ag_r.at[3], core_dev).start()
    for p in parts[3:]:
        w_step_two(0, p)
    arrived(STATE.at[0, :, chunk(col_core, COLS)], ag_r.at[2])
    arrived(STATE.at[0, :, chunk(col_diag, COLS)], ag_r.at[3])
    S[...] = STATE[0, chunk(col), :].astype(F32)
    arrived(PF.at[:, pl.ds(0, 3 * COLS)], in_r.at[0])
    arrived(A2G.at[:, pl.ds(0, 3 * COLS)], in_r.at[1])
    U[...] = A2G[...].astype(F32)

    def ag_rows(owner, p):
        return pl.ds(pl.multiple_of(owner * OWN + p * 32, 32), 32)

    def ag_send(X):
        out = []
        for p in (0, 1):
            rows = ag_rows(col, p)
            out.append(remote(X.at[rows], X.at[rows], ag_s.at[0], ag_r.at[p], cross_dev))
        out.append(remote(X.at[chunk(col)], X.at[chunk(col)], ag_s.at[0], ag_r.at[2], core_dev))
        return out

    def ag_start(X):
        for c in ag_send(X):
            c.start()

    def ag_near(X):
        arrived(X.at[chunk(col_core)], ag_r.at[2])

    def ag_far(X):
        for p in (0, 1):
            rows = ag_rows(col_cross, p)
            arrived(X.at[rows], ag_r.at[p])
            remote(X.at[rows], X.at[rows], ag_s.at[0], ag_r.at[3], core_dev).start()
        arrived(X.at[chunk(col_diag)], ag_r.at[3])

    def ag_finish(X):
        ag_far(X)
        ag_near(X)

    near_rows, far_rows = chunk(xh, 2 * OWN), chunk(1 - xh, 2 * OWN)

    def ag_drain(X):
        arrived(X.at[pl.ds(0, 3 * OWN)], ag_s.at[0])

    def half(h):
        return pl.ds(h * 512, 512)

    def rs_first(par, h, t):
        to = (1 - xh) * 2 + (1 - core) if t == 0 else col_core
        return remote(
            PS.at[chunk(to), half(h)], L1.at[par, t, :, half(h)], rs_s.at[0], rs_r.at[h * 3 + t], core_dev
        )

    def rs_cross(par, h):
        return remote(XS.at[:, half(h)], L2.at[par, :, half(h)], rs_s.at[0], rs_r.at[h * 3 + 2], cross_dev)

    def rs_send(par, h):
        for t in (0, 1):
            rs_first(par, h, t).start()

    def rs_send_rows(par, t):
        for h in (0, 1):
            rs_first(par, h, t).start()

    def rs_mid(par, h):
        rs_first(par, h, 0).wait_recv()
        total = PS[chunk(col_cross), half(h)].astype(F32) + L1[par, 0, :, half(h)].astype(F32)
        XS[:, half(h)] = total.astype(BF)
        rs_cross(par, h).start()

    def rs_end(par, h):
        rs_first(par, h, 1).wait_recv()
        total = PS[chunk(col), half(h)].astype(F32) + L1[par, 1, :, half(h)].astype(F32)
        rs_cross(par, h).wait_recv()
        return total + L2[par, :, half(h)].astype(F32)

    def rs_drain():
        arrived(PS.at[pl.ds(0, 3 * OWN)], rs_s.at[0])

    first_half, second_half = pl.ds(0, 256), pl.ds(256, 256)

    def gr_block(l, s, d, lanes):
        return G.at[l, s, :, chunk(lax.rem(axis_place(s % 2) + d, 4), 128), lanes]

    def gr_relay(l, s, side):
        lanes, d = ((first_half, 1), (second_half, 3))[side]
        return remote(gr_block(l, s, 2, lanes), RL.at[l, s, side], gr_s.at[l, 0], gr_r.at[l, s, 0], axis_dev(s % 2, d))

    def gr_one(l, s, side, lanes):
        d = (1, 3)[side]
        return remote(
            gr_block(l, s, d, lanes), R1.at[l, s, side, :, :, lanes], gr_s.at[l, 1], gr_r.at[l, s, 1], axis_dev(s % 2, d)
        )

    def gr_two(l, s, d):
        axis = 1 - s % 2
        to = lax.rem(axis_place(axis) + d, 4)
        return remote(A1.at[l, s, :, chunk(to, 32), :], R2.at[l, s, d - 1], gr_s.at[l, 2], gr_r.at[l, s, 2], axis_dev(axis, d))

    def gr_row(l, s):
        return remote(A2.at[l, s, 1 - row], R3.at[l, s], gr_s.at[l, 3], gr_r.at[l, s, 3], row_dev)

    def gr_four(l, s, d, place):
        rows = FB.at[l, s, chunk(place, 32), :]
        return remote(rows, rows, gr_s.at[l, 4], gr_r.at[l, s, 4], axis_dev(1 - s % 2, d))

    def places(l, s, place):
        every = pl.ds(0, 512)
        if s < 4:
            out = []
            for q in (0, 1):
                if s < 2:
                    to = gd.at[l, pl.ds(pl.multiple_of(s * 512 + place * 128 + q * 64, 64), 64), :]
                else:
                    to = gu.at[l, pl.ds(pl.multiple_of(place * 128 + q * 64, 64), 64), pl.ds((s - 2) * 512, 512)]
                out.append([(pl.ds(q * 64, 64), every, to)])
            return out
        if s == 4:
            return [[(pl.ds(0, 128), pl.ds(j * COLS, COLS), gq.at[l, j, chunk(place, 128), :])] for j in (0, 1)]
        lower = pl.ds(64, 64)
        return [
            [(pl.ds(0, 64), every, go.at[l, chunk(place, 64), :])],
            [
                (lower, pl.ds(0, COLS), gq.at[l, 2, chunk(place, 64), :]),
                (lower, pl.ds(COLS, COLS), gq.at[l, 2, pl.ds(pl.multiple_of(256 + place * 64, 64), 64), :]),
            ],
        ]

    def gr_five(l, s, d):
        first, second = places(l, s, axis_place(s % 2))
        return [
            remote(FB.at[l, s, rows, lanes], to, gr_s.at[l, 5], gr_r.at[l, s, 5], axis_dev(s % 2, d))
            for rows, lanes, to in first + second
        ]

    def gr_six(l, s):
        out = []
        for side, (source, d) in enumerate(((3, 1), (1, 3))):
            place = lax.rem(axis_place(s % 2) + source, 4)
            for _, _, to in places(l, s, place)[side]:
                out.append(remote(to, to, gr_s.at[l, 6], gr_r.at[l, s, 6], axis_dev(s % 2, d)))
        return out

    def gr_local(l, s):
        first, second = places(l, s, axis_place(s % 2))
        return [pltpu.make_async_copy(FB.at[l, s, rows, lanes], to, lsem.at[l]) for rows, lanes, to in first + second]

    def t1(l, s):
        gr_relay(l, s, 0).start()
        gr_relay(l, s, 1).start()
        gr_one(l, s, 0, second_half).start()
        gr_one(l, s, 1, first_half).start()

    def t1b(l, s):
        arrived(RL.at[l, s], gr_r.at[l, s, 0])
        for side, lanes in ((0, first_half), (1, second_half)):
            rows = chunk(lax.rem(axis_place(s % 2) + (1, 3)[side], 4), 128)
            for r in (0, 1):
                total = G[l, s, r, rows, lanes].astype(F32) + RL[l, s, side, r].astype(F32)
                G[l, s, r, rows, lanes] = total.astype(BF)
            gr_one(l, s, side, lanes).start()

    def t2(l, s):
        arrived(R1.at[l, s], gr_r.at[l, s, 1])
        own = chunk(axis_place(s % 2), 128)
        for r in (0, 1):
            total = G[l, s, r, own, :].astype(F32)
            for side in (0, 1):
                total = total + R1[l, s, side, r].astype(F32)
            A1[l, s, r] = total.astype(BF)
        for d in (1, 2, 3):
            gr_two(l, s, d).start()

    def t3(l, s):
        arrived(R2.at[l, s], gr_r.at[l, s, 2])
        own = chunk(axis_place(1 - s % 2), 32)
        for r in (0, 1):
            total = A1[l, s, r, own, :].astype(F32)
            for d in (0, 1, 2):
                total = total + R2[l, s, d, r].astype(F32)
            A2[l, s, r] = total.astype(BF)
        gr_row(l, s).start()

    def t4(l, s):
        arrived(R3.at[l, s], gr_r.at[l, s, 3])
        place = axis_place(1 - s % 2)
        FB[l, s, chunk(place, 32), :] = (A2[l, s, row].astype(F32) + R3[l, s].astype(F32)).astype(BF)
        for d in (1, 2, 3):
            gr_four(l, s, d, place).start()

    def t5(l, s):
        arrived(FB.at[l, s, pl.ds(0, 96), :], gr_r.at[l, s, 4])
        for d in (1, 3):
            for c in gr_five(l, s, d):
                c.start()
        for c in gr_local(l, s):
            c.start()

    def t5b(l, s):
        arrived(R1.at[l, s, 0], gr_r.at[l, s, 5])
        for c in gr_six(l, s):
            c.start()

    def t6(l, s):
        arrived(FB.at[l, s], gr_r.at[l, s, 6])

    def gr_drain(l):
        arrived(FB.at[l], lsem.at[l])
        arrived(RL.at[l], gr_s.at[l, 0])
        arrived(R1.at[l], gr_s.at[l, 1])
        arrived(R2.at[l], gr_s.at[l, 2])
        arrived(R3.at[l], gr_s.at[l, 3])
        arrived(FB.at[l, :, pl.ds(0, 96), :], gr_s.at[l, 4])
        arrived(R1.at[l, :, 0], gr_s.at[l, 5])
        arrived(FB.at[l], gr_s.at[l, 6])

    def both(step, l, first):
        step(l, first)
        step(l, first + 1)

    def vec(l, r):
        return PF[pl.ds(l * 8 + r, 1), :]

    def norm_into(values, l, n, gain, shift):
        mean_row = jnp.sum(values, axis=1, keepdims=True) / D
        squares = jnp.sum(values * values, axis=1, keepdims=True) / D
        inverse = lax.rsqrt(squares - mean_row * mean_row + EPSILON)
        normed = (values - mean_row) * inverse
        NRM[l, n] = normed
        INV[l, n] = jnp.broadcast_to(inverse, (OWN, 128))
        return normed * gain + shift

    def forward(l, carry):
        X = STATE.at[l]

        @pl.when(l > 0)
        def _():
            X[chunk(col), :] = S[...].astype(BF)
            ag_start(X)

        w_wait(l, 0)

        def project(rows):
            for j in range(3):
                mixed = dot(STATE[l, rows, :512], WQ[l, 0, j]) + dot(STATE[l, rows, 512:], WQ[l, 1, j])
                if j != 1:
                    mixed = mixed + qvb[l, j // 2 : j // 2 + 1, :]
                QKV[l, j, rows, :] = mixed.astype(BF)

        @pl.when(l > 0)
        def _():
            ag_near(X)

        project(near_rows)

        @pl.when(l > 0)
        def _():
            ag_far(X)

        project(far_rows)
        ag_drain(X)

        @pl.when(l == 0)
        def _():
            for p in parts:
                w_piece(1, p, row).start()

        for h in range(HEADS_LOCAL):
            lanes = slice(h * HD, (h + 1) * HD)
            scores = dot_nt(QKV[l, 0, :, lanes], QKV[l, 1, :, lanes])
            scaled = jnp.where(mask[...] > 0.5, scores * SCALE, MASKED)
            raised = jnp.exp(scaled - jnp.max(scaled, axis=1, keepdims=True))
            probs = raised / jnp.sum(raised, axis=1, keepdims=True)
            PR[l, h] = probs
            CTX[l, :, lanes] = dot(probs.astype(BF), QKV[l, 2, :, lanes]).astype(BF)
        w_wait(l, 1)
        for t, rows in ((0, far_rows), (1, near_rows)):
            for h in (0, 1):
                PS[rows, half(h)] = dot(CTX[l, rows, :], WO[l, h]).astype(BF)
            rs_send_rows(0, t)
        rs_mid(0, 0)
        rs_mid(0, 1)
        for h in (0, 1):
            F1[:, half(h)] = S[:, half(h)] + rs_end(0, h)
        rs_drain()
        middle = norm_into(F1[...] + vec(l, 0), l, 0, vec(l, 1), vec(l, 2))
        M[...] = middle
        X = MID.at[l]
        X[chunk(col), :] = middle.astype(BF)
        ag_start(X)

        @pl.when(l == 0)
        def _():
            for p in parts:
                w_step_one(1, p)

        w_wait(l, 2)

        def lift_rows(rows):
            def lift(n, c):
                lanes = chunk(n, COLS)
                lifted = dot(MID[l, rows, :512], WU[l, 0, :, lanes]) + dot(MID[l, rows, 512:], WU[l, 1, :, lanes])
                lifted = lifted + upb[pl.ds(l, 1), lanes]
                phi = 0.5 * (1.0 + lax.erf(lifted * (0.5**0.5)))
                density = jnp.exp(-0.5 * lifted * lifted) * 0.3989422804014327
                DG[l, rows, lanes] = phi + lifted * density
                ACT[l, rows, lanes] = (lifted * phi).astype(BF)
                return c

            lax.fori_loop(0, 4, lift, 0)

        ag_near(X)
        lift_rows(near_rows)
        ag_far(X)
        lift_rows(far_rows)
        ag_drain(X)

        @pl.when(l == 0)
        def _():
            for p in parts:
                w_step_two(1, p)

        w_wait(l, 3)
        for t, rows in ((0, far_rows), (1, near_rows)):
            for h in (0, 1):
                for q in (0, 1):
                    lanes = pl.ds(h * 512 + q * 256, 256)
                    PS[rows, lanes] = dot(ACT[l, rows, :], WD[l, h, :, pl.ds(q * 256, 256)]).astype(BF)
            rs_send_rows(1, t)
        rs_mid(1, 0)
        rs_mid(1, 1)
        for h in (0, 1):
            F1[:, half(h)] = M[:, half(h)] + rs_end(1, h)
        rs_drain()
        S[...] = norm_into(F1[...] + vec(l, 5), l, 1, vec(l, 3), vec(l, 4))
        return carry

    lax.fori_loop(0, LAYERS, forward, 0)

    def out_copies(n, d):
        buf = (HOB, GIB)[n]
        to = lax.rem(col + d, 4)
        return remote(
            HS.at[n, :, chunk(to, COLS)], buf.at[chunk(col)], out_s.at[n], out_r.at[n], (dp, row, to)
        )

    HS[0] = S[...].astype(BF)
    for d in (1, 2, 3):
        out_copies(0, d).start()
    HOB[chunk(col), :] = HS[0, :, chunk(col, COLS)]

    def backward(i, carry):
        l = LAYERS - 1 - i
        prev = l + 1
        upstream = U[...]
        normed = NRM[l, 1]
        SGF[l, 3:4, :] = jnp.sum(upstream * normed, axis=0, keepdims=True)
        SGF[l, 4:5, :] = jnp.sum(upstream, axis=0, keepdims=True)
        grad_second = norm_back(upstream, normed, INV[l, 1, :, :1], vec(l, 3))
        GS[...] = grad_second
        SGF[l, 5:6, :] = jnp.sum(grad_second, axis=0, keepdims=True)
        SEC[chunk(col), :] = grad_second.astype(BF)
        ag_start(SEC)

        @pl.when(i > 0)
        def _():
            both(t4, prev, 0)
            both(t3, prev, 2)

        ag_finish(SEC)

        def down_grad(f, c):
            total = dot_tn(ACT[l, :, chunk(f, COLS)], SEC[...]).astype(BF)
            rows = chunk(lax.rem(f, 2), COLS)
            for r in (0, 1):
                G[l, lax.div(f, 2), r, rows, :] = total[:, r * 512 : (r + 1) * 512]
            return c

        lax.fori_loop(0, 4, down_grad, 0)
        both(t1, l, 0)

        def pull(n, c):
            lanes = chunk(n, COLS)
            grad_act = dot_nt(SEC[:, :512], WD[l, 0, lanes, :]) + dot_nt(SEC[:, 512:], WD[l, 1, lanes, :])
            grad_lifted = grad_act * DG[l, :, lanes]
            SU[l, :, lanes] = jnp.sum(grad_lifted, axis=0, keepdims=True)
            LL[:, lanes] = grad_lifted.astype(BF)
            return c

        lax.fori_loop(0, 4, pull, 0)
        ag_drain(SEC)

        @pl.when(i > 0)
        def _():
            both(t2, prev, 4)

        for h in (0, 1):
            for q in (0, 1):
                lanes = pl.ds(h * 512 + q * 256, 256)
                PS[:, lanes] = dot_nt(LL[...], WU[l, h, pl.ds(q * 256, 256), :]).astype(BF)
            rs_send(0, h)
        rs_mid(0, 0)
        rs_mid(0, 1)

        def up_grad(n, c):
            total = dot_tn(MID[l, :, chunk(n, COLS)], LL[...]).astype(BF)
            rows = chunk(lax.rem(n, 2), COLS)
            for r in (0, 1):
                G[l, 2 + r, lax.div(n, 2), rows, :] = total[:, r * 512 : (r + 1) * 512]
            return c

        lax.fori_loop(0, 4, up_grad, 0)
        both(t1, l, 2)

        both(t1b, l, 0)

        @pl.when(i > 0)
        def _():
            both(t4, prev, 2)
            both(t3, prev, 4)


        for h in (0, 1):
            GS[:, half(h)] = GS[:, half(h)] + rs_end(0, h)
        rs_drain()
        grad_middle = GS[...]
        normed = NRM[l, 0]
        SGF[l, 1:2, :] = jnp.sum(grad_middle * normed, axis=0, keepdims=True)
        SGF[l, 2:3, :] = jnp.sum(grad_middle, axis=0, keepdims=True)
        grad_first = norm_back(grad_middle, normed, INV[l, 0, :, :1], vec(l, 1))
        GF[...] = grad_first
        SGF[l, 0:1, :] = jnp.sum(grad_first, axis=0, keepdims=True)
        FIR[chunk(col), :] = grad_first.astype(BF)
        ag_start(FIR)

        @pl.when(i > 0)
        def _():
            both(t4, prev, 4)
            both(t5, prev, 0)

        ag_finish(FIR)
        GC[...] = (dot_nt(FIR[:, :512], WO[l, 0]) + dot_nt(FIR[:, 512:], WO[l, 1])).astype(BF)
        for h in range(HEADS_LOCAL):
            lanes = slice(h * HD, (h + 1) * HD)
            probs = PR[l, h]
            grad_probs = dot_nt(GC[:, lanes], QKV[l, 2, :, lanes])
            centre = jnp.sum(probs * grad_probs, axis=1, keepdims=True)
            grad_scores = (probs * (grad_probs - centre) * SCALE).astype(BF)
            grad_query = dot(grad_scores, QKV[l, 1, :, lanes])
            grad_key = dot_tn(grad_scores, QKV[l, 0, :, lanes])
            grad_value = dot_tn(probs.astype(BF), GC[:, lanes])
            SQ[l, 0:1, lanes] = jnp.sum(grad_query, axis=0, keepdims=True)
            SQ[l, 1:2, lanes] = jnp.sum(grad_value, axis=0, keepdims=True)
            ML[:, h * HD : (h + 1) * HD] = grad_query.astype(BF)
            ML[:, COLS + h * HD : COLS + (h + 1) * HD] = grad_key.astype(BF)
            ML[:, 2 * COLS + h * HD : 2 * COLS + (h + 1) * HD] = grad_value.astype(BF)
        ag_drain(FIR)
        total = dot_tn(CTX[l], FIR[...]).astype(BF)
        for r in (0, 1):
            for q in range(4):
                G[l, 5, r, q * 128 : q * 128 + 64, :] = total[q * 64 : (q + 1) * 64, r * 512 : (r + 1) * 512]

        def qkv_grad(r, c):
            for q in (0, 1):
                total = dot_tn(STATE[l, :, chunk(2 * r + q, COLS)], ML[...]).astype(BF)
                G[l, 4, r, q * 256 : (q + 1) * 256, :] = total[:, :512]
                for b in range(4):
                    G[l, 5, r, b * 128 + 64 : b * 128 + 128, q * 256 : (q + 1) * 256] = total[b * 64 : (b + 1) * 64, 512:]
            return c

        lax.fori_loop(0, 2, qkv_grad, 0)
        both(t1, l, 4)
        both(t1b, l, 2)
        both(t2, l, 0)

        @pl.when(i > 0)
        def _():
            both(t5, prev, 2)


        for h in (0, 1):
            for q in (0, 1):
                lanes = pl.ds(h * 512 + q * 256, 256)
                PS[:, lanes] = sum(
                    dot_nt(ML[:, j * COLS : (j + 1) * COLS], WQ[l, h, j, pl.ds(q * 256, 256), :]) for j in range(3)
                ).astype(BF)
            rs_send(1, h)
        rs_mid(1, 0)
        rs_mid(1, 1)
        both(t3, l, 0)
        both(t2, l, 2)
        both(t1b, l, 4)

        for h in (0, 1):
            U[:, half(h)] = GF[:, half(h)] + rs_end(1, h)
        rs_drain()
        return carry

    lax.fori_loop(0, LAYERS, backward, 0)

    HS[1] = U[...].astype(BF)
    for d in (1, 2, 3):
        out_copies(1, d).start()
    GIB[chunk(col), :] = HS[1, :, chunk(col, COLS)]

    def sc_copy(d):
        to = lax.rem(col + d, 4)
        return remote(SGF.at[:, :, chunk(to, COLS)], RC.at[d - 1], sm_s.at[0], sm_r.at[0], (dp, row, to))

    def sd_copy(axis, d, place):
        buf = (SZ, SY)[axis]
        return remote(
            buf.at[axis_place(axis)], buf.at[place], sm_s.at[1 + axis], sm_r.at[1 + axis], axis_dev(axis, d)
        )

    def sr_copy():
        return remote(SM, SR, sm_s.at[3], sm_r.at[3], row_dev)

    for d in (1, 2, 3):
        sc_copy(d).start()
    both(t4, 0, 0)
    both(t3, 0, 2)
    both(t2, 0, 4)
    both(t5b, 1, 0)
    arrived(RC, sm_r.at[0])
    feature = SGF[:, :, chunk(col, COLS)]
    for d in (0, 1, 2):
        feature = feature + RC[d]
    for l in range(LAYERS):
        SZ[z, 8 * l : 8 * l + 8, :] = feature[l]
        for q in range(4):
            SZ[z, 16 + 4 * l + q : 17 + 4 * l + q, :] = SU[l, :, q * COLS : (q + 1) * COLS]
        SZ[z, 24 + 2 * l : 26 + 2 * l, :] = SQ[l]
    SZ[z, 28:32, :] = jnp.zeros((4, COLS), F32)
    for d in (1, 2, 3):
        sd_copy(0, d, z).start()
    both(t3, 0, 4)
    both(t4, 0, 2)
    both(t5, 1, 4)
    both(t5, 0, 0)
    both(t5b, 1, 2)
    arrived(SZ.at[pl.ds(0, 3)], sm_r.at[1])
    SY[y] = SZ[0] + SZ[1] + SZ[2] + SZ[3]
    for d in (1, 2, 3):
        sd_copy(1, d, y).start()
    both(t4, 0, 4)
    both(t5, 0, 2)
    both(t5b, 1, 4)
    arrived(SY.at[pl.ds(0, 3)], sm_r.at[2])
    SM[...] = SY[0] + SY[1] + SY[2] + SY[3]
    sr_copy().start()
    both(t5, 0, 4)
    both(t5b, 0, 0)
    both(t5b, 0, 2)
    sr_copy().wait_recv()
    gsmall[...] = SM[...] + SR[...]
    for n in (0, 1):
        buf = (HOB, GIB)[n]
        arrived(buf.at[pl.ds(0, 3 * OWN)], out_r.at[n])
    hout[...] = HOB[...]
    gin[...] = GIB[...]
    both(t5b, 0, 4)

    arrived(PF.at[:, pl.ds(0, 3 * COLS)], in_s.at[0])
    arrived(A2G.at[:, pl.ds(0, 3 * COLS)], in_s.at[1])
    for n in (0, 1):
        arrived(HOB.at[pl.ds(0, 3 * OWN)], out_s.at[n])
    arrived(RC, sm_s.at[0])
    arrived(SZ.at[pl.ds(0, 3)], sm_s.at[1])
    arrived(SY.at[pl.ds(0, 3)], sm_s.at[2])
    sr_copy().wait_send()

    def finish(l, c):
        w_drain(l)
        for s in range(SLABS):
            t6(l, s)
        gr_drain(l)
        return c

    lax.fori_loop(0, LAYERS, finish, 0)


def step_call(*args):
    vmem = pl.BlockSpec(memory_space=pltpu.VMEM)
    hbm = pl.BlockSpec(memory_space=pl.ANY)
    dma = pltpu.SemaphoreType.DMA
    V = pltpu.VMEM
    L = LAYERS
    scratch = [
        V((TOK, TOK), F32), V((16, COLS), F32),
        V((L, 2, 3, 512, COLS), BF), V((L, 2, 256, 512), BF), V((L, 2, 512, 1024), BF), V((L, 2, 1024, 512), BF),
        V((16, 1024), F32), V((OWN, D), BF),
        V((OWN, D), F32), V((OWN, D), F32), V((OWN, D), F32), V((OWN, D), F32), V((OWN, D), F32), V((OWN, D), F32),
        V((L, TOK, D), BF), V((L, TOK, D), BF), V((TOK, D), BF), V((TOK, D), BF),
        V((L, 3, TOK, COLS), BF), V((L, TOK, COLS), BF), V((L, HEADS_LOCAL, TOK, TOK), F32),
        V((L, TOK, 1024), F32), V((L, TOK, 1024), BF), V((L, 2, OWN, D), F32), V((L, 2, OWN, 128), F32),
        V((TOK, 1024), BF), V((TOK, 768), BF), V((TOK, COLS), BF),
        V((TOK, D), BF), V((OWN, D), BF), V((2, 2, OWN, D), BF), V((2, OWN, D), BF),
        V((2, OWN, D), BF), V((TOK, COLS), BF), V((TOK, COLS), BF),
        V((L, SLABS, 2, 512, 512), BF), V((L, SLABS, 2, 2, 128, 256), BF),
        V((L, SLABS, 2, 2, 128, 512), BF), V((L, SLABS, 2, 128, 512), BF),
        V((L, SLABS, 3, 2, 32, 512), BF), V((L, SLABS, 2, 32, 512), BF), V((L, SLABS, 32, 512), BF),
        V((L, SLABS, 128, 512), BF),
        V((L, 8, D), F32), V((L, 1, 1024), F32), V((L, 2, COLS), F32), V((3, L, 8, COLS), F32),
        V((32, COLS), F32), V((4, 32, COLS), F32), V((4, 32, COLS), F32), V((32, COLS), F32),
        dma((L, 3)), dma((L, len(PARTS), 2)), dma((L, 4)), dma((L, 4)), dma((2,)), dma((2,)),
        dma((1,)), dma((4,)), dma((1,)), dma((6,)),
        dma((L, 7)), dma((L, SLABS, 7)), dma((2,)), dma((2,)), dma((L,)), dma((4,)), dma((4,)),
    ]
    return pl.pallas_call(
        kernel,
        out_shape=[
            jax.ShapeDtypeStruct((TOK, COLS), BF),
            jax.ShapeDtypeStruct((TOK, COLS), BF),
            jax.ShapeDtypeStruct((L, 3, 512, COLS), BF),
            jax.ShapeDtypeStruct((L, 256, 512), BF),
            jax.ShapeDtypeStruct((L, 512, 1024), BF),
            jax.ShapeDtypeStruct((L, 1024, 512), BF),
            jax.ShapeDtypeStruct((32, COLS), F32),
        ],
        in_specs=[vmem] * 10 + [hbm] * 4,
        out_specs=[vmem, vmem, hbm, hbm, hbm, hbm, vmem],
        scratch_shapes=scratch,
        compiler_params=pltpu.CompilerParams(
            collective_id=0, has_side_effects=True, vmem_limit_bytes=63 * 2**20
        ),
        name="encoder_step",
    )(*args)


def finish_kernel(
    hout, gin, sums, gq, go, gu, gd,
    out_h, out_g, qvb, outb, gain, shift, upb, downb, fq, fo, fu, fd,
    low, high, low_q, high_q, in_sem, out_sem,
):
    blocks = []
    for l in range(LAYERS):
        for j in range(3):
            blocks.append((gq.at[l, j], fq.at[l, j], low_q.at[l * 3 + j], high_q.at[l * 3 + j]))
    n = 0
    for l in range(LAYERS):
        places = [(gd, fd, (l, pl.ds(q * 256, 256))) for q in range(4)] + [(go, fo, (l,))]
        places += [(gu, fu, (l, pl.ds(q * 256, 256), pl.ds(h * 512, 512))) for q in range(2) for h in range(2)]
        for src, dst, where in places:
            blocks.append((src.at[where], dst.at[where], low.at[n], high.at[n]))
            n += 1
    for k, (src, _, here, _) in enumerate(blocks):
        pltpu.make_async_copy(src, here, in_sem.at[k]).start()
    out_h[...] = hout[...]
    out_g[...] = gin[...]
    for l in range(LAYERS):
        outb[l : l + 1, :] = sums[8 * l : 8 * l + 1, :]
        for n in (0, 1):
            gain[l, n : n + 1, :] = sums[8 * l + 1 + 2 * n : 8 * l + 2 + 2 * n, :]
            shift[l, n : n + 1, :] = sums[8 * l + 2 + 2 * n : 8 * l + 3 + 2 * n, :]
        downb[l : l + 1, :] = sums[8 * l + 5 : 8 * l + 6, :]
        for q in range(4):
            upb[l : l + 1, q * COLS : (q + 1) * COLS] = sums[16 + 4 * l + q : 17 + 4 * l + q, :]
        qvb[l] = sums[24 + 2 * l : 26 + 2 * l, :]
    for k, (src, dst, here, wide) in enumerate(blocks):
        pltpu.make_async_copy(src, here, in_sem.at[k]).wait()
        wide[...] = here[...].astype(F32)
        pltpu.make_async_copy(wide, dst, out_sem.at[k]).start()
    for k, (_, dst, _, wide) in enumerate(blocks):
        pltpu.make_async_copy(wide, dst, out_sem.at[k]).wait()


def finish_call(*args):
    vmem = pl.BlockSpec(memory_space=pltpu.VMEM)
    hbm = pl.BlockSpec(memory_space=pl.ANY)
    L = LAYERS
    small = ((L, 2, COLS), (L, COLS), (L, 2, COLS), (L, 2, COLS), (L, 1024), (L, COLS))
    large = ((L, 3, 512, COLS), (L, 256, 512), (L, 512, 1024), (L, 1024, 512))
    return pl.pallas_call(
        finish_kernel,
        out_shape=[jax.ShapeDtypeStruct((TOK, COLS), BF)] * 2 + [jax.ShapeDtypeStruct(d, F32) for d in small + large],
        in_specs=[vmem] * 3 + [hbm] * 4,
        out_specs=[vmem] * 8 + [hbm] * 4,
        scratch_shapes=[
            pltpu.VMEM((9 * L, 256, 512), BF), pltpu.VMEM((9 * L, 256, 512), F32),
            pltpu.VMEM((3 * L, 512, COLS), BF), pltpu.VMEM((3 * L, 512, COLS), F32),
            pltpu.SemaphoreType.DMA((12 * L,)), pltpu.SemaphoreType.DMA((12 * L,)),
        ],
        compiler_params=pltpu.CompilerParams(vmem_limit_bytes=32 * 2**20),
        name="finish",
    )(*args)


def shards(
    hidden_in, seg_ids, key_mask, w_qkv, qv_bias, w_out, out_bias, ln_gain, ln_shift,
    w_up, up_bias, w_down, down_bias, grad_out,
):
    hout, gin, grad_qkv, grad_out_w, grad_up, grad_down, sums = step_call(
        hidden_in, grad_out, seg_ids.reshape(1, TOK), key_mask.reshape(1, TOK), out_bias, ln_gain, ln_shift, down_bias,
        up_bias, qv_bias, w_qkv.transpose(0, 2, 1, 3), w_out, w_up, w_down,
    )
    hout, gin, qvb, outb, gain, shift, upb, downb, grad_qkv, grad_out_w, grad_up, grad_down = finish_call(
        hout, gin, sums, grad_qkv, grad_out_w, grad_up, grad_down
    )
    return (
        hout, gin, grad_qkv.transpose(0, 2, 1, 3), qvb, grad_out_w, outb, gain, shift, grad_up, upb, grad_down, downb,
    )


def solution(mesh):
    tokens = P(("dp", "row"), "col")
    return jax.shard_map(
        shards,
        mesh=mesh,
        in_specs=(
            tokens, P(("dp", "row")), P(("dp", "row")), P(None, "row", None, "col"), P(None, None, "col"),
            P(None, "col", "row"), P(None, "col"), P(None, None, "col"), P(None, None, "col"),
            P(None, "row", "col"), P(None, "col"), P(None, "col", "row"), P(None, "col"), tokens,
        ),
        out_specs=(
            tokens, tokens, P(None, "row", None, "col"), P(None, None, "col"), P(None, "col", "row"),
            P(None, "col"), P(None, None, "col"), P(None, None, "col"), P(None, "row", "col"),
            P(None, "col"), P(None, "col", "row"), P(None, "col"),
        ),
        check_vma=False,
    )
```
